32 devices in a mesh: gx: 4 (over y, core), gy: 8 (over z, x).
Axes of the slice: x: 2, y: 2, z: 4, core: 2. Of those that a mesh axis runs over, the one named last changes fastest.
Arguments:
- volume: bfloat16 [32, 128, 2048], P('gx', 'gy'), may hold values from -6 to 6
- cotangent: bfloat16 [32, 128, 2048], P('gx', 'gy'), may hold values from -6 to 6
- weight: bfloat16 [3, 3, 3, 32, 32], replicated, may hold values from -0.21875 to 0.21875
- bias: float32 [32], replicated, may hold values from -4 to 4
Outputs:
- data_grad: bfloat16 [32, 128, 2048], P('gx', 'gy')
- filter_grad: float32 [3, 3, 3, 32, 32], replicated
- bias_grad: float32 [32], replicated
The draws below stay inside these ranges and needn't reach their ends.
All inputs are finite; a program needn't handle non-finite values.
Results may differ from the reference program's by a relative error of at most 0.008.
Values may be sent and summed in bfloat16 or wider, within the bound.
No kernel may reach another device: no remote copies, remote signals or barrier semaphores. Data moves between devices by JAX's collectives and lax.ppermute only.
A program may use at most 128 MiB of HBM per device.

```python
import math
import jax
import jax.numpy as jnp
from jax import lax

C = 32
CX = 8
NZ = 64
NX = 32
NY = 128


def levels(key, shape, split, smallest, high):
    factor_of = 1.0
    for axis_at, shards_of in split:
        draws = jax.random.uniform(jax.random.fold_in(jax.random.fold_in(key, 6), axis_at), (shards_of,), jnp.float32, smallest / len(split), high / len(split))
        factor_of = factor_of * jnp.repeat(jnp.exp(draws), shape[axis_at] // shards_of).reshape((-1,) + (1,) * (len(shape) - 1 - axis_at))
    return factor_of


def scatter_about(key, extent, spread, most, shards=(), kind=jnp.bfloat16):
    result = jax.random.normal(key, extent, jnp.float32) * spread
    if len(shards) > 0:
        result = levels(key, extent, shards, -0.22, 0.18) * result
    return jnp.clip(result, min=-most, max=most).astype(kind)


def setup_inputs(seed: int = 0) -> dict:
    key_list = jax.random.split(jax.random.key(seed), 5)
    return {
        "volume": scatter_about(key_list[0], (NX, NY, C * NZ), 1.0, 6.0, ((0, 4), (1, 8))),
        "cotangent": scatter_about(key_list[1], (NX, NY, C * NZ), 1.0, 6.0, ((0, 4), (1, 8))),
        "weight": scatter_about(key_list[2], (3, 3, 3, C, C), (27 * C) ** -0.5, 0.21875),
        "bias": scatter_about(key_list[3], (C,), 1.0, 4.0, (), jnp.float32),
    }


def forward_pre(block, weight, bias):
    out = lax.conv_general_dilated(block[None], weight, (1, 1, 1), ((0, 0), (0, 0), (1, 1)), dimension_numbers=('NDHCW', 'DHWIO', 'NDHCW'), preferred_element_type=jnp.float32)[0]
    return out + bias[:, None]

def activation_grad(pre, grad_out):
    sig = jax.nn.sigmoid(pre)
    return (grad_out.astype(jnp.float32) * sig * (1.0 + pre * (1.0 - sig))).astype(jnp.bfloat16)

def input_grad(grad_pre, weight):
    flipped = weight[::-1, ::-1, ::-1]
    out = lax.conv_general_dilated(grad_pre[None], flipped, (1, 1, 1), ((0, 0), (0, 0), (1, 1)), dimension_numbers=('NDHCW', 'DHWOI', 'NDHCW'), preferred_element_type=jnp.float32)[0]
    return out.astype(jnp.bfloat16)

def weight_grad(inputs, grad_pre):
    padded = jnp.pad(inputs, ((0, 0), (0, 0), (0, 0), (1, 1)))
    return lax.conv_general_dilated(padded[None], grad_pre[None], (1, 1, 1), ((0, 0), (0, 0), (0, 0)), dimension_numbers=('CDHNW', 'IDHOW', 'DHWNC'), preferred_element_type=jnp.float32)

def reference(volume, cotangent, weight, bias):
    field = volume.reshape(NX, NY, C, NZ)
    grads = cotangent.reshape(NX, NY, C, NZ)
    field_pad = jnp.pad(field, ((2, 2), (2, 2), (0, 0), (0, 0)))
    grads_pad = jnp.pad(grads, ((1, 1), (1, 1), (0, 0), (0, 0)))

    def one_block(index):
        start = (index * CX).astype(jnp.int32)
        xblock = lax.dynamic_slice_in_dim(field_pad, start, CX + 4, 0)
        gblock = lax.dynamic_slice_in_dim(grads_pad, start, CX + 2, 0)
        pre = forward_pre(xblock, weight, bias)
        grad_pre = activation_grad(pre, gblock)
        dx = input_grad(grad_pre, weight)
        own = grad_pre[1:-1, 1:-1]
        dw = weight_grad(xblock[1:-1, 1:-1], own)
        db = lax.optimization_barrier(jnp.sum(own.astype(jnp.float32), axis=(0, 1, 3)))
        return (dx, dw, db)
    dxs, dws, dbs = lax.map(one_block, jnp.arange(NX // CX, dtype=jnp.int32))
    scale = 1.0 / math.sqrt(NX * NY * NZ)
    data_grad = dxs.reshape(NX, NY, C * NZ)
    return (data_grad, lax.optimization_barrier(jnp.sum(dws, axis=0)) * scale, lax.optimization_barrier(jnp.sum(dbs, axis=0)) * scale)
```

```python
import math

import jax
import jax.numpy as jnp
from jax import lax
from jax.experimental import pallas as pl
from jax.experimental.pallas import tpu as pltpu
from jax.sharding import PartitionSpec as P

C = 32
Z = 64
T = 128
F32 = jnp.float32
BF16 = jnp.bfloat16
VMEM_LIMIT = 48 * 1024 * 1024


def call(body, out_shape, scratch_shapes, flops, *args):
    traffic = sum(math.prod(a.shape) * a.dtype.itemsize for a in (*args, *jax.tree.leaves(out_shape)))
    return pl.pallas_call(
        body,
        out_shape=out_shape,
        in_specs=[pl.BlockSpec(memory_space=pltpu.VMEM)] * len(args),
        out_specs=jax.tree.map(lambda _: pl.BlockSpec(memory_space=pltpu.VMEM), out_shape),
        scratch_shapes=scratch_shapes,
        compiler_params=pltpu.CompilerParams(vmem_limit_bytes=VMEM_LIMIT),
        cost_estimate=pl.CostEstimate(flops=flops, bytes_accessed=traffic, transcendentals=0),
    )(*args)


def lane(shape):
    return lax.broadcasted_iota(jnp.int32, shape, len(shape) - 1)


def swap_halves(a):
    return pltpu.roll(a, T // 2, a.ndim - 1)


def halves(low, high):
    return jnp.where(lane(low.shape) < T // 2, low, high)


def exchange_halves(a, b):
    mixed = swap_halves(halves(b, a))
    return halves(a, mixed), halves(mixed, b)


def from_below(a):
    return jnp.where(lane(a.shape) % Z == 0, 0.0, pltpu.roll(a, 1, a.ndim - 1))


def from_above(a):
    return jnp.where(lane(a.shape) % Z == Z - 1, 0.0, pltpu.roll(a, T - 1, a.ndim - 1))


def to_channels(rows, stage):
    rows = rows.astype(F32)
    for pair in range(C // 2):
        at = slice(pair * T, pair * T + T)
        even, odd = exchange_halves(rows[:8, at], rows[8:, at])
        stage[pl.ds(pair * 16, 8), :] = even
        stage[pl.ds(pair * 16 + 8, 8), :] = odd
    return [stage[pl.ds(t, C, stride=8), :] for t in range(8)]


def pack_body(v, g, vx, gx, xlow, xhigh, ylow, yhigh, cll, clh, chl, chh, stage):
    gfirst, glast = [], []
    for x in range(8):
        tiles = to_channels(v[x], stage.at[x])
        for t in range(8):
            vx[x, :, t * T : t * T + T] = tiles[t].astype(BF16)
        down = halves(tiles[1], swap_halves(tiles[0])).astype(BF16)
        up = halves(swap_halves(tiles[7]), tiles[6]).astype(BF16)
        ylow[x] = down
        yhigh[x] = up
        if x < 2:
            xlow[x] = vx[x]
            cll[x], clh[x] = down, up
        if x >= 6:
            xhigh[x - 6] = vx[x]
            chl[x - 6], chh[x - 6] = down, up
        tiles = to_channels(g[x], stage.at[8 + x])
        for t in range(8):
            gx[x, :, t * T : t * T + T] = tiles[t].astype(BF16)
        gfirst.append(tiles[0])
        glast.append(tiles[7])
    for x in range(4):
        ylow[8 + x] = halves(gfirst[x + 4], swap_halves(gfirst[x])).astype(BF16)
        yhigh[8 + x] = halves(swap_halves(glast[x]), glast[x + 4]).astype(BF16)
    xlow[2] = gx[0]
    xhigh[2] = gx[7]
    cll[2] = swap_halves(gfirst[0]).astype(BF16)
    chl[2] = swap_halves(gfirst[7]).astype(BF16)
    clh[2] = swap_halves(glast[0]).astype(BF16)
    chh[2] = swap_halves(glast[7]).astype(BF16)


def pack(volume, cotangent):
    def of(*shape):
        return jax.ShapeDtypeStruct(shape, BF16)

    field, face, edge, corner = of(8, C, 8 * T), of(3, C, 8 * T), of(12, C, T), of(3, C, T)
    out = (field, field, face, face, edge, edge, corner, corner, corner, corner)
    return call(pack_body, out, [pltpu.VMEM((16, 8 * C, T), F32)], 2_000_000, volume, cotangent)


def band_body(fstrip, dstrip, wf, wd, wr):
    for strip, out in ((fstrip, wf), (dstrip, wd)):
        out[...] = jnp.zeros_like(out)
        for dz in range(3):
            for dy in range(3):
                base = strip[dz * 3 + dy].astype(F32)
                turned = [base if r == 0 else pltpu.roll(base, 32 * r, 1) for r in range(4)]
                for x in range(8):
                    tile, r = divmod(10 * dy + x, 4)
                    rows = slice(dz * 256 + x * C, dz * 256 + x * C + C)
                    keep = lane((C, T)) >= 32 * r
                    out[rows, tile * T : tile * T + T] = jnp.where(keep, turned[r], 0.0).astype(BF16)
                    if r >= 2:
                        rest = jnp.where(keep, 0.0, turned[r])
                        out[rows, tile * T + T : tile * T + 2 * T] = rest.astype(BF16)
    wr[...] = jnp.zeros_like(wr)
    for dz in range(3):
        for dy in range(3):
            base = fstrip[dz * 3 + dy].astype(F32)
            for side in range(2):
                tile, r = divmod(6 * dy + 3 * side, 4)
                rows = slice(dz * 64 + side * C, dz * 64 + side * C + C)
                moved = base if r == 0 else pltpu.roll(base, 32 * r, 1)
                keep = lane((C, T)) >= 32 * r
                old = wr[rows, tile * T : tile * T + T].astype(F32)
                wr[rows, tile * T : tile * T + T] = jnp.where(keep, moved, old).astype(BF16) if r else moved.astype(BF16)
                if r >= 2:
                    wr[rows, tile * T + T : tile * T + 2 * T] = jnp.where(keep, 0.0, moved).astype(BF16)


def bands(weight):
    forward = jnp.transpose(weight, (2, 1, 4, 0, 3)).reshape(9, C, 3 * C)
    backward = jnp.transpose(weight[::-1, ::-1, ::-1], (2, 1, 3, 0, 4)).reshape(9, C, 3 * C)
    pad = ((0, 0), (0, 0), (0, T - 3 * C))
    out = (
        jax.ShapeDtypeStruct((768, 1024), BF16),
        jax.ShapeDtypeStruct((768, 1024), BF16),
        jax.ShapeDtypeStruct((192, 640), BF16),
    )
    return call(band_body, out, [], 2_000_000, jnp.pad(forward, pad), jnp.pad(backward, pad))


def activation(pre, grad_out):
    sig = 1.0 / (1.0 + jnp.exp(-pre))
    return grad_out.astype(F32) * sig * (1.0 + pre * (1.0 - sig))


def below_tile(own_last, nearest):
    return halves(nearest.astype(F32), swap_halves(own_last.astype(F32))).astype(BF16)


def above_tile(own_first, nearest):
    return halves(swap_halves(own_first.astype(F32)), nearest.astype(F32)).astype(BF16)


def stack(out, row, width, field, below, above):
    out[row : row + C, :T] = below
    out[row : row + C, T : 8 * T] = field[:, : 7 * T]
    out[width + row : width + row + C, : 8 * T] = field
    out[2 * width + row : 2 * width + row + C, : 7 * T] = field[:, T:]
    out[2 * width + row : 2 * width + row + C, 7 * T : 8 * T] = above


def front_body(vx, gx, xlow, xhigh, ylow, yhigh, cll, clh, chl, chh, wf, bias, gp, wire, cols, gps, prod):
    for i in range(10):
        x = i - 1
        if x < 0:
            field, low, high = xlow[1], cll[1], clh[1]
        elif x > 7:
            field, low, high = xhigh[0], chl[0], chh[0]
        else:
            field, low, high = vx[x], ylow[x], yhigh[x]
        stack(cols, i * C, 320, field, below_tile(field[:, 7 * T :], low), above_tile(field[:, :T], high))
    cols[960:976, :] = jnp.ones((16, 8 * T), BF16)
    cols[976:1024, :] = jnp.zeros((48, 8 * T), BF16)
    offset = bias[...]
    for pair in range(4):
        at = slice(pair * 2 * T, pair * 2 * T + 2 * T)
        both = jnp.dot(wf[...], cols[:, at], preferred_element_type=F32)
        for half in range(2):
            part = both[:, half * T : half * T + T]
            here = slice((pair * 2 + half) * T, (pair * 2 + half + 1) * T)
            pre = from_below(part[:256]) + part[256:512] + from_above(part[512:]) + offset
            grad = activation(pre, gx[:, :, here].reshape(256, T)).astype(BF16)
            gp[:, here] = grad
            grad = grad.astype(F32)
            gps[:256, here] = from_above(grad).astype(BF16)
            gps[256:512, here] = grad.astype(BF16)
            gps[512:, here] = from_below(grad).astype(BF16)
    for dz in range(3):
        prod[...] = lax.dot_general(
            cols[...], gps[dz * 256 : dz * 256 + 256, :], (((1,), (1,)), ((), ())), preferred_element_type=F32
        )
        group = lane((C, T)) // C
        for dx in range(3):
            for dy in range(3):
                total = jnp.zeros((C, T), F32)
                for x in range(4):
                    a = prod[dy * 320 + (x + dx) * C : dy * 320 + (x + dx) * C + C, :T]
                    b = prod[dy * 320 + (x + 4 + dx) * C : dy * 320 + (x + 4 + dx) * C + C, T:]
                    total = jnp.where(group == x, a + b, total)
                wire[dx * 9 + dy * 3 + dz] = spread(total)
        if dz == 1:
            total = prod[960:968, :T] + prod[960:968, T:]
            total = total + swap_halves(total)
            wire[27] = total + pltpu.roll(total, C, 1)


def spread(total):
    total = total + swap_halves(total)
    total = total + pltpu.roll(total, C, 1)
    group = lane((8, T)) // C
    out = total[:8]
    for q in range(1, 4):
        out = jnp.where(group == q, total[8 * q : 8 * q + 8], out)
    return out


def front(parts, wf, bias):
    out = (jax.ShapeDtypeStruct((256, 8 * T), BF16), jax.ShapeDtypeStruct((28, 8, T), F32))
    scratch = [pltpu.VMEM((1024, 8 * T), BF16), pltpu.VMEM((768, 8 * T), BF16), pltpu.VMEM((1024, 256), F32)]
    return call(front_body, out, scratch, 3_000_000_000, *parts, wf, bias)


def back_body(
    vx, gx, xlow, xhigh, ylow, yhigh, cll, clh, chl, chh, gp, wf, wr, wd, bias, data, side, ring, cols, stage
):
    def edge(x):
        if x < 0:
            return xlow[x + 2], cll[x + 2], clh[x + 2]
        if x > 7:
            return xhigh[x - 8], chl[x - 8], chh[x - 8]
        return vx[x], ylow[x], yhigh[x]

    side[...] = jnp.zeros_like(side)
    ring[960:, :] = jnp.zeros((64, T), BF16)
    for x in range(-2, 10):
        field, low, high = edge(x)
        lo, hi = low.astype(F32), high.astype(F32)
        first, last = field[:, :T].astype(F32), field[:, 7 * T :].astype(F32)
        near = halves(lo, hi).astype(BF16)
        before = halves(swap_halves(lo), last).astype(BF16)
        after = halves(first, swap_halves(hi)).astype(BF16)
        if x <= 0 or x >= 7:
            row = (x + 2 if x <= 0 else x - 4) * C
            stack(side, row, 192, field, below_tile(field[:, 7 * T :], low), above_tile(field[:, :T], high))
            for dy, tile in enumerate((before, near, after)):
                side[dy * 192 + row : dy * 192 + row + C, 8 * T :] = tile
        if -1 <= x <= 8:
            row = (x + 1) * C
            for dy, tile in enumerate((before, near, after)):
                ring[dy * 320 + row : dy * 320 + row + C, :] = tile
    offset = bias[...]

    def finish(part, n, grad_out):
        pre = from_below(part[:n]) + part[n : 2 * n] + from_above(part[2 * n :]) + offset[:n]
        return activation(pre, grad_out)

    both = jnp.dot(wr[...], side[...], preferred_element_type=F32)
    faces = []
    for t in range(8):
        here = slice(t * T, t * T + T)
        grad_out = jnp.concatenate([xlow[2, :, here], xhigh[2, :, here]], axis=0)
        faces.append(finish(both[:, here], 64, grad_out))
    corner = jnp.concatenate(
        [
            halves(cll[2].astype(F32), clh[2].astype(F32)),
            halves(chl[2].astype(F32), chh[2].astype(F32)),
        ],
        axis=0,
    )
    corner = finish(both[:, 8 * T :], 64, corner)
    part = jnp.dot(wf[...], ring[...], preferred_element_type=F32)
    rows = []
    for x in range(8):
        lo, hi = ylow[8 + x % 4].astype(F32), yhigh[8 + x % 4].astype(F32)
        rows.append(halves(lo, hi) if x < 4 else halves(swap_halves(lo), swap_halves(hi)))
    edges = finish(part, 256, jnp.concatenate(rows, axis=0))
    for x in range(-1, 9):
        if x < 0:
            field, near = jnp.concatenate([f[:C] for f in faces], axis=1).astype(BF16), corner[:C]
        elif x > 7:
            field, near = jnp.concatenate([f[C:] for f in faces], axis=1).astype(BF16), corner[C:]
        else:
            field, near = gp[x * C : x * C + C, :], edges[x * C : x * C + C]
        stack(cols, (x + 1) * C, 320, field, below_tile(field[:, 7 * T :], near), above_tile(field[:, :T], near))
    cols[960:, :] = jnp.zeros((64, 8 * T), BF16)
    for pair in range(4):
        both = jnp.dot(wd[...], cols[:, pair * 2 * T : pair * 2 * T + 2 * T], preferred_element_type=F32)
        for half in range(2):
            part = both[:, half * T : half * T + T]
            out = from_below(part[:256]) + part[256:512] + from_above(part[512:])
            for x in range(8):
                stage[x, pl.ds(pair * 2 + half, C, stride=8), :] = out[x * C : x * C + C]
    for x in range(8):
        for pair in range(C // 2):
            low, high = exchange_halves(stage[x, pl.ds(pair * 16, 8), :], stage[x, pl.ds(pair * 16 + 8, 8), :])
            data[x, :, pair * T : pair * T + T] = jnp.concatenate([low, high], axis=0).astype(BF16)


def back(parts, gp, wf, wr, wd, bias):
    scratch = [
        pltpu.VMEM((640, 9 * T), BF16),
        pltpu.VMEM((1024, T), BF16),
        pltpu.VMEM((1024, 8 * T), BF16),
        pltpu.VMEM((8, 8 * C, T), F32),
    ]
    out = jax.ShapeDtypeStruct((8, 16, C * Z), BF16)
    return call(back_body, out, scratch, 2_500_000_000, *parts, gp, wf, wr, wd, bias)


def finish_body(scale, wire, filters, biases):
    for k in range(27):
        tile = wire[k].astype(F32) * scale
        for q in range(4):
            moved = tile if q == 0 else pltpu.roll(tile, T - q * C, 1)
            filters[k, 8 * q : 8 * q + 8, :] = moved[:, :C]
    biases[...] = wire[27].astype(F32)[:1, :C] * scale


def finish(wire, scale):
    out = (jax.ShapeDtypeStruct((27, C, C), F32), jax.ShapeDtypeStruct((1, C), F32))
    return call(lambda *refs: finish_body(scale, *refs), out, [], 100_000, wire)


def shifted(array, axes, moves, sizes):
    pairs = []
    count = math.prod(sizes)
    for source in range(count):
        at, target, rest, inside = [], 0, source, True
        for size in reversed(sizes):
            at.append(rest % size)
            rest //= size
        for place, move, size in zip(reversed(at), moves, sizes):
            inside = inside and 0 <= place + move < size
            target = target * size + place + move
        if inside:
            pairs.append((source, target))
    return lax.ppermute(array, axes, pairs)


def total_over(wire, axis, size):
    step = 1
    while step < size:
        sent = wire.astype(BF16)
        got = lax.ppermute(sent, axis, [(i, i ^ step) for i in range(size)])
        wire = sent.astype(F32) + got.astype(F32)
        step *= 2
    return wire


def shards(volume, cotangent, weight, bias):
    nx, ny = lax.axis_size("gx"), lax.axis_size("gy")
    both, sizes = ("gx", "gy"), (nx, ny)
    vx, gx, xlow, xhigh, ylow, yhigh, cll, clh, chl, chh = pack(volume, cotangent)
    parts = (
        vx,
        gx,
        shifted(xhigh, both, (1, 0), sizes),
        shifted(xlow, both, (-1, 0), sizes),
        shifted(yhigh, both, (0, 1), sizes),
        shifted(ylow, both, (0, -1), sizes),
        shifted(chh, both, (1, 1), sizes),
        shifted(chl, both, (1, -1), sizes),
        shifted(clh, both, (-1, 1), sizes),
        shifted(cll, both, (-1, -1), sizes),
    )
    wf, wd, wr = bands(weight)
    offset = jnp.broadcast_to(jnp.tile(bias, 8)[:, None], (256, T))
    gp, wire = front(parts, wf, offset)
    data_grad = back(parts, gp, wf, wr, wd, offset)
    wire = wire.reshape(224, T)
    for axis, size in (("gx", nx), ("gy", ny)):
        wire = total_over(wire, axis, size)
    scale = 1.0 / math.sqrt(8 * nx * 16 * ny * Z)
    filters, biases = finish(wire.reshape(28, 8, T), scale)
    return data_grad, filters.reshape(3, 3, 3, C, C), biases.reshape(C)


def solution(mesh):
    in_specs = (P("gx", "gy", None), P("gx", "gy", None), P(), P())
    out_specs = (P("gx", "gy", None), P(), P())
    return jax.shard_map(shards, mesh=mesh, in_specs=in_specs, out_specs=out_specs, check_vma=False)
```

```python
import math

import jax
import jax.numpy as jnp
from jax import lax
from jax.experimental import pallas as pl
from jax.experimental.pallas import tpu as pltpu
from jax.sharding import PartitionSpec as P

C = 32
Z = 64
T = 128
ROW = 8 * T
F32 = jnp.float32
BF16 = jnp.bfloat16
VMEM_LIMIT = 48 * 1024 * 1024
VMEM = pl.BlockSpec(memory_space=pltpu.VMEM)
ANY = pl.BlockSpec(memory_space=pl.ANY)


def call(body, out_shape, scratch_shapes, flops, *args, in_specs=None, out_specs=None, aliases=None):
    traffic = sum(math.prod(a.shape) * a.dtype.itemsize for a in (*args, *jax.tree.leaves(out_shape)))
    return pl.pallas_call(
        body,
        out_shape=out_shape,
        in_specs=in_specs or [VMEM] * len(args),
        out_specs=out_specs or jax.tree.map(lambda _: VMEM, out_shape),
        scratch_shapes=scratch_shapes,
        input_output_aliases=aliases or {},
        compiler_params=pltpu.CompilerParams(vmem_limit_bytes=VMEM_LIMIT),
        cost_estimate=pl.CostEstimate(flops=flops, bytes_accessed=traffic, transcendentals=0),
    )(*args)


def like(dtype, *shape):
    return jax.ShapeDtypeStruct(shape, dtype)


def lane(shape):
    return lax.broadcasted_iota(jnp.int32, shape, len(shape) - 1)


def swap_halves(a):
    return pltpu.roll(a, T // 2, a.ndim - 1)


def halves(low, high):
    return jnp.where(lane(low.shape) < T // 2, low, high)


def exchange_halves(a, b):
    mixed = swap_halves(halves(b, a))
    return halves(a, mixed), halves(mixed, b)


def from_below(a):
    return jnp.where(lane(a.shape) % Z == 0, 0.0, pltpu.roll(a, 1, a.ndim - 1))


def from_above(a):
    return jnp.where(lane(a.shape) % Z == Z - 1, 0.0, pltpu.roll(a, T - 1, a.ndim - 1))


def tile(t):
    return slice(t * T, t * T + T)


def to_channels(rows, stage):
    rows = rows.astype(F32)
    for pair in range(C // 2):
        even, odd = exchange_halves(rows[:8, tile(pair)], rows[8:, tile(pair)])
        stage[pl.ds(pair * 16, 8), :] = even
        stage[pl.ds(pair * 16 + 8, 8), :] = odd
    return [stage[pl.ds(t, C, stride=8), :] for t in range(8)]


def going_down(first, second):
    return halves(second, swap_halves(first)).astype(BF16)


def going_up(last, second):
    return halves(swap_halves(last), second).astype(BF16)


def is_even(axis):
    return lax.axis_index(axis) % 2 == 0


def pack_body(v, g, vx, gx, even, odd, down, up, vbuf, gbuf, stage, sems):
    copies = []
    for x in (0, 7, 1, 6, 2, 3, 4, 5):
        pair = (
            pltpu.make_async_copy(v.at[x], vbuf.at[x], sems.at[0, x]),
            pltpu.make_async_copy(g.at[x], gbuf.at[x], sems.at[1, x]),
        )
        for copy in pair:
            copy.start()
        copies.append((x, pair))
    first, last = {}, {}
    for x, pair in copies:
        pair[0].wait()
        tiles = to_channels(vbuf[x], stage.at[x])
        for t in range(8):
            vx[x, :, tile(t)] = tiles[t].astype(BF16)
        down[x] = going_down(tiles[0], tiles[1])
        up[x] = going_up(tiles[7], tiles[6])
        pair[1].wait()
        tiles = to_channels(gbuf[x], stage.at[8 + x])
        for t in range(8):
            gx[x, :, tile(t)] = tiles[t].astype(BF16)
        first[x], last[x] = tiles[0], tiles[7]
    for x in range(4):
        down[8 + x] = going_down(first[x], first[x + 4])
        up[8 + x] = going_up(last[x], last[x + 4])
    low_out, high_out = is_even("gx"), jnp.logical_not(is_even("gx"))
    for when, low, high in ((low_out, odd, even), (high_out, even, odd)):

        @pl.when(when)
        def _(low=low, high=high):
            low[0:2] = vx[0:2]
            low[2] = gx[0]
            high[0:2] = vx[6:8]
            high[2] = gx[7]


def pack(volume, cotangent):
    field, face, edge = like(BF16, 8, C, ROW), like(BF16, 3, C, ROW), like(BF16, 12, C, T)
    scratch = [pltpu.VMEM((8, 16, C * Z), BF16)] * 2 + [pltpu.VMEM((16, 8 * C, T), F32), pltpu.SemaphoreType.DMA((2, 8))]
    out = (field, field, face, face, edge, edge)
    return call(pack_body, out, scratch, 2_000_000, volume, cotangent, in_specs=[ANY] * 2)


def sort(axis, even, odd, low, high):
    @pl.when(is_even(axis))
    def _():
        low[...] = odd[...]
        high[...] = even[...]

    @pl.when(jnp.logical_not(is_even(axis)))
    def _():
        low[...] = even[...]
        high[...] = odd[...]


def edges_body(down, up, xeven, xodd, even, odd, xlow, xhigh):
    sort("gx", xeven, xodd, xlow, xhigh)
    for when, to_low, to_high in ((is_even("gy"), odd, even), (jnp.logical_not(is_even("gy")), even, odd)):

        @pl.when(when)
        def _(to_low=to_low, to_high=to_high):
            to_low[2:10] = down[:8]
            to_low[12:16] = down[8:]
            to_high[2:10] = up[:8]
            to_high[12:16] = up[8:]
            for row, face, at in ((0, xlow, 0), (1, xlow, 1), (10, xhigh, 0), (11, xhigh, 1)):
                to_low[row] = going_down(face[at, :, tile(0)].astype(F32), face[at, :, tile(1)].astype(F32))
                to_high[row] = going_up(face[at, :, tile(7)].astype(F32), face[at, :, tile(6)].astype(F32))
            to_low[16] = going_down(xlow[2, :, tile(0)].astype(F32), xhigh[2, :, tile(0)].astype(F32))
            to_high[16] = going_up(xlow[2, :, tile(7)].astype(F32), xhigh[2, :, tile(7)].astype(F32))


def edges(down, up, xeven, xodd):
    edge, face = like(BF16, 17, C, T), like(BF16, 3, C, ROW)
    return call(edges_body, (edge, edge, face, face), [], 100_000, down, up, xeven, xodd)


def activation(pre, grad_out):
    sig = 1.0 / (1.0 + jnp.exp(-pre))
    return grad_out.astype(F32) * sig * (1.0 + pre * (1.0 - sig))


def below_tile(own_last, nearest):
    return halves(nearest.astype(F32), swap_halves(own_last.astype(F32))).astype(BF16)


def above_tile(own_first, nearest):
    return halves(swap_halves(own_first.astype(F32)), nearest.astype(F32)).astype(BF16)


def stack(out, i, field, below, above):
    row = i * 3 * C
    out[row : row + C, :T] = below
    out[row : row + C, T:ROW] = field[:, : 7 * T]
    out[row + C : row + 2 * C, :ROW] = field
    out[row + 2 * C : row + 3 * C, : 7 * T] = field[:, T:]
    out[row + 2 * C : row + 3 * C, 7 * T : ROW] = above


def step_z(part):
    return from_below(part[:64]) + part[64:128] + from_above(part[128:])


def volume_at(x, vx, xlow, xhigh, ylow, yhigh):
    field = xlow[x + 2] if x < 0 else xhigh[x - 8] if x > 7 else vx[x]
    return field, ylow[x + 2], yhigh[x + 2]


def front_body(vx, gx, xlow, xhigh, yeven, yodd, wf, bias, gp, wire, ylow, yhigh, cols, gps):
    sort("gy", yeven, yodd, ylow, yhigh)
    for x in range(-1, 9):
        field, low, high = volume_at(x, vx, xlow, xhigh, ylow, yhigh)
        stack(cols, x + 1, field, below_tile(field[:, tile(7)], low), above_tile(field[:, tile(0)], high))
    offset = jnp.concatenate([bias[...]] * 2, axis=0)
    total = jnp.zeros((64, T), F32)
    for q in range(4):
        both = jnp.dot(wf[...], cols[q * 192 : q * 192 + 384, :], preferred_element_type=F32)
        for t in range(8):
            grad_out = gx[2 * q : 2 * q + 2, :, tile(t)].reshape(64, T)
            grad = activation(step_z(both[:, tile(t)]) + offset, grad_out).astype(BF16)
            gp[q * 64 : q * 64 + 64, tile(t)] = grad
            grad = grad.astype(F32)
            total = total + grad
            gps[q * 192 : q * 192 + 64, tile(t)] = from_above(grad).astype(BF16)
            gps[q * 192 + 64 : q * 192 + 128, tile(t)] = grad.astype(BF16)
            gps[q * 192 + 128 : q * 192 + 192, tile(t)] = from_below(grad).astype(BF16)
    prod = jnp.zeros((384, 192), F32)
    for q in range(4):
        prod = prod + lax.dot_general(
            cols[q * 192 : q * 192 + 384, :],
            gps[q * 192 : q * 192 + 192, :],
            (((1,), (1,)), ((), ())),
            preferred_element_type=F32,
        )
    group = lane((8, T)) // C
    rows = []
    for row in range(0, 288, 8):
        a, b = prod[row : row + 8], prod[row + 96 : row + 104]
        a = jnp.concatenate([a[:, T:], jnp.zeros((8, 64), F32)], axis=1), a[:, :T]
        b = jnp.concatenate([b[:, T:], jnp.zeros((8, 64), F32)], axis=1), b[:, :T]
        near = a[1] + pltpu.roll(b[1], T - C, 1)
        far = a[0] + pltpu.roll(b[0], T - C, 1)
        rows.append((near, pltpu.roll(near, T - C, 1), pltpu.roll(far, 2 * C, 1), far))
    for i in range(27):
        near, moved, far, _ = rows[i]
        dz, at = divmod(i, 9)
        near2, moved2, far2, plain2 = rows[27 + at]
        last = pltpu.roll((near2, near2, plain2)[dz], (3 * C, C, 3 * C)[dz], 1)
        out = jnp.where(group == 0, near, jnp.where(group == 1, moved, jnp.where(group == 2, far, last)))
        wire[8 * i : 8 * i + 8] = out
    total = jnp.concatenate([total[:C] + total[C:], jnp.zeros((T - C, T), F32)], axis=0)
    total = jnp.sum(total.T, axis=0, keepdims=True)
    wire[216:] = jnp.broadcast_to(total, (8, T))


def front(vx, gx, xlow, xhigh, yeven, yodd, wf, bias):
    edge = like(BF16, 17, C, T)
    out = (like(BF16, 256, ROW), like(F32, 224, T), edge, edge)
    scratch = [pltpu.VMEM((960, ROW), BF16), pltpu.VMEM((768, ROW), BF16)]
    return call(front_body, out, scratch, 2_500_000_000, vx, gx, xlow, xhigh, yeven, yodd, wf, bias)


def ring_body(vx, xlow, xhigh, ylow, yhigh, wf, bias, faces, border, side, ring):
    for x in range(-2, 10):
        field, low, high = volume_at(x, vx, xlow, xhigh, ylow, yhigh)
        lo, hi = low.astype(F32), high.astype(F32)
        first, last = field[:, tile(0)].astype(F32), field[:, tile(7)].astype(F32)
        near = halves(lo, hi).astype(BF16)
        before = halves(swap_halves(lo), last).astype(BF16)
        after = halves(first, swap_halves(hi)).astype(BF16)
        if x <= 1 or x >= 6:
            i = x + 2 if x <= 1 else x - 2
            stack(side, i, field, below_tile(field[:, tile(7)], low), above_tile(field[:, tile(0)], high))
            for dy, part in enumerate((before, near, after)):
                side[i * 96 + dy * C : i * 96 + dy * C + C, ROW:] = part
        if -1 <= x <= 8:
            for dy, part in enumerate((before, near, after)):
                ring[(x + 1) * 96 + dy * C : (x + 1) * 96 + dy * C + C, :] = part
    offset = jnp.concatenate([bias[...]] * 2, axis=0)
    for face in range(2):
        both = jnp.dot(wf[...], side[face * 384 : face * 384 + 384, :], preferred_element_type=F32)
        mine = slice(face * C, face * C + C)
        far = (xlow, xhigh)[face]
        lo, hi = ylow[16].astype(F32), yhigh[16].astype(F32)
        corner = halves(swap_halves(lo), swap_halves(hi)) if face else halves(lo, hi)
        for t in range(9):
            pre = (step_z(both[:, tile(t)]) + offset)[mine]
            if t < 8:
                faces[face, :, tile(t)] = activation(pre, far[2, :, tile(t)]).astype(BF16)
            else:
                border[9 * face] = activation(pre, corner).astype(BF16)
    for q in range(4):
        part = jnp.dot(wf[...], ring[q * 192 : q * 192 + 384, :], preferred_element_type=F32)
        pre = step_z(part) + offset
        for side_x in range(2):
            x = 2 * q + side_x
            lo, hi = ylow[12 + x % 4].astype(F32), yhigh[12 + x % 4].astype(F32)
            grad_out = halves(lo, hi) if x < 4 else halves(swap_halves(lo), swap_halves(hi))
            border[x + 1] = activation(pre[side_x * C : side_x * C + C], grad_out).astype(BF16)


def ring(vx, xlow, xhigh, ylow, yhigh, wf, bias):
    scratch = [pltpu.VMEM((768, 9 * T), BF16), pltpu.VMEM((960, T), BF16)]
    out = (like(BF16, 2, C, ROW), like(BF16, 10, C, T))
    return call(ring_body, out, scratch, 800_000_000, vx, xlow, xhigh, ylow, yhigh, wf, bias)


def data_body(q, gp, faces, border, wd, *refs):
    data, cols, stage, block, sem = refs[-5:]
    for i in range(4):
        x = 2 * q + i - 1
        field = faces[0] if x < 0 else faces[1] if x > 7 else gp[x * C : x * C + C, :]
        near = border[x + 1]
        stack(cols, i, field, below_tile(field[:, tile(7)], near), above_tile(field[:, tile(0)], near))
    both = jnp.dot(wd[...], cols[...], preferred_element_type=F32)
    for t in range(8):
        out = step_z(both[:, tile(t)])
        for x in range(2):
            stage[x, pl.ds(t, C, stride=8), :] = out[x * C : x * C + C]
    for x in range(2):
        for pair in range(C // 2):
            low, high = exchange_halves(stage[x, pl.ds(pair * 16, 8), :], stage[x, pl.ds(pair * 16 + 8, 8), :])
            block[x, :, tile(pair)] = jnp.concatenate([low, high], axis=0).astype(BF16)
    copy = pltpu.make_async_copy(block, data.at[pl.ds(2 * q, 2)], sem)
    copy.start()
    copy.wait()


def data_piece(q, gp, faces, border, wd, before):
    scratch = [
        pltpu.VMEM((384, ROW), BF16),
        pltpu.VMEM((2, 8 * C, T), F32),
        pltpu.VMEM((2, 16, C * Z), BF16),
        pltpu.SemaphoreType.DMA,
    ]
    out = like(BF16, 8, 16, C * Z)
    args, specs, aliases = (gp, faces, border, wd), [VMEM] * 4, None
    if before is not None:
        args, specs, aliases = (*args, before), [*specs, ANY], {4: 0}
    return call(
        lambda *refs: data_body(q, *refs), out, scratch, 200_000_000, *args, in_specs=specs, out_specs=ANY, aliases=aliases
    )


def finish_body(scale, wire, filters, biases):
    for row in range(0, 288, 8):
        for dz in range(3):
            at, group = (row, dz) if row < 216 else (row - 216 + 72 * dz, 3)
            part = wire[at : at + 8]
            moved = part if group == 0 else pltpu.roll(part, T - group * C, 1)
            block, inside = divmod(row, C)
            filters[block * 3 + dz, inside : inside + 8, :] = moved[:, :C] * scale
    biases[...] = wire[216:217, :C] * scale


def finish(wire, scale):
    out = (like(F32, 27, C, C), like(F32, 1, C))
    return call(lambda *refs: finish_body(scale, *refs), out, [], 100_000, wire)


def swap(array, axis, size, odd):
    pairs = []
    for low in range(odd, size - 1, 2):
        pairs += [(low, low + 1), (low + 1, low)]
    return lax.ppermute(array, axis, pairs)


def band(strip):
    pad = [jnp.pad(strip, ((0, 0), (0, 0), (96 * x, 96 - 96 * x))) for x in range(2)]
    return jnp.stack(pad, axis=1).reshape(192, 384)


def shards(volume, cotangent, weight, bias):
    nx, ny = lax.axis_size("gx"), lax.axis_size("gy")
    wf = band(jnp.transpose(weight, (2, 4, 0, 1, 3)).reshape(3, C, 288))
    wd = band(jnp.transpose(weight[::-1, ::-1, ::-1], (2, 3, 0, 1, 4)).reshape(3, C, 288))
    offset = jnp.broadcast_to(bias[:, None], (C, T))
    vx, gx, xeven, xodd, down, up = pack(volume, cotangent)
    xodd = swap(xodd, "gx", nx, 1)
    xeven = swap(xeven, "gx", nx, 0)
    yeven, yodd, xlow, xhigh = edges(down, up, xeven, xodd)
    yodd = swap(yodd, "gy", ny, 1)
    yeven = swap(yeven, "gy", ny, 0)
    gp, wire, ylow, yhigh = front(vx, gx, xlow, xhigh, yeven, yodd, wf, offset)

    state = {}

    def border_piece(vx):
        state["ring"] = ring(vx, xlow, xhigh, ylow, yhigh, wf, offset)
        return state["ring"][0]

    def piece(q):
        def run(gp):
            state["data"] = data_piece(q, gp, *state["ring"], wd, state.get("data"))
            return state["data"]

        return run

    pieces = [(border_piece, vx, "ring")] + [(piece(q), gp, "data") for q in range(4)]
    steps = [(axis, size, 1 << b) for axis, size in (("gx", nx), ("gy", ny)) for b in range(size.bit_length() - 1)]
    for axis, size, step in steps:
        sent = wire.astype(BF16)
        work = pieces.pop(0) if pieces else None
        if work:
            sent, operand = lax.optimization_barrier((sent, work[1]))
        got = lax.ppermute(sent, axis, [(i, i ^ step) for i in range(size)])
        if work:
            work[0](operand)
            got, state[work[2]] = lax.optimization_barrier((got, state[work[2]]))
        wire = sent.astype(F32) + got.astype(F32)
    for work in pieces:
        work[0](work[1])
    scale = 1.0 / math.sqrt(8 * nx * 16 * ny * Z)
    filters, biases = finish(wire, scale)
    return state["data"], filters.reshape(3, 3, 3, C, C), biases.reshape(C)


def solution(mesh):
    in_specs = (P("gx", "gy", None), P("gx", "gy", None), P(), P())
    out_specs = (P("gx", "gy", None), P(), P())
    return jax.shard_map(shards, mesh=mesh, in_specs=in_specs, out_specs=out_specs, check_vma=False)
```

```python
import math

import jax
import jax.numpy as jnp
from jax import lax
from jax.experimental import pallas as pl
from jax.experimental.pallas import tpu as pltpu
from jax.sharding import PartitionSpec as P

C = 32
Z = 64
T = 128
ROW = 8 * T
F32 = jnp.float32
BF16 = jnp.bfloat16
VMEM_LIMIT = 48 * 1024 * 1024
VMEM = pl.BlockSpec(memory_space=pltpu.VMEM)
HBM = pl.BlockSpec(memory_space=pltpu.HBM)


def call(body, out_shape, scratch_shapes, flops, *args, in_specs=None, out_specs=None, aliases=None):
    traffic = sum(math.prod(a.shape) * a.dtype.itemsize for a in (*args, *jax.tree.leaves(out_shape)))
    return pl.pallas_call(
        body,
        out_shape=out_shape,
        in_specs=in_specs or [VMEM] * len(args),
        out_specs=out_specs or jax.tree.map(lambda _: VMEM, out_shape),
        scratch_shapes=scratch_shapes,
        input_output_aliases=aliases or {},
        compiler_params=pltpu.CompilerParams(vmem_limit_bytes=VMEM_LIMIT),
        cost_estimate=pl.CostEstimate(flops=flops, bytes_accessed=traffic, transcendentals=0),
    )(*args)


def like(dtype, *shape):
    return jax.ShapeDtypeStruct(shape, dtype)


def lane(shape):
    return lax.broadcasted_iota(jnp.int32, shape, len(shape) - 1)


def swap_halves(a):
    return pltpu.roll(a, T // 2, a.ndim - 1)


def halves(low, high):
    return jnp.where(lane(low.shape) < T // 2, low, high)


def exchange_halves(a, b):
    mixed = swap_halves(halves(b, a))
    return halves(a, mixed), halves(mixed, b)


def from_below(a):
    return jnp.where(lane(a.shape) % Z == 0, 0.0, pltpu.roll(a, 1, a.ndim - 1))


def from_above(a):
    return jnp.where(lane(a.shape) % Z == Z - 1, 0.0, pltpu.roll(a, T - 1, a.ndim - 1))


def tile(t):
    return slice(t * T, t * T + T)


def to_channels(rows, stage):
    rows = rows.astype(F32)
    for pair in range(C // 2):
        even, odd = exchange_halves(rows[:8, tile(pair)], rows[8:, tile(pair)])
        stage[pl.ds(pair * 16, 8), :] = even
        stage[pl.ds(pair * 16 + 8, 8), :] = odd
    return [stage[pl.ds(t, C, stride=8), :] for t in range(8)]


def is_even(axis):
    return lax.axis_index(axis) % 2 == 0


def pack_body(v, g, vx, gx, even, odd, vbuf, gbuf, stage, sems):
    copies = []
    for x in (0, 7, 1, 2, 3, 4, 5, 6):
        copies.append((x, v, vbuf, vx, 0))
    for x in range(8):
        copies.append((x, g, gbuf, gx, 1))
    copies = [(x, out, buf, pltpu.make_async_copy(src.at[x], buf.at[x], sems.at[k, x])) for x, src, buf, out, k in copies]
    for *_, copy in copies:
        copy.start()
    for n, (x, out, buf, copy) in enumerate(copies):
        copy.wait()
        for t, part in enumerate(to_channels(buf[x], stage.at[n])):
            out[x, :, tile(t)] = part.astype(BF16)
    faces(vx, even, odd)


def faces(field, even, odd):
    for when, low, high in ((is_even("gx"), odd, even), (jnp.logical_not(is_even("gx")), even, odd)):

        @pl.when(when)
        def _(low=low, high=high):
            low[...] = field[0]
            high[...] = field[7]


def pack(volume, cotangent):
    field, face = like(BF16, 8, C, ROW), like(BF16, C, ROW)
    scratch = [pltpu.VMEM((8, 16, C * Z), BF16)] * 2 + [pltpu.VMEM((16, 8 * C, T), F32), pltpu.SemaphoreType.DMA((2, 8))]
    return call(pack_body, (field, field, face, face), scratch, 2_000_000, volume, cotangent, in_specs=[HBM] * 2)


def sort(axis, even, odd, low, high):
    @pl.when(is_even(axis))
    def _():
        low[...] = odd[...]
        high[...] = even[...]

    @pl.when(jnp.logical_not(is_even(axis)))
    def _():
        low[...] = even[...]
        high[...] = odd[...]


def edges_body(field, xeven, xodd, even, odd, xlow, xhigh):
    sort("gx", xeven, xodd, xlow, xhigh)

    def at(x, t):
        source = xlow if x < 0 else xhigh if x > 7 else field.at[x]
        return source[:, tile(t)].astype(F32)

    for when, to_low, to_high in ((is_even("gy"), odd, even), (jnp.logical_not(is_even("gy")), even, odd)):

        @pl.when(when)
        def _(to_low=to_low, to_high=to_high):
            for row in range(5):
                to_low[row] = halves(at(row + 4, 0), swap_halves(at(row - 1, 0))).astype(BF16)
                to_high[row] = halves(swap_halves(at(row - 1, 7)), at(row + 4, 7)).astype(BF16)


def edges(field, xeven, xodd):
    edge, face = like(BF16, 5, C, T), like(BF16, C, ROW)
    return call(edges_body, (edge, edge, face, face), [], 100_000, field, xeven, xodd)


def sort_edges(even, odd, near):
    for when, low, high in ((is_even("gy"), odd, even), (jnp.logical_not(is_even("gy")), even, odd)):

        @pl.when(when)
        def _(low=low, high=high):
            for row in range(5):
                a, b = low[row].astype(F32), high[row].astype(F32)
                near[row] = halves(a, b)
                near[row + 5] = halves(swap_halves(a), swap_halves(b))


def activation(pre, grad_out):
    sig = 1.0 / (1.0 + jnp.exp(-pre))
    return grad_out.astype(F32) * sig * (1.0 + pre * (1.0 - sig))


def stack(out, i, field, near):
    row = i * 3 * C
    out[row : row + C, :T] = halves(near, swap_halves(field[:, tile(7)].astype(F32))).astype(BF16)
    out[row : row + C, T:] = field[:, : 7 * T]
    out[row + C : row + 2 * C, :] = field[...]
    out[row + 2 * C : row + 3 * C, : 7 * T] = field[:, T:]
    out[row + 2 * C : row + 3 * C, 7 * T :] = halves(swap_halves(field[:, tile(0)].astype(F32)), near).astype(BF16)


def step_z(part):
    return from_below(part[:64]) + part[64:128] + from_above(part[128:])


def field_at(x, field, xlow, xhigh):
    return xlow if x < 0 else xhigh if x > 7 else field.at[x]


def front_body(vx, gx, xlow, xhigh, yeven, yodd, wf, bias, gp, even, odd, wire, near, cols, gps):
    sort_edges(yeven, yodd, near)
    for x in range(-1, 9):
        stack(cols, x + 1, field_at(x, vx, xlow, xhigh), near[x + 1])
    offset = jnp.concatenate([bias[...]] * 2, axis=0)
    total = jnp.zeros((64, T), F32)
    for q in range(4):
        both = jnp.dot(wf[...], cols[q * 192 : q * 192 + 384, :], preferred_element_type=F32)
        for t in range(8):
            grad_out = gx[2 * q : 2 * q + 2, :, tile(t)].reshape(64, T)
            grad = activation(step_z(both[:, tile(t)]) + offset, grad_out).astype(BF16)
            gp[2 * q : 2 * q + 2, :, tile(t)] = grad.reshape(2, C, T)
            grad = grad.astype(F32)
            total = total + grad
            gps[q * 192 : q * 192 + 64, tile(t)] = from_above(grad).astype(BF16)
            gps[q * 192 + 64 : q * 192 + 128, tile(t)] = grad.astype(BF16)
            gps[q * 192 + 128 : q * 192 + 192, tile(t)] = from_below(grad).astype(BF16)
    faces(gp, even, odd)
    prod = jnp.zeros((384, 192), F32)
    for q in range(4):
        prod = prod + lax.dot_general(
            cols[q * 192 : q * 192 + 384, :],
            gps[q * 192 : q * 192 + 192, :],
            (((1,), (1,)), ((), ())),
            preferred_element_type=F32,
        )
    group = lane((8, T)) // C
    rows = []
    for row in range(0, 288, 8):
        a, b = prod[row : row + 8], prod[row + 96 : row + 104]
        a = jnp.concatenate([a[:, T:], jnp.zeros((8, 64), F32)], axis=1), a[:, :T]
        b = jnp.concatenate([b[:, T:], jnp.zeros((8, 64), F32)], axis=1), b[:, :T]
        near = a[1] + pltpu.roll(b[1], T - C, 1)
        far = a[0] + pltpu.roll(b[0], T - C, 1)
        rows.append((near, pltpu.roll(near, T - C, 1), pltpu.roll(far, 2 * C, 1), far))
    for i in range(27):
        near, moved, far, _ = rows[i]
        dz, at = divmod(i, 9)
        near2, moved2, far2, plain2 = rows[27 + at]
        last = pltpu.roll((near2, near2, plain2)[dz], (3 * C, C, 3 * C)[dz], 1)
        out = jnp.where(group == 0, near, jnp.where(group == 1, moved, jnp.where(group == 2, far, last)))
        wire[8 * i : 8 * i + 8] = out
    total = jnp.concatenate([total[:C] + total[C:], jnp.zeros((T - C, T), F32)], axis=0)
    total = jnp.sum(total.T, axis=0, keepdims=True)
    wire[216:] = jnp.broadcast_to(total, (8, T))


def front(vx, gx, xlow, xhigh, yeven, yodd, wf, bias):
    face = like(BF16, C, ROW)
    out = (like(BF16, 8, C, ROW), face, face, like(F32, 224, T))
    scratch = [pltpu.VMEM((10, C, T), F32), pltpu.VMEM((960, ROW), BF16), pltpu.VMEM((768, ROW), BF16)]
    return call(front_body, out, scratch, 2_500_000_000, vx, gx, xlow, xhigh, yeven, yodd, wf, bias)


def back_body(gp, xlow, xhigh, yeven, yodd, wd, data, near, cols, stage, block, sems):
    sort_edges(yeven, yodd, near)
    for x in range(-1, 9):
        stack(cols, x + 1, field_at(x, gp, xlow, xhigh), near[x + 1])
    copies = []
    for q in range(4):
        both = jnp.dot(wd[...], cols[q * 192 : q * 192 + 384, :], preferred_element_type=F32)
        for t in range(8):
            out = step_z(both[:, tile(t)])
            for x in range(2):
                stage[2 * q + x, pl.ds(t, C, stride=8), :] = out[x * C : x * C + C]
        for x in (2 * q, 2 * q + 1):
            for pair in range(C // 2):
                even, odd = stage[x, pl.ds(pair * 16, 8), :], stage[x, pl.ds(pair * 16 + 8, 8), :]
                block[x, :, tile(pair)] = jnp.concatenate(exchange_halves(even, odd), axis=0).astype(BF16)
        copies.append(pltpu.make_async_copy(block.at[pl.ds(2 * q, 2)], data.at[pl.ds(2 * q, 2)], sems.at[q]))
        copies[-1].start()
    for copy in copies:
        copy.wait()


def back(gp, xlow, xhigh, yeven, yodd, wd):
    scratch = [
        pltpu.VMEM((10, C, T), F32),
        pltpu.VMEM((960, ROW), BF16),
        pltpu.VMEM((8, 8 * C, T), F32),
        pltpu.VMEM((8, 16, C * Z), BF16),
        pltpu.SemaphoreType.DMA((4,)),
    ]
    out = like(BF16, 8, 16, C * Z)
    return call(back_body, out, scratch, 1_000_000_000, gp, xlow, xhigh, yeven, yodd, wd, out_specs=HBM)


def add_body(a, b, out):
    out[...] = (a[...].astype(F32) + b[...].astype(F32)).astype(out.dtype)


def add(a, b, dtype):
    return call(add_body, like(dtype, *a.shape), [], 100_000, a, b)


def finish_body(scale, own, other, filters, biases):
    for when, wire in ((is_even("gx"), other), (jnp.logical_not(is_even("gx")), own)):

        @pl.when(when)
        def _(wire=wire):
            for row in range(0, 288, 8):
                for dz in range(3):
                    at, group = (row, dz) if row < 216 else (row - 216 + 72 * dz, 3)
                    part = wire[at : at + 8]
                    moved = part if group == 0 else pltpu.roll(part, T - group * C, 1)
                    block, inside = divmod(row, C)
                    filters[block * 3 + dz, inside : inside + 8, :] = moved[:, :C] * scale
            biases[...] = wire[216:217, :C] * scale


def finish(own, other, scale):
    out = (like(F32, 27, C, C), like(F32, 1, C))
    return call(lambda *refs: finish_body(scale, *refs), out, [], 100_000, own, other)


def swap(array, axis, size, odd):
    pairs = []
    for low in range(odd, size - 1, 2):
        pairs += [(low, low + 1), (low + 1, low)]
    return lax.ppermute(array, axis, pairs)


def band(strip):
    pad = [jnp.pad(strip, ((0, 0), (0, 0), (96 * x, 96 - 96 * x))) for x in range(2)]
    return jnp.stack(pad, axis=1).reshape(192, 384)


def shards(volume, cotangent, weight, bias):
    nx, ny = lax.axis_size("gx"), lax.axis_size("gy")
    wf = band(jnp.transpose(weight, (2, 4, 0, 1, 3)).reshape(3, C, 288))
    wd = band(jnp.transpose(weight[::-1, ::-1, ::-1], (2, 3, 0, 1, 4)).reshape(3, C, 288))
    vx, gx, xeven, xodd = pack(volume, cotangent)
    xodd, bias = lax.optimization_barrier((xodd, bias))
    offset = jnp.broadcast_to(bias[:, None], (C, T))
    xodd = swap(xodd, "gx", nx, 1)
    xeven = swap(xeven, "gx", nx, 0)
    xodd, offset = lax.optimization_barrier((xodd, offset))
    yeven, yodd, xlow, xhigh = edges(vx, xeven, xodd)
    yodd = swap(yodd, "gy", ny, 1)
    yeven = swap(yeven, "gy", ny, 0)
    gp, xeven, xodd, wire = front(vx, gx, xlow, xhigh, yeven, yodd, wf, offset)

    state = dict(gp=gp, xeven=xeven, xodd=xodd)

    def along_x():
        state["xodd"] = swap(state["xodd"], "gx", nx, 1)
        state["xeven"] = swap(state["xeven"], "gx", nx, 0)

    def along_y():
        yeven, yodd, xlow, xhigh = edges(state["gp"], state.pop("xeven"), state.pop("xodd"))
        state.update(yeven=yeven, yodd=yodd, xlow=xlow, xhigh=xhigh)
        state["yeven"] = swap(yeven, "gy", ny, 0)

    def along_y_odd():
        state["yodd"] = swap(state["yodd"], "gy", ny, 1)

    def data():
        state["data"] = back(state["gp"], state["xlow"], state["xhigh"], state["yeven"], state["yodd"], wd)

    def beside(work, sent, move):
        sent, given = lax.optimization_barrier((sent, dict(state)))
        state.update(given)
        got = move(sent)
        work()
        return sent, got

    def between(axis, step):
        pairs = []
        for x in range(1, nx, 2):
            for y in range(ny):
                to = (x ^ step, y) if axis == "gx" else (x, y ^ step)
                pairs.append((x * ny + y, to[0] * ny + to[1]))
        return lambda sent: lax.ppermute(sent, ("gx", "gy"), pairs)

    wire = add(wire, swap(wire, "gx", nx, 0), BF16)
    steps = [("gx", 1 << b) for b in range(1, nx.bit_length() - 1)] + [("gy", 1 << b) for b in range(ny.bit_length() - 1)]
    works = [along_x, along_y, along_y_odd, data]
    for n, (axis, step) in enumerate(steps):
        work = works.pop(0) if works else lambda: None
        sent, got = beside(work, wire, between(axis, step))
        last = n == len(steps) - 1
        if "data" in state:
            got, state["data"] = lax.optimization_barrier((got, state["data"]))
        wire = add(sent, got, F32 if last else BF16)
    for work in works:
        work()
    scale = 1.0 / math.sqrt(8 * nx * 16 * ny * Z)
    filters, biases = finish(wire, swap(wire, "gx", nx, 0), scale)
    return state["data"], filters.reshape(3, 3, 3, C, C), biases.reshape(C)


def solution(mesh):
    in_specs = (P("gx", "gy", None), P("gx", "gy", None), P(), P())
    out_specs = (P("gx", "gy", None), P(), P())
    return jax.shard_map(shards, mesh=mesh, in_specs=in_specs, out_specs=out_specs, check_vma=False)
```

```python
import math

import jax
import jax.numpy as jnp
from jax import lax
from jax.experimental import pallas as pl
from jax.experimental.pallas import tpu as pltpu
from jax.sharding import PartitionSpec as P

C = 32
Z = 64
T = 128
ROW = 8 * T
HALF = 112
F32 = jnp.float32
BF16 = jnp.bfloat16
VMEM_LIMIT = 48 * 1024 * 1024
VMEM = pl.BlockSpec(memory_space=pltpu.VMEM)
HBM = pl.BlockSpec(memory_space=pltpu.HBM)


def call(body, out_shape, scratch_shapes, flops, *args, in_specs=None, out_specs=None, aliases=None):
    traffic = sum(math.prod(a.shape) * a.dtype.itemsize for a in (*args, *jax.tree.leaves(out_shape)))
    return pl.pallas_call(
        body,
        out_shape=out_shape,
        in_specs=in_specs or [VMEM] * len(args),
        out_specs=out_specs or jax.tree.map(lambda _: VMEM, out_shape),
        scratch_shapes=scratch_shapes,
        input_output_aliases=aliases or {},
        compiler_params=pltpu.CompilerParams(vmem_limit_bytes=VMEM_LIMIT),
        cost_estimate=pl.CostEstimate(flops=flops, bytes_accessed=traffic, transcendentals=0),
    )(*args)


def like(dtype, *shape):
    return jax.ShapeDtypeStruct(shape, dtype)


def lane(shape):
    return lax.broadcasted_iota(jnp.int32, shape, len(shape) - 1)


def swap_halves(a):
    return pltpu.roll(a, T // 2, a.ndim - 1)


def halves(low, high):
    return jnp.where(lane(low.shape) < T // 2, low, high)


def exchange_halves(a, b):
    mixed = swap_halves(halves(b, a))
    return halves(a, mixed), halves(mixed, b)


def from_below(a):
    return jnp.where(lane(a.shape) % Z == 0, 0.0, pltpu.roll(a, 1, a.ndim - 1))


def from_above(a):
    return jnp.where(lane(a.shape) % Z == Z - 1, 0.0, pltpu.roll(a, T - 1, a.ndim - 1))


def tile(t):
    return slice(t * T, t * T + T)


def to_channels(rows, stage):
    rows = rows.astype(F32)
    for pair in range(C // 2):
        even, odd = exchange_halves(rows[:8, tile(pair)], rows[8:, tile(pair)])
        stage[pl.ds(pair * 16, 8), :] = even
        stage[pl.ds(pair * 16 + 8, 8), :] = odd
    return [stage[pl.ds(t, C, stride=8), :] for t in range(8)]


def is_even(axis):
    return lax.axis_index(axis) % 2 == 0


def clear_ends(axis, low, high):
    @pl.when(lax.axis_index(axis) == 0)
    def _():
        low[...] = jnp.zeros_like(low)

    @pl.when(lax.axis_index(axis) == lax.axis_size(axis) - 1)
    def _():
        high[...] = jnp.zeros_like(high)


def my_half():
    total = 0
    for axis in ("gx", "gy"):
        for b in range(lax.axis_size(axis).bit_length() - 1):
            total = total + lax.axis_index(axis) // (1 << b)
    return total % 2


def faces(field, even, odd):
    for when, low, high in ((is_even("gx"), odd, even), (jnp.logical_not(is_even("gx")), even, odd)):

        @pl.when(when)
        def _(low=low, high=high):
            for t in range(8):
                low[:, tile(t)] = field(0, t)
                high[:, tile(t)] = field(7, t)


def pack_body(v, vx, *refs):
    stage = refs[-1]
    for x in range(8):
        for t, part in enumerate(to_channels(v[x], stage.at[x])):
            vx[x, :, tile(t)] = part.astype(BF16)
    if len(refs) > 1:
        faces(whole(vx), *refs[:2])


def pack(array, with_faces):
    face = like(BF16, C, ROW)
    out = (like(BF16, 8, C, ROW),) + (face, face) * with_faces
    return call(pack_body, out, [pltpu.VMEM((8, 8 * C, T), F32)], 1_000_000, array)


def whole(ref):
    return lambda x, t: ref[x, :, tile(t)]


def split(mid, edge):
    return lambda x, t: edge[x, :, tile(t // 7)] if t in (0, 7) else mid[x, :, tile(t - 1)]


def with_faces(field, xlow, xhigh):
    return lambda x, t: xlow[:, tile(t)] if x < 0 else xhigh[:, tile(t)] if x > 7 else field(x, t)


def faces_body(mid, edge, even, odd):
    faces(split(mid, edge), even, odd)


def gradient_faces(mid, edge):
    face = like(BF16, C, ROW)
    return call(faces_body, (face, face), [], 100_000, mid, edge)


def sort(axis, even, odd, low, high):
    @pl.when(is_even(axis))
    def _():
        low[...] = odd[...]
        high[...] = even[...]

    @pl.when(jnp.logical_not(is_even(axis)))
    def _():
        low[...] = even[...]
        high[...] = odd[...]

    clear_ends(axis, low, high)


def edge_message(field, low_when, out):
    @pl.when(low_when)
    def _():
        for row in range(5):
            out[row] = halves(field(row + 4, 0).astype(F32), swap_halves(field(row - 1, 0).astype(F32))).astype(BF16)

    @pl.when(jnp.logical_not(low_when))
    def _():
        for row in range(5):
            out[row] = halves(swap_halves(field(row - 1, 7).astype(F32)), field(row + 4, 7).astype(F32)).astype(BF16)


def ends(ref):
    last = ref.shape[-1] // T - 1
    return lambda x, t: ref[x, :, tile(last if t else 0)]


def odd_edge_body(field, xeven, xodd, out, xlow, xhigh):
    sort("gx", xeven, xodd, xlow, xhigh)
    edge_message(with_faces(ends(field), xlow, xhigh), is_even("gy"), out)


def odd_edge(field, xeven, xodd):
    face = like(BF16, C, ROW)
    return call(odd_edge_body, (like(BF16, 5, C, T), face, face), [], 100_000, field, xeven, xodd)


def even_edge_body(field, xlow, xhigh, out):
    edge_message(with_faces(ends(field), xlow, xhigh), jnp.logical_not(is_even("gy")), out)


def even_edge(field, xlow, xhigh):
    return call(even_edge_body, like(BF16, 5, C, T), [], 100_000, field, xlow, xhigh)


def sort_edges(even, odd, near):
    for when, low, high in ((is_even("gy"), odd, even), (jnp.logical_not(is_even("gy")), even, odd)):

        @pl.when(when)
        def _(low=low, high=high):
            for row in range(5):
                a, b = low[row].astype(F32), high[row].astype(F32)
                near[row] = halves(a, b)
                near[row + 5] = halves(swap_halves(a), swap_halves(b))

    place = lax.axis_index("gy")
    for when, empty in ((place == 0, 0), (place == lax.axis_size("gy") - 1, 1)):

        @pl.when(when)
        def _(empty=empty):
            for row in range(10):
                near[row] = halves(near[row], jnp.zeros((C, T), F32)) if empty else halves(jnp.zeros((C, T), F32), near[row])


def activation(pre, grad_out):
    sig = 1.0 / (1.0 + jnp.exp(-pre))
    return grad_out.astype(F32) * sig * (1.0 + pre * (1.0 - sig))


def stack(out, i, tiles, field, near=None):
    for n, t in enumerate(tiles):
        for dy in range(3):
            if t + dy == 0:
                part = halves(near, swap_halves(field(7).astype(F32))).astype(BF16)
            elif t + dy == 9:
                part = halves(swap_halves(field(0).astype(F32)), near).astype(BF16)
            else:
                part = field(t + dy - 1)
            out[(3 * i + dy) * C : (3 * i + dy + 1) * C, tile(n)] = part


def step_z(part):
    return from_below(part[:64]) + part[64:128] + from_above(part[128:])


def gradient(tiles, gx, wf, bias, cols, gps, out):
    offset = jnp.concatenate([bias[...]] * 2, axis=0)
    total = jnp.zeros((64, T), F32)
    for q in range(4):
        both = jnp.dot(wf[...], cols[q * 192 : q * 192 + 384, :], preferred_element_type=F32)
        for n, t in enumerate(tiles):
            grad_out = gx[2 * q : 2 * q + 2, :, tile(t)].reshape(64, T)
            grad = activation(step_z(both[:, tile(n)]) + offset, grad_out).astype(BF16)
            out[2 * q : 2 * q + 2, :, tile(n)] = grad.reshape(2, C, T)
            grad = grad.astype(F32)
            total = total + grad
            gps[q * 192 : q * 192 + 64, tile(n)] = from_above(grad).astype(BF16)
            gps[q * 192 + 64 : q * 192 + 128, tile(n)] = grad.astype(BF16)
            gps[q * 192 + 128 : q * 192 + 192, tile(n)] = from_below(grad).astype(BF16)
    prod = jnp.zeros((384, 192), F32)
    for q in range(4):
        prod = prod + lax.dot_general(
            cols[q * 192 : q * 192 + 384, :],
            gps[q * 192 : q * 192 + 192, :],
            (((1,), (1,)), ((), ())),
            preferred_element_type=F32,
        )
    return total, prod


MID = range(1, 7)
EDGE = (0, 7)


def middle_body(vx, gx, xlow, xhigh, wf, bias, gmid, total, prod, cols, gps):
    field = with_faces(whole(vx), xlow, xhigh)
    for x in range(-1, 9):
        stack(cols, x + 1, MID, lambda t, x=x: field(x, t))
    total[...], prod[...] = gradient(MID, gx, wf, bias, cols, gps, gmid)


def middle(vx, gx, xlow, xhigh, wf, bias):
    out = (like(BF16, 8, C, 6 * T), like(F32, 64, T), like(F32, 384, 192))
    scratch = [pltpu.VMEM((960, 6 * T), BF16), pltpu.VMEM((768, 6 * T), BF16)]
    return call(middle_body, out, scratch, 1_800_000_000, vx, gx, xlow, xhigh, wf, bias)


def outer_body(vx, gx, xlow, xhigh, yeven, yodd, wf, bias, total, prod, gedge, keep, give, near, cols, gps, wire):
    sort_edges(yeven, yodd, near)
    field = with_faces(whole(vx), xlow, xhigh)
    for x in range(-1, 9):
        stack(cols, x + 1, EDGE, lambda t, x=x: field(x, t), near[x + 1])
    more_total, more = gradient(EDGE, gx, wf, bias, cols, gps, gedge)
    total, prod = total[...] + more_total, prod[...] + more
    group = lane((8, T)) // C
    rows = []
    for row in range(0, 288, 8):
        a, b = prod[row : row + 8], prod[row + 96 : row + 104]
        a = jnp.concatenate([a[:, T:], jnp.zeros((8, 64), F32)], axis=1), a[:, :T]
        b = jnp.concatenate([b[:, T:], jnp.zeros((8, 64), F32)], axis=1), b[:, :T]
        near = a[1] + pltpu.roll(b[1], T - C, 1)
        far = a[0] + pltpu.roll(b[0], T - C, 1)
        rows.append((near, pltpu.roll(near, T - C, 1), pltpu.roll(far, 2 * C, 1), far))
    for i in range(27):
        near, moved, far, _ = rows[i]
        dz, at = divmod(i, 9)
        near2, moved2, far2, plain2 = rows[27 + at]
        last = pltpu.roll((near2, near2, plain2)[dz], (3 * C, C, 3 * C)[dz], 1)
        out = jnp.where(group == 0, near, jnp.where(group == 1, moved, jnp.where(group == 2, far, last)))
        wire[8 * i : 8 * i + 8] = out
    total = jnp.concatenate([total[:C] + total[C:], jnp.zeros((T - C, T), F32)], axis=0)
    total = jnp.sum(total.T, axis=0, keepdims=True)
    wire[216:] = jnp.broadcast_to(total, (8, T))
    for half in range(2):

        @pl.when(my_half() == half)
        def _(half=half):
            keep[...] = wire[half * HALF : half * HALF + HALF]
            give[...] = wire[HALF - half * HALF : 2 * HALF - half * HALF]


def outer(vx, gx, xlow, xhigh, yeven, yodd, wf, bias, total, prod):
    out = (like(BF16, 8, C, 2 * T), like(F32, HALF, T), like(F32, HALF, T))
    scratch = [
        pltpu.VMEM((10, C, T), F32),
        pltpu.VMEM((960, 2 * T), BF16),
        pltpu.VMEM((768, 2 * T), BF16),
        pltpu.VMEM((2 * HALF, T), F32),
    ]
    args = (vx, gx, xlow, xhigh, yeven, yodd, wf, bias, total, prod)
    return call(outer_body, out, scratch, 700_000_000, *args)


def back_body(gmid, gedge, xlow, xhigh, yeven, yodd, wd, data, near, cols, stage, block, sems):
    sort_edges(yeven, yodd, near)
    field = with_faces(split(gmid, gedge), xlow, xhigh)
    for x in range(-1, 9):
        stack(cols, x + 1, range(8), lambda t, x=x: field(x, t), near[x + 1])
    copies = []
    for q in range(4):
        both = jnp.dot(wd[...], cols[q * 192 : q * 192 + 384, :], preferred_element_type=F32)
        for t in range(8):
            out = step_z(both[:, tile(t)])
            for x in range(2):
                stage[2 * q + x, pl.ds(t, C, stride=8), :] = out[x * C : x * C + C]
        for x in (2 * q, 2 * q + 1):
            for pair in range(C // 2):
                even, odd = stage[x, pl.ds(pair * 16, 8), :], stage[x, pl.ds(pair * 16 + 8, 8), :]
                block[x, :, tile(pair)] = jnp.concatenate(exchange_halves(even, odd), axis=0).astype(BF16)
        copies.append(pltpu.make_async_copy(block.at[pl.ds(2 * q, 2)], data.at[pl.ds(2 * q, 2)], sems.at[q]))
        copies[-1].start()
    for copy in copies:
        copy.wait()


def back(gmid, gedge, xlow, xhigh, yeven, yodd, wd):
    scratch = [
        pltpu.VMEM((10, C, T), F32),
        pltpu.VMEM((960, ROW), BF16),
        pltpu.VMEM((8, 8 * C, T), F32),
        pltpu.VMEM((8, 16, C * Z), BF16),
        pltpu.SemaphoreType.DMA((4,)),
    ]
    out = like(BF16, 8, 16, C * Z)
    return call(back_body, out, scratch, 1_000_000_000, gmid, gedge, xlow, xhigh, yeven, yodd, wd, out_specs=HBM)


def add_body(a, b, out):
    out[...] = (a[...].astype(F32) + b[...].astype(F32)).astype(out.dtype)


def add(a, b, dtype):
    return call(add_body, like(dtype, *a.shape), [], 100_000, a, b)


def finish_body(scale, own, other, filters, biases):
    for half, halves_of in enumerate(((own, other), (other, own))):

        @pl.when(my_half() == half)
        def _(halves_of=halves_of):
            for row in range(0, 288, 8):
                for dz in range(3):
                    at, group = (row, dz) if row < 216 else (row - 216 + 72 * dz, 3)
                    part = halves_of[at // HALF][at % HALF : at % HALF + 8]
                    moved = part if group == 0 else pltpu.roll(part, T - group * C, 1)
                    block, inside = divmod(row, C)
                    filters[block * 3 + dz, inside : inside + 8, :] = moved[:, :C] * scale
            biases[...] = halves_of[1][216 - HALF : 217 - HALF, :C] * scale


def finish(own, other, scale):
    out = (like(F32, 27, C, C), like(F32, 1, C))
    return call(lambda *refs: finish_body(scale, *refs), out, [], 100_000, own, other)


def permute(array, target):
    nx, ny = lax.axis_size("gx"), lax.axis_size("gy")
    pairs = []
    for x in range(nx):
        for y in range(ny):
            to = target(x, y)
            pairs.append((x * ny + y, to[0] * ny + to[1]))
    return lax.ppermute(array, ("gx", "gy"), pairs)


def swap_x(array, odd):
    nx = lax.axis_size("gx")
    return permute(array, lambda x, y: ((((x + odd) ^ 1) - odd) % nx, y))


def swap_y(array, odd):
    ny = lax.axis_size("gy")

    def target(x, y):
        to = ((y + odd) ^ 1) - odd
        return (x, to) if 0 <= to < ny else (x ^ 1, y)

    return permute(array, target)


def band(strip):
    pad = [jnp.pad(strip, ((0, 0), (0, 0), (96 * x, 96 - 96 * x))) for x in range(2)]
    return jnp.stack(pad, axis=1).reshape(192, 384)


def shards(volume, cotangent, weight, bias):
    nx, ny = lax.axis_size("gx"), lax.axis_size("gy")
    wf = band(jnp.transpose(weight, (2, 4, 0, 1, 3)).reshape(3, C, 288))
    wd = band(jnp.transpose(weight[::-1, ::-1, ::-1], (2, 3, 0, 1, 4)).reshape(3, C, 288))
    barrier = lax.optimization_barrier
    vx, xeven, xodd = pack(volume, True)
    xodd, bias, cotangent = barrier((xodd, bias, cotangent))
    offset = jnp.broadcast_to(bias[:, None], (C, T))
    xodd = swap_x(xodd, 1)
    xeven = swap_x(xeven, 0)
    (gx,) = pack(cotangent, False)
    xodd, offset, gx = barrier((xodd, offset, gx))
    yodd, xlow, xhigh = odd_edge(vx, xeven, xodd)
    yodd, xlow, xhigh = barrier((yodd, xlow, xhigh))
    yeven = even_edge(vx, xlow, xhigh)
    yodd = swap_y(yodd, 1)
    yeven, xlow, xhigh = barrier((yeven, xlow, xhigh))
    yeven = swap_y(yeven, 0)
    gmid, total, prod = middle(vx, gx, xlow, xhigh, wf, offset)
    gedge, keep, give = outer(vx, gx, xlow, xhigh, yeven, yodd, wf, offset, total, prod)

    state = dict(gmid=gmid, gedge=gedge)

    def along_x():
        xeven, xodd = gradient_faces(state["gmid"], state["gedge"])
        state["xodd"] = swap_x(xodd, 1)
        state["xeven"] = swap_x(xeven, 0)

    def along_y_odd():
        yodd, state["xlow"], state["xhigh"] = odd_edge(state["gedge"], state.pop("xeven"), state.pop("xodd"))
        state["yodd"] = swap_y(yodd, 1)

    def along_y_even():
        state["yeven"] = swap_y(even_edge(state["gedge"], state["xlow"], state["xhigh"]), 0)

    def data():
        names = ("gmid", "gedge", "xlow", "xhigh", "yeven", "yodd")
        state["data"] = back(*(state[name] for name in names), wd)

    def step(sent, move, work, then):
        if work:
            sent, given = barrier((sent, dict(state)))
            state.update(given)
        got = move(sent)
        if work:
            work()
        if then:
            got, state[then] = barrier((got, state[then]))
        return got

    got = step(give, lambda sent: swap_x(sent, 0), along_x, None)
    wire = add(keep, got, BF16)
    steps = [(1 << b, 0) for b in range(1, nx.bit_length() - 1)] + [(0, 1 << b) for b in range(ny.bit_length() - 1)]
    works = [(None, None), (along_y_odd, None), (along_y_even, None), (data, "data")]
    for n, (dx, dy) in enumerate(steps):
        work, then = works.pop(0) if works else (None, None)
        got = step(wire, lambda sent: permute(sent, lambda x, y: (x ^ dx ^ 1, y ^ dy)), work, then)
        wire = add(wire, got, F32 if n == len(steps) - 1 else BF16)
    for work, _ in works:
        if work:
            work()
    scale = 1.0 / math.sqrt(8 * nx * 16 * ny * Z)
    filters, biases = finish(wire, swap_x(wire, 0), scale)
    return state["data"], filters.reshape(3, 3, 3, C, C), biases.reshape(C)


def solution(mesh):
    in_specs = (P("gx", "gy", None), P("gx", "gy", None), P(), P())
    out_specs = (P("gx", "gy", None), P(), P())
    return jax.shard_map(shards, mesh=mesh, in_specs=in_specs, out_specs=out_specs, check_vma=False)
```

```python
import math

import jax
import jax.numpy as jnp
from jax import lax
from jax.experimental import pallas as pl
from jax.experimental.pallas import tpu as pltpu
from jax.sharding import PartitionSpec as P

C = 32
Z = 64
T = 128
ROW = 8 * T
HALF = 112
F32 = jnp.float32
BF16 = jnp.bfloat16
VMEM_LIMIT = 48 * 1024 * 1024
VMEM = pl.BlockSpec(memory_space=pltpu.VMEM)
HBM = pl.BlockSpec(memory_space=pltpu.HBM)


def call(body, out_shape, scratch_shapes, flops, *args, in_specs=None, out_specs=None, aliases=None):
    traffic = sum(math.prod(a.shape) * a.dtype.itemsize for a in (*args, *jax.tree.leaves(out_shape)))
    return pl.pallas_call(
        body,
        out_shape=out_shape,
        in_specs=in_specs or [VMEM] * len(args),
        out_specs=out_specs or jax.tree.map(lambda _: VMEM, out_shape),
        scratch_shapes=scratch_shapes,
        input_output_aliases=aliases or {},
        compiler_params=pltpu.CompilerParams(vmem_limit_bytes=VMEM_LIMIT),
        cost_estimate=pl.CostEstimate(flops=flops, bytes_accessed=traffic, transcendentals=0),
    )(*args)


def like(dtype, *shape):
    return jax.ShapeDtypeStruct(shape, dtype)


def lane(shape):
    return lax.broadcasted_iota(jnp.int32, shape, len(shape) - 1)


def swap_halves(a):
    return pltpu.roll(a, T // 2, a.ndim - 1)


def halves(low, high):
    return jnp.where(lane(low.shape) < T // 2, low, high)


def exchange_halves(a, b):
    mixed = swap_halves(halves(b, a))
    return halves(a, mixed), halves(mixed, b)


def from_below(a):
    return jnp.where(lane(a.shape) % Z == 0, 0.0, pltpu.roll(a, 1, a.ndim - 1))


def from_above(a):
    return jnp.where(lane(a.shape) % Z == Z - 1, 0.0, pltpu.roll(a, T - 1, a.ndim - 1))


def tile(t):
    return slice(t * T, t * T + T)


def to_channels(rows, stage):
    rows = rows.astype(F32)
    for pair in range(C // 2):
        even, odd = exchange_halves(rows[:8, tile(pair)], rows[8:, tile(pair)])
        stage[pl.ds(pair * 16, 8), :] = even
        stage[pl.ds(pair * 16 + 8, 8), :] = odd
    return [stage[pl.ds(t, C, stride=8), :] for t in range(8)]


def is_even(axis):
    return lax.axis_index(axis) % 2 == 0


def clear_ends(axis, low, high):
    @pl.when(lax.axis_index(axis) == 0)
    def _():
        low[...] = jnp.zeros_like(low)

    @pl.when(lax.axis_index(axis) == lax.axis_size(axis) - 1)
    def _():
        high[...] = jnp.zeros_like(high)


def my_half():
    total = 0
    for axis in ("gx", "gy"):
        for b in range(lax.axis_size(axis).bit_length() - 1):
            total = total + lax.axis_index(axis) // (1 << b)
    return total % 2


def faces(field, even, odd):
    for when, low, high in ((is_even("gx"), odd, even), (jnp.logical_not(is_even("gx")), even, odd)):

        @pl.when(when)
        def _(low=low, high=high):
            for t in range(8):
                low[:, tile(t)] = field(0, t)
                high[:, tile(t)] = field(7, t)


def pack_body(array, out, stage):
    for x in range(array.shape[0]):
        for t, part in enumerate(to_channels(array[x], stage.at[x])):
            out[x, :, tile(t)] = part.astype(BF16)


def pack(array):
    return call(pack_body, like(BF16, 8, C, ROW), [pltpu.VMEM((8, 8 * C, T), F32)], 1_000_000, array)


def whole(ref):
    return lambda x, t: ref[x, :, tile(t)]


def split(mid, edge):
    return lambda x, t: edge[x, :, tile(t // 7)] if t in (0, 7) else mid[x, :, tile(t - 1)]


def with_faces(field, xlow, xhigh):
    return lambda x, t: xlow[:, tile(t)] if x < 0 else xhigh[:, tile(t)] if x > 7 else field(x, t)


def faces_body(mid, edge, even, odd):
    faces(split(mid, edge), even, odd)


def gradient_faces(mid, edge):
    face = like(BF16, C, ROW)
    return call(faces_body, (face, face), [], 100_000, mid, edge)


def sort(axis, even, odd, low, high):
    @pl.when(is_even(axis))
    def _():
        low[...] = odd[...]
        high[...] = even[...]

    @pl.when(jnp.logical_not(is_even(axis)))
    def _():
        low[...] = even[...]
        high[...] = odd[...]

    clear_ends(axis, low, high)


def edge_message(field, low_when, out):
    @pl.when(low_when)
    def _():
        for row in range(5):
            out[row] = halves(field(row + 4, 0).astype(F32), swap_halves(field(row - 1, 0).astype(F32))).astype(BF16)

    @pl.when(jnp.logical_not(low_when))
    def _():
        for row in range(5):
            out[row] = halves(swap_halves(field(row - 1, 7).astype(F32)), field(row + 4, 7).astype(F32)).astype(BF16)


def ends(ref):
    last = ref.shape[-1] // T - 1
    return lambda x, t: ref[x, :, tile(last if t else 0)]


def odd_edge_body(field, xeven, xodd, out, xlow, xhigh, *scratch):
    if scratch:
        stage, packed = scratch
        pack_body(xeven, packed.at[pl.ds(0, 1)], stage.at[pl.ds(0, 1)])
        pack_body(xodd, packed.at[pl.ds(1, 1)], stage.at[pl.ds(1, 1)])
        xeven, xodd = packed.at[0], packed.at[1]
    sort("gx", xeven, xodd, xlow, xhigh)
    edge_message(with_faces(ends(field), xlow, xhigh), is_even("gy"), out)


def odd_edge(field, xeven, xodd):
    face = like(BF16, C, ROW)
    scratch = [pltpu.VMEM((2, 8 * C, T), F32), pltpu.VMEM((2, C, ROW), BF16)] if xeven.ndim == 3 else []
    return call(odd_edge_body, (like(BF16, 5, C, T), face, face), scratch, 100_000, field, xeven, xodd)


def even_edge_body(field, xlow, xhigh, out):
    edge_message(with_faces(ends(field), xlow, xhigh), jnp.logical_not(is_even("gy")), out)


def even_edge(field, xlow, xhigh):
    return call(even_edge_body, like(BF16, 5, C, T), [], 100_000, field, xlow, xhigh)


def sort_edges(even, odd, near):
    for when, low, high in ((is_even("gy"), odd, even), (jnp.logical_not(is_even("gy")), even, odd)):

        @pl.when(when)
        def _(low=low, high=high):
            for row in range(5):
                a, b = low[row].astype(F32), high[row].astype(F32)
                near[row] = halves(a, b)
                near[row + 5] = halves(swap_halves(a), swap_halves(b))

    place = lax.axis_index("gy")
    for when, empty in ((place == 0, 0), (place == lax.axis_size("gy") - 1, 1)):

        @pl.when(when)
        def _(empty=empty):
            for row in range(10):
                near[row] = halves(near[row], jnp.zeros((C, T), F32)) if empty else halves(jnp.zeros((C, T), F32), near[row])


def activation(pre, grad_out):
    sig = 1.0 / (1.0 + jnp.exp(-pre))
    return grad_out.astype(F32) * sig * (1.0 + pre * (1.0 - sig))


def stack(out, i, tiles, field, near=None):
    for n, t in enumerate(tiles):
        for dy in range(3):
            if t + dy == 0:
                part = halves(near, swap_halves(field(7).astype(F32))).astype(BF16)
            elif t + dy == 9:
                part = halves(swap_halves(field(0).astype(F32)), near).astype(BF16)
            else:
                part = field(t + dy - 1)
            out[(3 * i + dy) * C : (3 * i + dy + 1) * C, tile(n)] = part


def step_z(part):
    return from_below(part[:64]) + part[64:128] + from_above(part[128:])


def gradient(tiles, gx, wf, bias, cols, gps, out):
    offset = jnp.concatenate([bias[...]] * 2, axis=0)
    total = jnp.zeros((64, T), F32)
    for q in range(4):
        both = jnp.dot(wf[...], cols[q * 192 : q * 192 + 384, :], preferred_element_type=F32)
        for n, t in enumerate(tiles):
            grad_out = gx[2 * q : 2 * q + 2, :, tile(t)].reshape(64, T)
            grad = activation(step_z(both[:, tile(n)]) + offset, grad_out).astype(BF16)
            out[2 * q : 2 * q + 2, :, tile(n)] = grad.reshape(2, C, T)
            grad = grad.astype(F32)
            total = total + grad
            gps[q * 192 : q * 192 + 64, tile(n)] = from_above(grad).astype(BF16)
            gps[q * 192 + 64 : q * 192 + 128, tile(n)] = grad.astype(BF16)
            gps[q * 192 + 128 : q * 192 + 192, tile(n)] = from_below(grad).astype(BF16)
    prod = jnp.zeros((384, 192), F32)
    for q in range(4):
        prod = prod + lax.dot_general(
            cols[q * 192 : q * 192 + 384, :],
            gps[q * 192 : q * 192 + 192, :],
            (((1,), (1,)), ((), ())),
            preferred_element_type=F32,
        )
    return total, prod


MID = range(1, 7)
EDGE = (0, 7)


def middle_body(vx, gx, xlow, xhigh, wf, bias, gmid, total, prod, cols, gps):
    field = with_faces(whole(vx), xlow, xhigh)
    for x in range(-1, 9):
        stack(cols, x + 1, MID, lambda t, x=x: field(x, t))
    total[...], prod[...] = gradient(MID, gx, wf, bias, cols, gps, gmid)


def middle(vx, gx, xlow, xhigh, wf, bias):
    out = (like(BF16, 8, C, 6 * T), like(F32, 64, T), like(F32, 384, 192))
    scratch = [pltpu.VMEM((960, 6 * T), BF16), pltpu.VMEM((768, 6 * T), BF16)]
    return call(middle_body, out, scratch, 1_800_000_000, vx, gx, xlow, xhigh, wf, bias)


def outer_body(vx, gx, xlow, xhigh, yodd, yeven, wf, bias, total, prod, gedge, keep, give, near, cols, gps, wire):
    sort_edges(yeven, yodd, near)
    field = with_faces(whole(vx), xlow, xhigh)
    for x in range(-1, 9):
        stack(cols, x + 1, EDGE, lambda t, x=x: field(x, t), near[x + 1])
    more_total, more = gradient(EDGE, gx, wf, bias, cols, gps, gedge)
    total, prod = total[...] + more_total, prod[...] + more
    group = lane((8, T)) // C
    rows = []
    for row in range(0, 288, 8):
        a, b = prod[row : row + 8], prod[row + 96 : row + 104]
        a = jnp.concatenate([a[:, T:], jnp.zeros((8, 64), F32)], axis=1), a[:, :T]
        b = jnp.concatenate([b[:, T:], jnp.zeros((8, 64), F32)], axis=1), b[:, :T]
        near = a[1] + pltpu.roll(b[1], T - C, 1)
        far = a[0] + pltpu.roll(b[0], T - C, 1)
        rows.append((near, pltpu.roll(near, T - C, 1), pltpu.roll(far, 2 * C, 1), far))
    for i in range(27):
        near, moved, far, _ = rows[i]
        dz, at = divmod(i, 9)
        near2, moved2, far2, plain2 = rows[27 + at]
        last = pltpu.roll((near2, near2, plain2)[dz], (3 * C, C, 3 * C)[dz], 1)
        out = jnp.where(group == 0, near, jnp.where(group == 1, moved, jnp.where(group == 2, far, last)))
        wire[8 * i : 8 * i + 8] = out
    total = jnp.concatenate([total[:C] + total[C:], jnp.zeros((T - C, T), F32)], axis=0)
    total = jnp.sum(total.T, axis=0, keepdims=True)
    wire[216:] = jnp.broadcast_to(total, (8, T))
    for half in range(2):

        @pl.when(my_half() == half)
        def _(half=half):
            keep[...] = wire[half * HALF : half * HALF + HALF]
            give[...] = wire[HALF - half * HALF : 2 * HALF - half * HALF]


def outer(vx, gx, xlow, xhigh, yodd, yeven, wf, bias, total, prod):
    out = (like(BF16, 8, C, 2 * T), like(F32, HALF, T), like(F32, HALF, T))
    scratch = [
        pltpu.VMEM((10, C, T), F32),
        pltpu.VMEM((960, 2 * T), BF16),
        pltpu.VMEM((768, 2 * T), BF16),
        pltpu.VMEM((2 * HALF, T), F32),
    ]
    args = (vx, gx, xlow, xhigh, yodd, yeven, wf, bias, total, prod)
    return call(outer_body, out, scratch, 700_000_000, *args)


def products(tiles, wd, cols, stage):
    for q in range(4):
        both = jnp.dot(wd[...], cols[q * 192 : q * 192 + 384, :], preferred_element_type=F32)
        for n, t in enumerate(tiles):
            out = step_z(both[:, tile(n)])
            for x in range(2):
                stage[2 * q + x, pl.ds(t, C, stride=8), :] = out[x * C : x * C + C]


def back_middle_body(*refs):
    gmid, gedge, xlow, xhigh, wd, stage, cols = refs
    field = with_faces(split(gmid, gedge), xlow, xhigh)
    for x in range(-1, 9):
        stack(cols, x + 1, MID, lambda t, x=x: field(x, t))
    products(MID, wd, cols, stage)


def back_middle(gmid, gedge, xlow, xhigh, wd):
    out = like(F32, 8, 8 * C, T)
    return call(back_middle_body, out, [pltpu.VMEM((960, 6 * T), BF16)], 800_000_000, gmid, gedge, xlow, xhigh, wd)


def back_outer_body(*refs):
    gmid, gedge, xlow, xhigh, yodd, yeven, wd, mid, data, near, cols, stage, block, sems = refs
    sort_edges(yeven, yodd, near)
    field = with_faces(split(gmid, gedge), xlow, xhigh)
    for x in range(-1, 9):
        stack(cols, x + 1, EDGE, lambda t, x=x: field(x, t), near[x + 1])
    products(EDGE, wd, cols, stage)
    row = lax.broadcasted_iota(jnp.int32, (8, T), 0)
    inside = jnp.logical_and(row > 0, row < 7)
    copies = []
    for x in range(8):
        for pair in range(C // 2):
            at = [pl.ds(pair * 16 + 8 * k, 8) for k in range(2)]
            even, odd = (jnp.where(inside, mid[x, rows, :], stage[x, rows, :]) for rows in at)
            block[x, :, tile(pair)] = jnp.concatenate(exchange_halves(even, odd), axis=0).astype(BF16)
        if x % 2:
            copies.append(pltpu.make_async_copy(block.at[pl.ds(x - 1, 2)], data.at[pl.ds(x - 1, 2)], sems.at[x // 2]))
            copies[-1].start()
    for copy in copies:
        copy.wait()


def back_outer(gmid, gedge, xlow, xhigh, yodd, yeven, wd, mid):
    scratch = [
        pltpu.VMEM((10, C, T), F32),
        pltpu.VMEM((960, 2 * T), BF16),
        pltpu.VMEM((8, 8 * C, T), F32),
        pltpu.VMEM((8, 16, C * Z), BF16),
        pltpu.SemaphoreType.DMA((4,)),
    ]
    out = like(BF16, 8, 16, C * Z)
    args = (gmid, gedge, xlow, xhigh, yodd, yeven, wd, mid)
    return call(back_outer_body, out, scratch, 300_000_000, *args, out_specs=HBM)


def add_body(a, b, out):
    out[...] = (a[...].astype(F32) + b[...].astype(F32)).astype(out.dtype)


def add(a, b, dtype):
    return call(add_body, like(dtype, *a.shape), [], 100_000, a, b)


def finish_body(scale, own, other, filters, biases):
    for half, halves_of in enumerate(((own, other), (other, own))):

        @pl.when(my_half() == half)
        def _(halves_of=halves_of):
            for row in range(0, 288, 8):
                for dz in range(3):
                    at, group = (row, dz) if row < 216 else (row - 216 + 72 * dz, 3)
                    part = halves_of[at // HALF][at % HALF : at % HALF + 8]
                    moved = part if group == 0 else pltpu.roll(part, T - group * C, 1)
                    block, inside = divmod(row, C)
                    filters[block * 3 + dz, inside : inside + 8, :] = moved[:, :C] * scale
            biases[...] = halves_of[1][216 - HALF : 217 - HALF, :C] * scale


def finish(own, other, scale):
    out = (like(F32, 27, C, C), like(F32, 1, C))
    return call(lambda *refs: finish_body(scale, *refs), out, [], 100_000, own, other)


def permute(array, target):
    nx, ny = lax.axis_size("gx"), lax.axis_size("gy")
    pairs = []
    for x in range(nx):
        for y in range(ny):
            to = target(x, y)
            pairs.append((x * ny + y, to[0] * ny + to[1]))
    return lax.ppermute(array, ("gx", "gy"), pairs)


def swap_x(array, odd):
    nx = lax.axis_size("gx")
    return permute(array, lambda x, y: ((((x + odd) ^ 1) - odd) % nx, y))


def swap_y(array, odd):
    ny = lax.axis_size("gy")

    def target(x, y):
        to = ((y + odd) ^ 1) - odd
        return (x, to) if 0 <= to < ny else (x ^ 1, y)

    return permute(array, target)


def band(strip):
    pad = [jnp.pad(strip, ((0, 0), (0, 0), (96 * x, 96 - 96 * x))) for x in range(2)]
    return jnp.stack(pad, axis=1).reshape(192, 384)


def shards(volume, cotangent, weight, bias):
    nx, ny = lax.axis_size("gx"), lax.axis_size("gy")
    wf = band(jnp.transpose(weight, (2, 4, 0, 1, 3)).reshape(3, C, 288))
    wd = band(jnp.transpose(weight[::-1, ::-1, ::-1], (2, 3, 0, 1, 4)).reshape(3, C, 288))
    barrier = lax.optimization_barrier
    up = 7 * (1 - lax.axis_index("gx") % 2)
    xeven = lax.dynamic_slice_in_dim(volume, up, 1, 0)
    xodd = lax.dynamic_slice_in_dim(volume, 7 - up, 1, 0)
    xodd, xeven, bias, cotangent = barrier((xodd, xeven, bias, cotangent))
    vx = pack(volume)
    offset = jnp.broadcast_to(bias[:, None], (C, T))
    xodd = swap_x(xodd, 1)
    xeven = swap_x(xeven, 0)
    gx = pack(cotangent)
    xodd, offset, gx = barrier((xodd, offset, gx))
    yodd, xlow, xhigh = odd_edge(vx, xeven, xodd)
    yodd, xlow, xhigh = barrier((yodd, xlow, xhigh))
    yeven = even_edge(vx, xlow, xhigh)
    yeven, xlow, xhigh = barrier((yeven, xlow, xhigh))
    yeven = swap_y(yeven, 0)
    yodd = swap_y(yodd, 1)
    gmid, total, prod = middle(vx, gx, xlow, xhigh, wf, offset)
    yodd, total = barrier((yodd, total))
    gedge, keep, give = outer(vx, gx, xlow, xhigh, yodd, yeven, wf, offset, total, prod)

    state = dict(gmid=gmid, gedge=gedge)

    def along_x():
        xeven, xodd = gradient_faces(state["gmid"], state["gedge"])
        state["xodd"] = swap_x(xodd, 1)
        state["xeven"] = swap_x(xeven, 0)

    def along_y():
        yodd, state["xlow"], state["xhigh"] = odd_edge(state["gedge"], state["xeven"], state["xodd"])
        state["yeven"] = swap_y(even_edge(state["gedge"], state["xlow"], state["xhigh"]), 0)
        state["yodd"] = swap_y(yodd, 1)

    def data():
        args = state["gmid"], state["gedge"], state["xlow"], state["xhigh"]
        mid, yodd = barrier((back_middle(*args, wd), state["yodd"]))
        state["data"] = back_outer(*args, yodd, state["yeven"], wd, mid)

    works = [
        (None, (), None),
        (along_x, ("gmid",), None),
        (None, (), None),
        (along_y, ("gedge", "xeven", "xodd"), None),
        (data, ("gmid",), "data"),
    ]

    def step(sent, target):
        work, tied, then = works.pop(0) if works else (None, None, None)
        if work:
            sent, given = barrier((sent, {name: state[name] for name in tied}))
            state.update(given)
        got = permute(sent, target)
        if work:
            work()
        if then:
            got, state[then] = barrier((got, state[then]))
        return sent, got

    _, got = step(give, lambda x, y: (x ^ 1, y))
    wire = add(keep, got, BF16)
    steps = [(1 << b, 0) for b in range(1, nx.bit_length() - 1)] + [(0, 1 << b) for b in range(ny.bit_length() - 1)]
    for n, (dx, dy) in enumerate(steps):
        sent, got = step(wire, lambda x, y: (x ^ dx ^ 1, y ^ dy))
        wire = add(sent, got, F32 if n == len(steps) - 1 else BF16)
    for work, tied, _ in works:
        if work:
            work()
    scale = 1.0 / math.sqrt(8 * nx * 16 * ny * Z)
    filters, biases = finish(wire, swap_x(wire, 0), scale)
    return state["data"], filters.reshape(3, 3, 3, C, C), biases.reshape(C)


def solution(mesh):
    in_specs = (P("gx", "gy", None), P("gx", "gy", None), P(), P())
    out_specs = (P("gx", "gy", None), P(), P())
    return jax.shard_map(shards, mesh=mesh, in_specs=in_specs, out_specs=out_specs, check_vma=False)
```

```python
import math

import jax
import jax.numpy as jnp
from jax import lax
from jax.experimental import pallas as pl
from jax.experimental.pallas import tpu as pltpu
from jax.sharding import PartitionSpec as P

C = 32
Z = 64
T = 128
ROW = 8 * T
HALF = 112
F32 = jnp.float32
BF16 = jnp.bfloat16
VMEM_LIMIT = 48 * 1024 * 1024
VMEM = pl.BlockSpec(memory_space=pltpu.VMEM)
HBM = pl.BlockSpec(memory_space=pltpu.HBM)


def call(body, out_shape, scratch_shapes, flops, *args, in_specs=None, out_specs=None, aliases=None):
    traffic = sum(math.prod(a.shape) * a.dtype.itemsize for a in (*args, *jax.tree.leaves(out_shape)))
    return pl.pallas_call(
        body,
        out_shape=jax.tree.map(lambda a: like(a.dtype, *a.shape), out_shape),
        in_specs=in_specs or [VMEM] * len(args),
        out_specs=out_specs or jax.tree.map(lambda _: VMEM, out_shape),
        scratch_shapes=scratch_shapes,
        input_output_aliases=aliases or {},
        compiler_params=pltpu.CompilerParams(vmem_limit_bytes=VMEM_LIMIT),
        cost_estimate=pl.CostEstimate(flops=flops, bytes_accessed=traffic, transcendentals=0),
    )(*args)


def like(dtype, *shape):
    return jax.ShapeDtypeStruct(shape, dtype)


def lane(shape):
    return lax.broadcasted_iota(jnp.int32, shape, len(shape) - 1)


def swap_halves(a):
    return pltpu.roll(a, T // 2, a.ndim - 1)


def halves(low, high):
    return jnp.where(lane(low.shape) < T // 2, low, high)


def exchange_halves(a, b):
    mixed = swap_halves(halves(b, a))
    return halves(a, mixed), halves(mixed, b)


def from_below(a):
    return jnp.where(lane(a.shape) % Z == 0, 0.0, pltpu.roll(a, 1, a.ndim - 1))


def from_above(a):
    return jnp.where(lane(a.shape) % Z == Z - 1, 0.0, pltpu.roll(a, T - 1, a.ndim - 1))


def tile(t):
    return slice(t * T, t * T + T)


def to_channels(rows, stage):
    rows = rows.astype(F32)
    for pair in range(C // 2):
        even, odd = exchange_halves(rows[:8, tile(pair)], rows[8:, tile(pair)])
        stage[pl.ds(pair * 16, 8), :] = even
        stage[pl.ds(pair * 16 + 8, 8), :] = odd
    return [stage[pl.ds(t, C, stride=8), :] for t in range(8)]


def is_even(axis):
    return lax.axis_index(axis) % 2 == 0


def clear_ends(axis, low, high):
    @pl.when(lax.axis_index(axis) == 0)
    def _():
        low[...] = jnp.zeros_like(low)

    @pl.when(lax.axis_index(axis) == lax.axis_size(axis) - 1)
    def _():
        high[...] = jnp.zeros_like(high)


def my_half():
    total = 0
    for axis in ("gx", "gy"):
        for b in range(lax.axis_size(axis).bit_length() - 1):
            total = total + lax.axis_index(axis) // (1 << b)
    return total % 2


def faces(field, even, odd):
    for when, low, high in ((is_even("gx"), odd, even), (jnp.logical_not(is_even("gx")), even, odd)):

        @pl.when(when)
        def _(low=low, high=high):
            for t in range(8):
                low[:, tile(t)] = field(0, t)
                high[:, tile(t)] = field(7, t)


def pack_body(array, out, stage):
    for x in range(array.shape[0]):
        for t, part in enumerate(to_channels(array[x], stage.at[x])):
            out[x, :, tile(t)] = part.astype(BF16)


def pack(array):
    return call(pack_body, like(BF16, 8, C, ROW), [pltpu.VMEM((8, 8 * C, T), F32)], 1_000_000, array)


def whole(ref):
    return lambda x, t: ref[x, :, tile(t)]


def split(mid, edge):
    return lambda x, t: edge[x, :, tile(t // 7)] if t in (0, 7) else mid[x, :, tile(t - 1)]


def with_faces(field, xlow, xhigh):
    return lambda x, t: xlow[:, tile(t)] if x < 0 else xhigh[:, tile(t)] if x > 7 else field(x, t)


def faces_body(mid, edge, even, odd):
    faces(split(mid, edge), even, odd)


def gradient_faces(mid, edge):
    face = like(BF16, C, ROW)
    return call(faces_body, (face, face), [], 100_000, mid, edge)


def sort(axis, even, odd, low, high):
    @pl.when(is_even(axis))
    def _():
        low[...] = odd[...]
        high[...] = even[...]

    @pl.when(jnp.logical_not(is_even(axis)))
    def _():
        low[...] = even[...]
        high[...] = odd[...]

    clear_ends(axis, low, high)


def edge_message(field, low_when, out):
    @pl.when(low_when)
    def _():
        for row in range(5):
            out[row] = halves(field(row + 4, 0).astype(F32), swap_halves(field(row - 1, 0).astype(F32))).astype(BF16)

    @pl.when(jnp.logical_not(low_when))
    def _():
        for row in range(5):
            out[row] = halves(swap_halves(field(row - 1, 7).astype(F32)), field(row + 4, 7).astype(F32)).astype(BF16)


def ends(ref):
    last = ref.shape[-1] // T - 1
    return lambda x, t: ref[x, :, tile(last if t else 0)]


def odd_edge_body(field, xeven, xodd, out, xlow, xhigh, *scratch):
    if scratch:
        stage, packed = scratch
        pack_body(xeven, packed.at[pl.ds(0, 1)], stage.at[pl.ds(0, 1)])
        pack_body(xodd, packed.at[pl.ds(1, 1)], stage.at[pl.ds(1, 1)])
        xeven, xodd = packed.at[0], packed.at[1]
    sort("gx", xeven, xodd, xlow, xhigh)
    edge_message(with_faces(ends(field), xlow, xhigh), is_even("gy"), out)


def odd_edge(field, xeven, xodd):
    face = like(BF16, C, ROW)
    scratch = [pltpu.VMEM((2, 8 * C, T), F32), pltpu.VMEM((2, C, ROW), BF16)] if xeven.ndim == 3 else []
    return call(odd_edge_body, (like(BF16, 5, C, T), face, face), scratch, 100_000, field, xeven, xodd)


def even_edge_body(field, xlow, xhigh, out):
    edge_message(with_faces(ends(field), xlow, xhigh), jnp.logical_not(is_even("gy")), out)


def even_edge(field, xlow, xhigh):
    return call(even_edge_body, like(BF16, 5, C, T), [], 100_000, field, xlow, xhigh)


def sort_edges(even, odd, near):
    for when, low, high in ((is_even("gy"), odd, even), (jnp.logical_not(is_even("gy")), even, odd)):

        @pl.when(when)
        def _(low=low, high=high):
            for row in range(5):
                a, b = low[row].astype(F32), high[row].astype(F32)
                near[row] = halves(a, b)
                near[row + 5] = halves(swap_halves(a), swap_halves(b))

    place = lax.axis_index("gy")
    for when, empty in ((place == 0, 0), (place == lax.axis_size("gy") - 1, 1)):

        @pl.when(when)
        def _(empty=empty):
            for row in range(10):
                near[row] = halves(near[row], jnp.zeros((C, T), F32)) if empty else halves(jnp.zeros((C, T), F32), near[row])


def activation(pre, grad_out):
    sig = 1.0 / (1.0 + jnp.exp(-pre))
    return grad_out.astype(F32) * sig * (1.0 + pre * (1.0 - sig))


def stack(out, i, tiles, field, near=None):
    for n, t in enumerate(tiles):
        for dy in range(3):
            if t + dy == 0:
                part = halves(near, swap_halves(field(7).astype(F32))).astype(BF16)
            elif t + dy == 9:
                part = halves(swap_halves(field(0).astype(F32)), near).astype(BF16)
            else:
                part = field(t + dy - 1)
            out[(3 * i + dy) * C : (3 * i + dy + 1) * C, tile(n)] = part


def step_z(part):
    return from_below(part[:64]) + part[64:128] + from_above(part[128:])


def gradient(tiles, gx, wf, bias, cols, gps, out):
    offset = jnp.concatenate([bias[...]] * 2, axis=0)
    total = jnp.zeros((64, T), F32)
    for q in range(4):
        both = jnp.dot(wf[...], cols[q * 192 : q * 192 + 384, :], preferred_element_type=F32)
        for n, t in enumerate(tiles):
            grad_out = gx[2 * q : 2 * q + 2, :, tile(t)].reshape(64, T)
            grad = activation(step_z(both[:, tile(n)]) + offset, grad_out).astype(BF16)
            out[2 * q : 2 * q + 2, :, tile(n)] = grad.reshape(2, C, T)
            grad = grad.astype(F32)
            total = total + grad
            gps[q * 192 : q * 192 + 64, tile(n)] = from_above(grad).astype(BF16)
            gps[q * 192 + 64 : q * 192 + 128, tile(n)] = grad.astype(BF16)
            gps[q * 192 + 128 : q * 192 + 192, tile(n)] = from_below(grad).astype(BF16)
    prod = jnp.zeros((384, 192), F32)
    for q in range(4):
        prod = prod + lax.dot_general(
            cols[q * 192 : q * 192 + 384, :],
            gps[q * 192 : q * 192 + 192, :],
            (((1,), (1,)), ((), ())),
            preferred_element_type=F32,
        )
    return total, prod


MID = range(1, 7)
EDGE = (0, 7)


def middle_body(vx, gx, xlow, xhigh, wf, bias, gmid, total, prod, cols, gps):
    field = with_faces(whole(vx), xlow, xhigh)
    for x in range(-1, 9):
        stack(cols, x + 1, MID, lambda t, x=x: field(x, t))
    total[...], prod[...] = gradient(MID, gx, wf, bias, cols, gps, gmid)


def middle(vx, gx, xlow, xhigh, wf, bias):
    out = (like(BF16, 8, C, 6 * T), like(F32, 64, T), like(F32, 384, 192))
    scratch = [pltpu.VMEM((960, 6 * T), BF16), pltpu.VMEM((768, 6 * T), BF16)]
    return call(middle_body, out, scratch, 1_000_000, vx, gx, xlow, xhigh, wf, bias)


def outer_body(vx, gx, xlow, xhigh, yodd, yeven, wf, bias, total, prod, gedge, keep, give, near, cols, gps, wire):
    sort_edges(yeven, yodd, near)
    field = with_faces(whole(vx), xlow, xhigh)
    for x in range(-1, 9):
        stack(cols, x + 1, EDGE, lambda t, x=x: field(x, t), near[x + 1])
    more_total, more = gradient(EDGE, gx, wf, bias, cols, gps, gedge)
    total, prod = total[...] + more_total, prod[...] + more
    group = lane((8, T)) // C
    rows = []
    for row in range(0, 288, 8):
        a, b = prod[row : row + 8], prod[row + 96 : row + 104]
        a = jnp.concatenate([a[:, T:], jnp.zeros((8, 64), F32)], axis=1), a[:, :T]
        b = jnp.concatenate([b[:, T:], jnp.zeros((8, 64), F32)], axis=1), b[:, :T]
        near = a[1] + pltpu.roll(b[1], T - C, 1)
        far = a[0] + pltpu.roll(b[0], T - C, 1)
        rows.append((near, pltpu.roll(near, T - C, 1), pltpu.roll(far, 2 * C, 1), far))
    for i in range(27):
        near, moved, far, _ = rows[i]
        dz, at = divmod(i, 9)
        near2, moved2, far2, plain2 = rows[27 + at]
        last = pltpu.roll((near2, near2, plain2)[dz], (3 * C, C, 3 * C)[dz], 1)
        out = jnp.where(group == 0, near, jnp.where(group == 1, moved, jnp.where(group == 2, far, last)))
        wire[8 * i : 8 * i + 8] = out
    total = jnp.concatenate([total[:C] + total[C:], jnp.zeros((T - C, T), F32)], axis=0)
    total = jnp.sum(total.T, axis=0, keepdims=True)
    wire[216:] = jnp.broadcast_to(total, (8, T))
    for half in range(2):

        @pl.when(my_half() == half)
        def _(half=half):
            keep[...] = wire[half * HALF : half * HALF + HALF]
            give[...] = wire[HALF - half * HALF : 2 * HALF - half * HALF]


def outer(vx, gx, xlow, xhigh, yodd, yeven, wf, bias, total, prod):
    out = (like(BF16, 8, C, 2 * T), like(F32, HALF, T), like(F32, HALF, T))
    scratch = [
        pltpu.VMEM((10, C, T), F32),
        pltpu.VMEM((960, 2 * T), BF16),
        pltpu.VMEM((768, 2 * T), BF16),
        pltpu.VMEM((2 * HALF, T), F32),
    ]
    args = (vx, gx, xlow, xhigh, yodd, yeven, wf, bias, total, prod)
    return call(outer_body, out, scratch, 700_000_000, *args)


def back_body(gmid, gedge, xlow, xhigh, yodd, yeven, wd, block, near, cols, stage):
    sort_edges(yeven, yodd, near)
    field = with_faces(split(gmid, gedge), xlow, xhigh)
    for x in range(-1, 9):
        stack(cols, x + 1, range(8), lambda t, x=x: field(x, t), near[x + 1])
    for q in range(4):
        both = jnp.dot(wd[...], cols[q * 192 : q * 192 + 384, :], preferred_element_type=F32)
        for t in range(8):
            out = step_z(both[:, tile(t)])
            for x in range(2):
                stage[2 * q + x, pl.ds(t, C, stride=8), :] = out[x * C : x * C + C]
        for x in (2 * q, 2 * q + 1):
            for pair in range(C // 2):
                even, odd = stage[x, pl.ds(pair * 16, 8), :], stage[x, pl.ds(pair * 16 + 8, 8), :]
                block[x, :, tile(pair)] = jnp.concatenate(exchange_halves(even, odd), axis=0).astype(BF16)


def back(gmid, gedge, xlow, xhigh, yodd, yeven, wd):
    scratch = [
        pltpu.VMEM((10, C, T), F32),
        pltpu.VMEM((960, ROW), BF16),
        pltpu.VMEM((8, 8 * C, T), F32),
    ]
    out = like(BF16, 8, 16, C * Z)
    return call(back_body, out, scratch, 1_000_000_000, gmid, gedge, xlow, xhigh, yodd, yeven, wd)


def flush_body(block, data, sem):
    copy = pltpu.make_async_copy(block, data, sem)
    copy.start()
    copy.wait()


def flush(block):
    return call(flush_body, block, [pltpu.SemaphoreType.DMA], 100_000, block, out_specs=HBM)


def add_body(a, b, out):
    out[...] = (a[...].astype(F32) + b[...].astype(F32)).astype(out.dtype)


def add(a, b, dtype, cost=100_000):
    return call(add_body, like(dtype, *a.shape), [], cost, a, b)


def finish_body(scale, own, other, filters, biases):
    for half, halves_of in enumerate(((own, other), (other, own))):

        @pl.when(my_half() == half)
        def _(halves_of=halves_of):
            for row in range(0, 288, 8):
                for dz in range(3):
                    at, group = (row, dz) if row < 216 else (row - 216 + 72 * dz, 3)
                    part = halves_of[at // HALF][at % HALF : at % HALF + 8]
                    moved = part if group == 0 else pltpu.roll(part, T - group * C, 1)
                    block, inside = divmod(row, C)
                    filters[block * 3 + dz, inside : inside + 8, :] = moved[:, :C] * scale
            biases[...] = halves_of[1][216 - HALF : 217 - HALF, :C] * scale


def finish(own, other, scale):
    out = (like(F32, 27, C, C), like(F32, 1, C))
    return call(lambda *refs: finish_body(scale, *refs), out, [], 100_000, own, other)


def permute(array, target):
    nx, ny = lax.axis_size("gx"), lax.axis_size("gy")
    pairs = []
    for x in range(nx):
        for y in range(ny):
            to = target(x, y)
            pairs.append((x * ny + y, to[0] * ny + to[1]))
    return lax.ppermute(array, ("gx", "gy"), pairs)


def swap_x(array, odd):
    nx = lax.axis_size("gx")
    return permute(array, lambda x, y: ((((x + odd) ^ 1) - odd) % nx, y))


def swap_y(array, odd):
    ny = lax.axis_size("gy")

    def target(x, y):
        to = ((y + odd) ^ 1) - odd
        return (x, to) if 0 <= to < ny else (x ^ 1, y)

    return permute(array, target)


def band(strip):
    pad = [jnp.pad(strip, ((0, 0), (0, 0), (96 * x, 96 - 96 * x))) for x in range(2)]
    return jnp.stack(pad, axis=1).reshape(192, 384)


def shards(volume, cotangent, weight, bias):
    nx, ny = lax.axis_size("gx"), lax.axis_size("gy")
    wf = band(jnp.transpose(weight, (2, 4, 0, 1, 3)).reshape(3, C, 288))
    wd = band(jnp.transpose(weight[::-1, ::-1, ::-1], (2, 3, 0, 1, 4)).reshape(3, C, 288))
    barrier = lax.optimization_barrier
    up = 7 * (1 - lax.axis_index("gx") % 2)
    xeven = lax.dynamic_slice_in_dim(volume, up, 1, 0)
    xodd = lax.dynamic_slice_in_dim(volume, 7 - up, 1, 0)
    xodd, xeven, bias = barrier((xodd, xeven, bias))
    vx = pack(volume)
    xodd = swap_x(xodd, 1)
    xeven = swap_x(xeven, 0)
    yodd, xlow, xhigh = odd_edge(vx, xeven, xodd)
    yodd, xlow, xhigh = barrier((yodd, xlow, xhigh))
    yeven = even_edge(vx, xlow, xhigh)
    yeven, xlow, xhigh, cotangent, bias = barrier((yeven, xlow, xhigh, cotangent, bias))
    offset = jnp.broadcast_to(bias[:, None], (C, T))
    yeven = swap_y(yeven, 0)
    yodd = swap_y(yodd, 1)
    gx = pack(cotangent)
    gmid, total, prod = middle(vx, gx, xlow, xhigh, wf, offset)
    yodd, total = barrier((yodd, total))
    gedge, keep, give = outer(vx, gx, xlow, xhigh, yodd, yeven, wf, offset, total, prod)

    state = dict(gmid=gmid, gedge=gedge)

    def along_x():
        xeven, xodd = gradient_faces(state["gmid"], state["gedge"])
        state["xodd"] = swap_x(xodd, 1)
        state["xeven"] = swap_x(xeven, 0)

    def along_y():
        yodd, state["xlow"], state["xhigh"] = odd_edge(state["gedge"], state["xeven"], state["xodd"])
        state["yeven"] = swap_y(even_edge(state["gedge"], state["xlow"], state["xhigh"]), 0)
        state["yodd"] = swap_y(yodd, 1)

    def data():
        names = ("gmid", "gedge", "xlow", "xhigh", "yodd", "yeven")
        state["block"] = back(*(state[name] for name in names), wd)

    def data_out():
        state["data"] = flush(state["block"])

    works = [
        (None, (), None),
        (along_x, ("gmid",), None),
        (None, (), None),
        (along_y, ("gedge", "xeven", "xodd"), None),
        (data, ("gmid",), "block"),
        (data_out, ("block",), "data"),
    ]

    def step(sent, target):
        work, tied, then = works.pop(0) if works else (None, None, None)
        if work:
            sent, given = barrier((sent, {name: state[name] for name in tied}))
            state.update(given)
        got = permute(sent, target)
        if work:
            work()
        if then:
            got, state[then] = barrier((got, state[then]))
        return sent, got

    _, got = step(give, lambda x, y: (x ^ 1, y))
    wire = add(keep, got, BF16)
    steps = [(1 << b, 0) for b in range(1, nx.bit_length() - 1)] + [(0, 1 << b) for b in range(ny.bit_length() - 1)]
    for n, (dx, dy) in enumerate(steps):
        sent, got = step(wire, lambda x, y: (x ^ dx ^ 1, y ^ dy))
        wire = add(sent, got, F32 if n == len(steps) - 1 else BF16, 10**9 if n == len(steps) - 2 else 100_000)
    scale = 1.0 / math.sqrt(8 * nx * 16 * ny * Z)
    sent, got = step(wire, lambda x, y: (x ^ 1, y))
    for work, tied, _ in works:
        if work:
            work()
    filters, biases = finish(sent, got, scale)
    return state["data"], filters.reshape(3, 3, 3, C, C), biases.reshape(C)


def solution(mesh):
    in_specs = (P("gx", "gy", None), P("gx", "gy", None), P(), P())
    out_specs = (P("gx", "gy", None), P(), P())
    return jax.shard_map(shards, mesh=mesh, in_specs=in_specs, out_specs=out_specs, check_vma=False)
```

```python
import math

import jax
import jax.numpy as jnp
from jax import lax
from jax.experimental import pallas as pl
from jax.experimental.pallas import tpu as pltpu
from jax.sharding import PartitionSpec as P

C = 32
Z = 64
T = 128
ROW = 8 * T
HALF = 112
F32 = jnp.float32
BF16 = jnp.bfloat16
VMEM_LIMIT = 48 * 1024 * 1024
VMEM = pl.BlockSpec(memory_space=pltpu.VMEM)
HBM = pl.BlockSpec(memory_space=pltpu.HBM)


def call(body, out_shape, scratch_shapes, flops, *args, in_specs=None, out_specs=None, aliases=None):
    traffic = sum(math.prod(a.shape) * a.dtype.itemsize for a in (*args, *jax.tree.leaves(out_shape)))
    return pl.pallas_call(
        body,
        out_shape=jax.tree.map(lambda a: like(a.dtype, *a.shape), out_shape),
        in_specs=in_specs or [VMEM] * len(args),
        out_specs=out_specs or jax.tree.map(lambda _: VMEM, out_shape),
        scratch_shapes=scratch_shapes,
        input_output_aliases=aliases or {},
        compiler_params=pltpu.CompilerParams(vmem_limit_bytes=VMEM_LIMIT),
        cost_estimate=pl.CostEstimate(flops=flops, bytes_accessed=traffic, transcendentals=0),
    )(*args)


def like(dtype, *shape):
    return jax.ShapeDtypeStruct(shape, dtype)


def lane(shape):
    return lax.broadcasted_iota(jnp.int32, shape, len(shape) - 1)


def swap_halves(a):
    return pltpu.roll(a, T // 2, a.ndim - 1)


def halves(low, high):
    return jnp.where(lane(low.shape) < T // 2, low, high)


def exchange_halves(a, b):
    mixed = swap_halves(halves(b, a))
    return halves(a, mixed), halves(mixed, b)


def from_below(a):
    return jnp.where(lane(a.shape) % Z == 0, 0.0, pltpu.roll(a, 1, a.ndim - 1))


def from_above(a):
    return jnp.where(lane(a.shape) % Z == Z - 1, 0.0, pltpu.roll(a, T - 1, a.ndim - 1))


def tile(t):
    return slice(t * T, t * T + T)


def to_channels(rows, stage):
    rows = rows.astype(F32)
    for pair in range(C // 2):
        even, odd = exchange_halves(rows[:8, tile(pair)], rows[8:, tile(pair)])
        stage[pl.ds(pair * 16, 8), :] = even
        stage[pl.ds(pair * 16 + 8, 8), :] = odd
    return [stage[pl.ds(t, C, stride=8), :] for t in range(8)]


def is_even(axis):
    return lax.axis_index(axis) % 2 == 0


def clear_ends(axis, low, high):
    @pl.when(lax.axis_index(axis) == 0)
    def _():
        low[...] = jnp.zeros_like(low)

    @pl.when(lax.axis_index(axis) == lax.axis_size(axis) - 1)
    def _():
        high[...] = jnp.zeros_like(high)


def my_half():
    total = 0
    for axis in ("gx", "gy"):
        for b in range(lax.axis_size(axis).bit_length() - 1):
            total = total + lax.axis_index(axis) // (1 << b)
    return total % 2


def faces(field, even, odd):
    for when, low, high in ((is_even("gx"), odd, even), (jnp.logical_not(is_even("gx")), even, odd)):

        @pl.when(when)
        def _(low=low, high=high):
            for t in range(8):
                low[:, tile(t)] = field(0, t)
                high[:, tile(t)] = field(7, t)


def pack_body(array, out, stage):
    for x in range(array.shape[0]):
        for t, part in enumerate(to_channels(array[x], stage.at[x])):
            out[x, :, tile(t)] = part.astype(BF16)


def pack(array, *after):
    def body(array, *refs):
        pack_body(array, *refs[-2:])

    return call(body, like(BF16, 8, C, ROW), [pltpu.VMEM((8, 8 * C, T), F32)], 1_000_000, array, *after)


def whole(ref):
    return lambda x, t: ref[x, :, tile(t)]


def split(mid, edge):
    return lambda x, t: edge[x, :, tile(t // 7)] if t in (0, 7) else mid[x, :, tile(t - 1)]


def with_faces(field, xlow, xhigh):
    return lambda x, t: xlow[:, tile(t)] if x < 0 else xhigh[:, tile(t)] if x > 7 else field(x, t)


def faces_body(mid, edge, even, odd):
    faces(split(mid, edge), even, odd)


def gradient_faces(mid, edge):
    face = like(BF16, C, ROW)
    return call(faces_body, (face, face), [], 100_000, mid, edge)


def sort(axis, even, odd, low, high):
    @pl.when(is_even(axis))
    def _():
        low[...] = odd[...]
        high[...] = even[...]

    @pl.when(jnp.logical_not(is_even(axis)))
    def _():
        low[...] = even[...]
        high[...] = odd[...]

    clear_ends(axis, low, high)


def edge_message(field, low_when, out):
    @pl.when(low_when)
    def _():
        for row in range(5):
            out[row] = halves(field(row + 4, 0).astype(F32), swap_halves(field(row - 1, 0).astype(F32))).astype(BF16)

    @pl.when(jnp.logical_not(low_when))
    def _():
        for row in range(5):
            out[row] = halves(swap_halves(field(row - 1, 7).astype(F32)), field(row + 4, 7).astype(F32)).astype(BF16)


def ends(ref):
    last = ref.shape[-1] // T - 1
    return lambda x, t: ref[x, :, tile(last if t else 0)]


def odd_edge_body(field, xeven, xodd, out, xlow, xhigh, *scratch):
    if scratch:
        stage, packed = scratch
        pack_body(xeven, packed.at[pl.ds(0, 1)], stage.at[pl.ds(0, 1)])
        pack_body(xodd, packed.at[pl.ds(1, 1)], stage.at[pl.ds(1, 1)])
        xeven, xodd = packed.at[0], packed.at[1]
    sort("gx", xeven, xodd, xlow, xhigh)
    edge_message(with_faces(ends(field), xlow, xhigh), is_even("gy"), out)


def odd_edge(field, xeven, xodd):
    face = like(BF16, C, ROW)
    scratch = [pltpu.VMEM((2, 8 * C, T), F32), pltpu.VMEM((2, C, ROW), BF16)] if xeven.ndim == 3 else []
    return call(odd_edge_body, (like(BF16, 5, C, T), face, face), scratch, 100_000, field, xeven, xodd)


def even_edge_body(field, xlow, xhigh, out):
    edge_message(with_faces(ends(field), xlow, xhigh), jnp.logical_not(is_even("gy")), out)


def even_edge(field, xlow, xhigh):
    return call(even_edge_body, like(BF16, 5, C, T), [], 100_000, field, xlow, xhigh)


def sort_edges(even, odd, near):
    for when, low, high in ((is_even("gy"), odd, even), (jnp.logical_not(is_even("gy")), even, odd)):

        @pl.when(when)
        def _(low=low, high=high):
            for row in range(5):
                a, b = low[row].astype(F32), high[row].astype(F32)
                near[row] = halves(a, b)
                near[row + 5] = halves(swap_halves(a), swap_halves(b))

    place = lax.axis_index("gy")
    for when, empty in ((place == 0, 0), (place == lax.axis_size("gy") - 1, 1)):

        @pl.when(when)
        def _(empty=empty):
            for row in range(10):
                near[row] = halves(near[row], jnp.zeros((C, T), F32)) if empty else halves(jnp.zeros((C, T), F32), near[row])


def activation(pre, grad_out):
    sig = 1.0 / (1.0 + jnp.exp(-pre))
    return grad_out.astype(F32) * sig * (1.0 + pre * (1.0 - sig))


def stack(out, i, tiles, field, near=None):
    for n, t in enumerate(tiles):
        for dy in range(3):
            if t + dy == 0:
                part = halves(near, swap_halves(field(7).astype(F32))).astype(BF16)
            elif t + dy == 9:
                part = halves(swap_halves(field(0).astype(F32)), near).astype(BF16)
            else:
                part = field(t + dy - 1)
            out[(3 * i + dy) * C : (3 * i + dy + 1) * C, tile(n)] = part


def step_z(part):
    return from_below(part[:64]) + part[64:128] + from_above(part[128:])


def gradient(tiles, gx, wf, bias, cols, gps, out):
    offset = jnp.concatenate([bias[...]] * 2, axis=0)
    total = jnp.zeros((64, T), F32)
    for q in range(4):
        both = jnp.dot(wf[...], cols[q * 192 : q * 192 + 384, :], preferred_element_type=F32)
        for n, t in enumerate(tiles):
            grad_out = gx[2 * q : 2 * q + 2, :, tile(t)].reshape(64, T)
            grad = activation(step_z(both[:, tile(n)]) + offset, grad_out).astype(BF16)
            out[2 * q : 2 * q + 2, :, tile(n)] = grad.reshape(2, C, T)
            grad = grad.astype(F32)
            total = total + grad
            gps[q * 192 : q * 192 + 64, tile(n)] = from_above(grad).astype(BF16)
            gps[q * 192 + 64 : q * 192 + 128, tile(n)] = grad.astype(BF16)
            gps[q * 192 + 128 : q * 192 + 192, tile(n)] = from_below(grad).astype(BF16)
    prod = jnp.zeros((384, 192), F32)
    for q in range(4):
        prod = prod + lax.dot_general(
            cols[q * 192 : q * 192 + 384, :],
            gps[q * 192 : q * 192 + 192, :],
            (((1,), (1,)), ((), ())),
            preferred_element_type=F32,
        )
    return total, prod


MID = range(1, 7)
EDGE = (0, 7)


def middle_body(vx, gx, xlow, xhigh, wf, bias, gmid, total, prod, cols, gps):
    field = with_faces(whole(vx), xlow, xhigh)
    for x in range(-1, 9):
        stack(cols, x + 1, MID, lambda t, x=x: field(x, t))
    total[...], prod[...] = gradient(MID, gx, wf, bias, cols, gps, gmid)


def middle(vx, gx, xlow, xhigh, wf, bias):
    out = (like(BF16, 8, C, 6 * T), like(F32, 64, T), like(F32, 384, 192))
    scratch = [pltpu.VMEM((960, 6 * T), BF16), pltpu.VMEM((768, 6 * T), BF16)]
    return call(middle_body, out, scratch, 1_000_000, vx, gx, xlow, xhigh, wf, bias)


def outer_body(vx, gx, xlow, xhigh, yodd, yeven, wf, bias, total, prod, gedge, keep, give, near, cols, gps, wire):
    sort_edges(yeven, yodd, near)
    field = with_faces(whole(vx), xlow, xhigh)
    for x in range(-1, 9):
        stack(cols, x + 1, EDGE, lambda t, x=x: field(x, t), near[x + 1])
    more_total, more = gradient(EDGE, gx, wf, bias, cols, gps, gedge)
    total, prod = total[...] + more_total, prod[...] + more
    group = lane((8, T)) // C
    rows = []
    for row in range(0, 288, 8):
        a, b = prod[row : row + 8], prod[row + 96 : row + 104]
        a = jnp.concatenate([a[:, T:], jnp.zeros((8, 64), F32)], axis=1), a[:, :T]
        b = jnp.concatenate([b[:, T:], jnp.zeros((8, 64), F32)], axis=1), b[:, :T]
        near = a[1] + pltpu.roll(b[1], T - C, 1)
        far = a[0] + pltpu.roll(b[0], T - C, 1)
        rows.append((near, pltpu.roll(near, T - C, 1), pltpu.roll(far, 2 * C, 1), far))
    for i in range(27):
        near, moved, far, _ = rows[i]
        dz, at = divmod(i, 9)
        near2, moved2, far2, plain2 = rows[27 + at]
        last = pltpu.roll((near2, near2, plain2)[dz], (3 * C, C, 3 * C)[dz], 1)
        out = jnp.where(group == 0, near, jnp.where(group == 1, moved, jnp.where(group == 2, far, last)))
        wire[8 * i : 8 * i + 8] = out
    total = jnp.concatenate([total[:C] + total[C:], jnp.zeros((T - C, T), F32)], axis=0)
    total = jnp.sum(total.T, axis=0, keepdims=True)
    wire[216:] = jnp.broadcast_to(total, (8, T))
    for half in range(2):

        @pl.when(my_half() == half)
        def _(half=half):
            keep[...] = wire[half * HALF : half * HALF + HALF]
            give[...] = wire[HALF - half * HALF : 2 * HALF - half * HALF]


def outer(vx, gx, xlow, xhigh, yodd, yeven, wf, bias, total, prod):
    out = (like(BF16, 8, C, 2 * T), like(F32, HALF, T), like(F32, HALF, T))
    scratch = [
        pltpu.VMEM((10, C, T), F32),
        pltpu.VMEM((960, 2 * T), BF16),
        pltpu.VMEM((768, 2 * T), BF16),
        pltpu.VMEM((2 * HALF, T), F32),
    ]
    args = (vx, gx, xlow, xhigh, yodd, yeven, wf, bias, total, prod)
    return call(outer_body, out, scratch, 700_000_000, *args)


def back_body(gmid, gedge, xlow, xhigh, yodd, yeven, wd, block, near, cols, stage):
    sort_edges(yeven, yodd, near)
    field = with_faces(split(gmid, gedge), xlow, xhigh)
    for x in range(-1, 9):
        stack(cols, x + 1, range(8), lambda t, x=x: field(x, t), near[x + 1])
    for q in range(4):
        both = jnp.dot(wd[...], cols[q * 192 : q * 192 + 384, :], preferred_element_type=F32)
        for t in range(8):
            out = step_z(both[:, tile(t)])
            for x in range(2):
                stage[2 * q + x, pl.ds(t, C, stride=8), :] = out[x * C : x * C + C]
        for x in (2 * q, 2 * q + 1):
            for pair in range(C // 2):
                even, odd = stage[x, pl.ds(pair * 16, 8), :], stage[x, pl.ds(pair * 16 + 8, 8), :]
                block[x, :, tile(pair)] = jnp.concatenate(exchange_halves(even, odd), axis=0).astype(BF16)


def back(gmid, gedge, xlow, xhigh, yodd, yeven, wd):
    scratch = [
        pltpu.VMEM((10, C, T), F32),
        pltpu.VMEM((960, ROW), BF16),
        pltpu.VMEM((8, 8 * C, T), F32),
    ]
    out = like(BF16, 8, 16, C * Z)
    return call(back_body, out, scratch, 1_000_000_000, gmid, gedge, xlow, xhigh, yodd, yeven, wd)


def flush_body(block, data, sem):
    copy = pltpu.make_async_copy(block, data, sem)
    copy.start()
    copy.wait()


def flush(block):
    return call(flush_body, block, [pltpu.SemaphoreType.DMA], 100_000, block, out_specs=HBM)


def add_body(a, b, out):
    out[...] = (a[...].astype(F32) + b[...].astype(F32)).astype(out.dtype)


def add(a, b, dtype, cost=100_000):
    return call(add_body, like(dtype, *a.shape), [], cost, a, b)


def finish_body(scale, own, other, filters, biases):
    for half, halves_of in enumerate(((own, other), (other, own))):

        @pl.when(my_half() == half)
        def _(halves_of=halves_of):
            for row in range(0, 288, 8):
                for dz in range(3):
                    at, group = (row, dz) if row < 216 else (row - 216 + 72 * dz, 3)
                    part = halves_of[at // HALF][at % HALF : at % HALF + 8]
                    moved = part if group == 0 else pltpu.roll(part, T - group * C, 1)
                    block, inside = divmod(row, C)
                    filters[block * 3 + dz, inside : inside + 8, :] = moved[:, :C] * scale
            biases[...] = halves_of[1][216 - HALF : 217 - HALF, :C] * scale


def finish(own, other, scale):
    out = (like(F32, 27, C, C), like(F32, 1, C))
    return call(lambda *refs: finish_body(scale, *refs), out, [], 100_000, own, other)


def permute(array, target):
    nx, ny = lax.axis_size("gx"), lax.axis_size("gy")
    pairs = []
    for x in range(nx):
        for y in range(ny):
            to = target(x, y)
            pairs.append((x * ny + y, to[0] * ny + to[1]))
    return lax.ppermute(array, ("gx", "gy"), pairs)


def swap_x(array, odd):
    nx = lax.axis_size("gx")
    return permute(array, lambda x, y: ((((x + odd) ^ 1) - odd) % nx, y))


def swap_y(array, odd):
    ny = lax.axis_size("gy")

    def target(x, y):
        to = ((y + odd) ^ 1) - odd
        return (x, to) if 0 <= to < ny else (x ^ 1, y)

    return permute(array, target)


def band(strip):
    pad = [jnp.pad(strip, ((0, 0), (0, 0), (96 * x, 96 - 96 * x))) for x in range(2)]
    return jnp.stack(pad, axis=1).reshape(192, 384)


def shards(volume, cotangent, weight, bias):
    nx, ny = lax.axis_size("gx"), lax.axis_size("gy")
    wf = band(jnp.transpose(weight, (2, 4, 0, 1, 3)).reshape(3, C, 288))
    wd = band(jnp.transpose(weight[::-1, ::-1, ::-1], (2, 3, 0, 1, 4)).reshape(3, C, 288))
    barrier = lax.optimization_barrier
    up = 7 * (1 - lax.axis_index("gx") % 2)
    xeven = lax.dynamic_slice_in_dim(volume, up, 1, 0)
    xodd = lax.dynamic_slice_in_dim(volume, 7 - up, 1, 0)
    xodd, xeven, bias = barrier((xodd, xeven, bias))
    offset = jnp.broadcast_to(bias[:, None], (C, T))
    vx = pack(volume, wf, offset)
    xodd = swap_x(xodd, 1)
    xeven = swap_x(xeven, 0)
    yodd, xlow, xhigh = odd_edge(vx, xeven, xodd)
    yodd, xlow, xhigh = barrier((yodd, xlow, xhigh))
    yeven = even_edge(vx, xlow, xhigh)
    yeven, xlow, xhigh, cotangent = barrier((yeven, xlow, xhigh, cotangent))
    yeven = swap_y(yeven, 0)
    yodd = swap_y(yodd, 1)
    gx = pack(cotangent)
    gmid, total, prod = middle(vx, gx, xlow, xhigh, wf, offset)
    yodd, total = barrier((yodd, total))
    gedge, keep, give = outer(vx, gx, xlow, xhigh, yodd, yeven, wf, offset, total, prod)

    state = dict(gmid=gmid, gedge=gedge)

    def along_x():
        xeven, xodd = gradient_faces(state["gmid"], state["gedge"])
        state["xodd"] = swap_x(xodd, 1)
        state["xeven"] = swap_x(xeven, 0)

    def along_y():
        yodd, state["xlow"], state["xhigh"] = odd_edge(state["gedge"], state["xeven"], state["xodd"])
        state["yeven"] = swap_y(even_edge(state["gedge"], state["xlow"], state["xhigh"]), 0)
        state["yodd"] = swap_y(yodd, 1)

    def data():
        names = ("gmid", "gedge", "xlow", "xhigh", "yodd", "yeven")
        state["block"] = back(*(state[name] for name in names), wd)

    def data_out():
        state["data"] = flush(state["block"])

    works = [
        (None, (), None),
        (along_x, ("gmid",), None),
        (None, (), None),
        (along_y, ("gedge", "xeven", "xodd"), None),
        (data, ("gmid",), "block"),
        (data_out, ("block",), "data"),
    ]

    def step(sent, target):
        work, tied, then = works.pop(0) if works else (None, None, None)
        if work:
            sent, given = barrier((sent, {name: state[name] for name in tied}))
            state.update(given)
        got = permute(sent, target)
        if work:
            work()
        if then:
            got, state[then] = barrier((got, state[then]))
        return sent, got

    _, got = step(give, lambda x, y: (x ^ 1, y))
    wire = add(keep, got, BF16)
    steps = [(1 << b, 0) for b in range(1, nx.bit_length() - 1)] + [(0, 1 << b) for b in range(ny.bit_length() - 1)]
    for n, (dx, dy) in enumerate(steps):
        sent, got = step(wire, lambda x, y: (x ^ dx ^ 1, y ^ dy))
        wire = add(sent, got, F32 if n == len(steps) - 1 else BF16, 10**9 if n == len(steps) - 2 else 100_000)
    scale = 1.0 / math.sqrt(8 * nx * 16 * ny * Z)
    sent, got = step(wire, lambda x, y: (x ^ 1, y))
    for work, tied, _ in works:
        if work:
            work()
    filters, biases = finish(sent, got, scale)
    return state["data"], filters.reshape(3, 3, 3, C, C), biases.reshape(C)


def solution(mesh):
    in_specs = (P("gx", "gy", None), P("gx", "gy", None), P(), P())
    out_specs = (P("gx", "gy", None), P(), P())
    return jax.shard_map(shards, mesh=mesh, in_specs=in_specs, out_specs=out_specs, check_vma=False)
```

```python
import math

import jax
import jax.numpy as jnp
from jax import lax
from jax.experimental import pallas as pl
from jax.experimental.pallas import tpu as pltpu
from jax.sharding import PartitionSpec as P

C = 32
Z = 64
T = 128
ROW = 8 * T
HALF = 128
FIRST = 104
BIAS = 112
F32 = jnp.float32
BF16 = jnp.bfloat16
VMEM_LIMIT = 48 * 1024 * 1024
VMEM = pl.BlockSpec(memory_space=pltpu.VMEM)
HBM = pl.BlockSpec(memory_space=pltpu.HBM)


def call(body, out_shape, scratch_shapes, flops, *args, in_specs=None, out_specs=None, aliases=None):
    traffic = sum(math.prod(a.shape) * a.dtype.itemsize for a in (*args, *jax.tree.leaves(out_shape)))
    return pl.pallas_call(
        body,
        out_shape=jax.tree.map(lambda a: like(a.dtype, *a.shape), out_shape),
        in_specs=in_specs or [VMEM] * len(args),
        out_specs=out_specs or jax.tree.map(lambda _: VMEM, out_shape),
        scratch_shapes=scratch_shapes,
        input_output_aliases=aliases or {},
        compiler_params=pltpu.CompilerParams(vmem_limit_bytes=VMEM_LIMIT),
        cost_estimate=pl.CostEstimate(flops=flops, bytes_accessed=traffic, transcendentals=0),
    )(*args)


def like(dtype, *shape):
    return jax.ShapeDtypeStruct(shape, dtype)


def lane(shape):
    return lax.broadcasted_iota(jnp.int32, shape, len(shape) - 1)


def swap_halves(a):
    return pltpu.roll(a, T // 2, a.ndim - 1)


def halves(low, high):
    return jnp.where(lane(low.shape) < T // 2, low, high)


def exchange_halves(a, b):
    mixed = swap_halves(halves(b, a))
    return halves(a, mixed), halves(mixed, b)


def from_below(a):
    return jnp.where(lane(a.shape) % Z == 0, 0.0, pltpu.roll(a, 1, a.ndim - 1))


def from_above(a):
    return jnp.where(lane(a.shape) % Z == Z - 1, 0.0, pltpu.roll(a, T - 1, a.ndim - 1))


def tile(t):
    return slice(t * T, t * T + T)


def to_channels(rows, stage):
    rows = rows.astype(F32)
    for pair in range(C // 2):
        even, odd = exchange_halves(rows[:8, tile(pair)], rows[8:, tile(pair)])
        stage[pl.ds(pair * 16, 8), :] = even
        stage[pl.ds(pair * 16 + 8, 8), :] = odd
    return [stage[pl.ds(t, C, stride=8), :] for t in range(8)]


def is_even(axis):
    return lax.axis_index(axis) % 2 == 0


def clear_ends(axis, low, high):
    @pl.when(lax.axis_index(axis) == 0)
    def _():
        low[...] = jnp.zeros_like(low)

    @pl.when(lax.axis_index(axis) == lax.axis_size(axis) - 1)
    def _():
        high[...] = jnp.zeros_like(high)


def my_half():
    total = 0
    for axis in ("gx", "gy"):
        for b in range(lax.axis_size(axis).bit_length() - 1):
            total = total + lax.axis_index(axis) // (1 << b)
    return total % 2


def faces(field, even, odd):
    for when, low, high in ((is_even("gx"), odd, even), (jnp.logical_not(is_even("gx")), even, odd)):

        @pl.when(when)
        def _(low=low, high=high):
            for t in range(8):
                low[:, tile(t)] = field(0, t)
                high[:, tile(t)] = field(7, t)


def pack_body(array, out, stage):
    for x in range(array.shape[0]):
        for t, part in enumerate(to_channels(array[x], stage.at[x])):
            out[x, :, tile(t)] = part.astype(BF16)


def pack(array, *after):
    def body(array, *refs):
        pack_body(array, *refs[-2:])

    return call(body, like(BF16, 8, C, ROW), [pltpu.VMEM((8, 8 * C, T), F32)], 1_000_000, array, *after)


def whole(ref):
    return lambda x, t: ref[x, :, tile(t)]


def split(mid, edge):
    return lambda x, t: edge[x, :, tile(t // 7)] if t in (0, 7) else mid[x, :, tile(t - 1)]


def with_faces(field, xlow, xhigh):
    return lambda x, t: xlow[:, tile(t)] if x < 0 else xhigh[:, tile(t)] if x > 7 else field(x, t)


def faces_body(mid, edge, even, odd):
    faces(split(mid, edge), even, odd)


def gradient_faces(mid, edge):
    face = like(BF16, C, ROW)
    return call(faces_body, (face, face), [], 100_000, mid, edge)


def sort(axis, even, odd, low, high):
    @pl.when(is_even(axis))
    def _():
        low[...] = odd[...]
        high[...] = even[...]

    @pl.when(jnp.logical_not(is_even(axis)))
    def _():
        low[...] = even[...]
        high[...] = odd[...]

    clear_ends(axis, low, high)


def edge_message(field, low_when, out):
    @pl.when(low_when)
    def _():
        for row in range(5):
            out[row] = halves(field(row + 4, 0).astype(F32), swap_halves(field(row - 1, 0).astype(F32))).astype(BF16)

    @pl.when(jnp.logical_not(low_when))
    def _():
        for row in range(5):
            out[row] = halves(swap_halves(field(row - 1, 7).astype(F32)), field(row + 4, 7).astype(F32)).astype(BF16)


def ends(ref):
    last = ref.shape[-1] // T - 1
    return lambda x, t: ref[x, :, tile(last if t else 0)]


def odd_edge_body(field, xeven, xodd, out, xlow, xhigh, *scratch):
    if scratch:
        stage, packed = scratch
        pack_body(xeven, packed.at[pl.ds(0, 1)], stage.at[pl.ds(0, 1)])
        pack_body(xodd, packed.at[pl.ds(1, 1)], stage.at[pl.ds(1, 1)])
        xeven, xodd = packed.at[0], packed.at[1]
    sort("gx", xeven, xodd, xlow, xhigh)
    edge_message(with_faces(ends(field), xlow, xhigh), is_even("gy"), out)


def odd_edge(field, xeven, xodd):
    face = like(BF16, C, ROW)
    scratch = [pltpu.VMEM((2, 8 * C, T), F32), pltpu.VMEM((2, C, ROW), BF16)] if xeven.ndim == 3 else []
    return call(odd_edge_body, (like(BF16, 5, C, T), face, face), scratch, 100_000, field, xeven, xodd)


def even_edge_body(field, xlow, xhigh, out):
    edge_message(with_faces(ends(field), xlow, xhigh), jnp.logical_not(is_even("gy")), out)


def even_edge(field, xlow, xhigh):
    return call(even_edge_body, like(BF16, 5, C, T), [], 100_000, field, xlow, xhigh)


def sort_edges(even, odd, near):
    for when, low, high in ((is_even("gy"), odd, even), (jnp.logical_not(is_even("gy")), even, odd)):

        @pl.when(when)
        def _(low=low, high=high):
            for row in range(5):
                a, b = low[row].astype(F32), high[row].astype(F32)
                near[row] = halves(a, b)
                near[row + 5] = halves(swap_halves(a), swap_halves(b))

    place = lax.axis_index("gy")
    for when, empty in ((place == 0, 0), (place == lax.axis_size("gy") - 1, 1)):

        @pl.when(when)
        def _(empty=empty):
            for row in range(10):
                near[row] = halves(near[row], jnp.zeros((C, T), F32)) if empty else halves(jnp.zeros((C, T), F32), near[row])


def activation(pre, grad_out):
    sig = 1.0 / (1.0 + jnp.exp(-pre))
    return grad_out.astype(F32) * sig * (1.0 + pre * (1.0 - sig))


def stack(out, i, tiles, field, near=None):
    for n, t in enumerate(tiles):
        for dy in range(3):
            if t + dy == 0:
                part = halves(near, swap_halves(field(7).astype(F32))).astype(BF16)
            elif t + dy == 9:
                part = halves(swap_halves(field(0).astype(F32)), near).astype(BF16)
            else:
                part = field(t + dy - 1)
            out[(3 * i + dy) * C : (3 * i + dy + 1) * C, tile(n)] = part


def step_z(part):
    return from_below(part[:64]) + part[64:128] + from_above(part[128:])


def gradient(tiles, gx, wf, bias, cols, gps, out):
    offset = jnp.concatenate([bias[...]] * 2, axis=0)
    total = jnp.zeros((64, T), F32)
    for q in range(4):
        both = jnp.dot(wf[...], cols[q * 192 : q * 192 + 384, :], preferred_element_type=F32)
        for n, t in enumerate(tiles):
            grad_out = gx[2 * q : 2 * q + 2, :, tile(t)].reshape(64, T)
            grad = activation(step_z(both[:, tile(n)]) + offset, grad_out).astype(BF16)
            out[2 * q : 2 * q + 2, :, tile(n)] = grad.reshape(2, C, T)
            grad = grad.astype(F32)
            total = total + grad
            gps[q * 192 : q * 192 + 64, tile(n)] = from_above(grad).astype(BF16)
            gps[q * 192 + 64 : q * 192 + 128, tile(n)] = grad.astype(BF16)
            gps[q * 192 + 128 : q * 192 + 192, tile(n)] = from_below(grad).astype(BF16)
    prod = jnp.zeros((384, 192), F32)
    for q in range(4):
        prod = prod + lax.dot_general(
            cols[q * 192 : q * 192 + 384, :],
            gps[q * 192 : q * 192 + 192, :],
            (((1,), (1,)), ((), ())),
            preferred_element_type=F32,
        )
    return total, prod


MID = range(1, 7)
EDGE = (0, 7)


def middle_body(vx, gx, xlow, xhigh, wf, bias, gmid, total, prod, cols, gps):
    field = with_faces(whole(vx), xlow, xhigh)
    for x in range(-1, 9):
        stack(cols, x + 1, MID, lambda t, x=x: field(x, t))
    total[...], prod[...] = gradient(MID, gx, wf, bias, cols, gps, gmid)


def middle(vx, gx, xlow, xhigh, wf, bias):
    out = (like(BF16, 8, C, 6 * T), like(F32, 64, T), like(F32, 384, 192))
    scratch = [pltpu.VMEM((960, 6 * T), BF16), pltpu.VMEM((768, 6 * T), BF16)]
    return call(middle_body, out, scratch, 1_000_000, vx, gx, xlow, xhigh, wf, bias)


def outer_body(vx, gx, xlow, xhigh, yodd, yeven, wf, bias, total, prod, gedge, keep, give, near, cols, gps, wire):
    sort_edges(yeven, yodd, near)
    field = with_faces(whole(vx), xlow, xhigh)
    for x in range(-1, 9):
        stack(cols, x + 1, EDGE, lambda t, x=x: field(x, t), near[x + 1])
    more_total, more = gradient(EDGE, gx, wf, bias, cols, gps, gedge)
    total, prod = total[...] + more_total, prod[...] + more
    group = lane((8, T)) // C
    rows = []
    for row in range(0, 288, 8):
        a, b = prod[row : row + 8], prod[row + 96 : row + 104]
        a = jnp.concatenate([a[:, T:], jnp.zeros((8, 64), F32)], axis=1), a[:, :T]
        b = jnp.concatenate([b[:, T:], jnp.zeros((8, 64), F32)], axis=1), b[:, :T]
        near = a[1] + pltpu.roll(b[1], T - C, 1)
        far = a[0] + pltpu.roll(b[0], T - C, 1)
        rows.append((near, pltpu.roll(near, T - C, 1), pltpu.roll(far, 2 * C, 1), far))
    for i in range(27):
        near, moved, far, _ = rows[i]
        dz, at = divmod(i, 9)
        near2, moved2, far2, plain2 = rows[27 + at]
        last = pltpu.roll((near2, near2, plain2)[dz], (3 * C, C, 3 * C)[dz], 1)
        out = jnp.where(group == 0, near, jnp.where(group == 1, moved, jnp.where(group == 2, far, last)))
        at = 8 * i if 8 * i < FIRST else 8 * i - FIRST + HALF
        wire[at : at + 8] = out
    total = jnp.concatenate([total[:C] + total[C:], jnp.zeros((T - C, T), F32)], axis=0)
    total = jnp.sum(total.T, axis=0, keepdims=True)
    total = jnp.where(lax.broadcasted_iota(jnp.int32, (16, T), 0) == 0, total, 0.0)
    wire[FIRST:BIAS] = jnp.zeros((8, T), F32)
    wire[BIAS:HALF] = total
    wire[HALF + BIAS :] = total
    for half in range(2):

        @pl.when(my_half() == half)
        def _(half=half):
            keep[...] = wire[half * HALF : half * HALF + HALF]
            give[...] = wire[HALF - half * HALF : 2 * HALF - half * HALF]


def outer(vx, gx, xlow, xhigh, yodd, yeven, wf, bias, total, prod):
    out = (like(BF16, 8, C, 2 * T), like(F32, HALF, T), like(F32, HALF, T))
    scratch = [
        pltpu.VMEM((10, C, T), F32),
        pltpu.VMEM((960, 2 * T), BF16),
        pltpu.VMEM((768, 2 * T), BF16),
        pltpu.VMEM((2 * HALF, T), F32),
    ]
    args = (vx, gx, xlow, xhigh, yodd, yeven, wf, bias, total, prod)
    return call(outer_body, out, scratch, 700_000_000, *args)


def back_body(gmid, gedge, xlow, xhigh, yodd, yeven, wd, block, near, cols, stage):
    sort_edges(yeven, yodd, near)
    field = with_faces(split(gmid, gedge), xlow, xhigh)
    for x in range(-1, 9):
        stack(cols, x + 1, range(8), lambda t, x=x: field(x, t), near[x + 1])
    for q in range(4):
        both = jnp.dot(wd[...], cols[q * 192 : q * 192 + 384, :], preferred_element_type=F32)
        for t in range(8):
            out = step_z(both[:, tile(t)])
            for x in range(2):
                stage[2 * q + x, pl.ds(t, C, stride=8), :] = out[x * C : x * C + C]
        for x in (2 * q, 2 * q + 1):
            for pair in range(C // 2):
                even, odd = stage[x, pl.ds(pair * 16, 8), :], stage[x, pl.ds(pair * 16 + 8, 8), :]
                block[x, :, tile(pair)] = jnp.concatenate(exchange_halves(even, odd), axis=0).astype(BF16)


def back(gmid, gedge, xlow, xhigh, yodd, yeven, wd):
    scratch = [
        pltpu.VMEM((10, C, T), F32),
        pltpu.VMEM((960, ROW), BF16),
        pltpu.VMEM((8, 8 * C, T), F32),
    ]
    out = like(BF16, 8, 16, C * Z)
    return call(back_body, out, scratch, 1_000_000_000, gmid, gedge, xlow, xhigh, yodd, yeven, wd)


def flush_body(block, data, sem):
    copy = pltpu.make_async_copy(block, data, sem)
    copy.start()
    copy.wait()


def flush(block):
    return call(flush_body, block, [pltpu.SemaphoreType.DMA], 100_000, block, out_specs=HBM)


def add_body(a, b, out):
    total = a[...].astype(F32) + b[...].astype(F32)
    out[:BIAS] = total[:BIAS].astype(out.dtype)
    last = total[BIAS:]
    row = lax.broadcasted_iota(jnp.int32, (16, T), 0)
    both = last + pltpu.roll(last, 15, 0)
    rounded = both.astype(out.dtype).astype(F32)
    rest = pltpu.roll(both - rounded, 1, 0)
    out[BIAS:] = jnp.where(row == 0, rounded, jnp.where(row == 1, rest, 0.0)).astype(out.dtype)


def add(a, b, dtype, cost=100_000):
    return call(add_body, like(dtype, *a.shape), [], cost, a, b)


def finish_body(scale, own, other, filters, biases):
    for half, halves_of in enumerate(((own, other), (other, own))):

        @pl.when(my_half() == half)
        def _(halves_of=halves_of):
            for row in range(0, 288, 8):
                for dz in range(3):
                    at, group = (row, dz) if row < 216 else (row - 216 + 72 * dz, 3)
                    which, at = (0, at) if at < FIRST else (1, at - FIRST)
                    part = halves_of[which][at : at + 8]
                    moved = part if group == 0 else pltpu.roll(part, T - group * C, 1)
                    block, inside = divmod(row, C)
                    filters[block * 3 + dz, inside : inside + 8, :] = moved[:, :C] * scale
            biases[...] = halves_of[0][BIAS : BIAS + 1, :C] * scale


def finish(own, other, scale):
    out = (like(F32, 27, C, C), like(F32, 1, C))
    return call(lambda *refs: finish_body(scale, *refs), out, [], 100_000, own, other)


def permute(array, target):
    nx, ny = lax.axis_size("gx"), lax.axis_size("gy")
    pairs = []
    for x in range(nx):
        for y in range(ny):
            to = target(x, y)
            pairs.append((x * ny + y, to[0] * ny + to[1]))
    return lax.ppermute(array, ("gx", "gy"), pairs)


def swap_x(array, odd):
    nx = lax.axis_size("gx")
    return permute(array, lambda x, y: ((((x + odd) ^ 1) - odd) % nx, y))


def swap_y(array, odd):
    ny = lax.axis_size("gy")

    def target(x, y):
        to = ((y + odd) ^ 1) - odd
        return (x, to) if 0 <= to < ny else (x ^ 1, y)

    return permute(array, target)


def band(strip):
    pad = [jnp.pad(strip, ((0, 0), (0, 0), (96 * x, 96 - 96 * x))) for x in range(2)]
    return jnp.stack(pad, axis=1).reshape(192, 384)


def shards(volume, cotangent, weight, bias):
    nx, ny = lax.axis_size("gx"), lax.axis_size("gy")
    wf = band(jnp.transpose(weight, (2, 4, 0, 1, 3)).reshape(3, C, 288))
    wd = band(jnp.transpose(weight[::-1, ::-1, ::-1], (2, 3, 0, 1, 4)).reshape(3, C, 288))
    barrier = lax.optimization_barrier
    up = 7 * (1 - lax.axis_index("gx") % 2)
    xeven = lax.dynamic_slice_in_dim(volume, up, 1, 0)
    xodd = lax.dynamic_slice_in_dim(volume, 7 - up, 1, 0)
    xodd, xeven, bias = barrier((xodd, xeven, bias))
    offset = jnp.broadcast_to(bias[:, None], (C, T))
    vx = pack(volume, wf, offset)
    xodd = swap_x(xodd, 1)
    xeven = swap_x(xeven, 0)
    yodd, xlow, xhigh = odd_edge(vx, xeven, xodd)
    yodd, xlow, xhigh = barrier((yodd, xlow, xhigh))
    yeven = even_edge(vx, xlow, xhigh)
    yeven, xlow, xhigh, cotangent = barrier((yeven, xlow, xhigh, cotangent))
    yeven = swap_y(yeven, 0)
    yodd = swap_y(yodd, 1)
    gx = pack(cotangent)
    gmid, total, prod = middle(vx, gx, xlow, xhigh, wf, offset)
    yodd, total = barrier((yodd, total))
    gedge, keep, give = outer(vx, gx, xlow, xhigh, yodd, yeven, wf, offset, total, prod)

    state = dict(gmid=gmid, gedge=gedge)

    def along_x():
        xeven, xodd = gradient_faces(state["gmid"], state["gedge"])
        state["xodd"] = swap_x(xodd, 1)
        state["xeven"] = swap_x(xeven, 0)

    def along_y():
        yodd, state["xlow"], state["xhigh"] = odd_edge(state["gedge"], state["xeven"], state["xodd"])
        state["yeven"] = swap_y(even_edge(state["gedge"], state["xlow"], state["xhigh"]), 0)
        state["yodd"] = swap_y(yodd, 1)

    def data():
        names = ("gmid", "gedge", "xlow", "xhigh", "yodd", "yeven")
        state["block"] = back(*(state[name] for name in names), wd)

    def data_out():
        state["data"] = flush(state["block"])

    works = [
        (None, (), None),
        (along_x, ("gmid",), None),
        (None, (), None),
        (along_y, ("gedge", "xeven", "xodd"), None),
        (data, ("gmid",), "block"),
        (data_out, ("block",), "data"),
    ]

    def step(sent, target):
        work, tied, then = works.pop(0) if works else (None, None, None)
        if work:
            sent, given = barrier((sent, {name: state[name] for name in tied}))
            state.update(given)
        got = permute(sent, target)
        if work:
            work()
        if then:
            got, state[then] = barrier((got, state[then]))
        return sent, got

    _, got = step(give, lambda x, y: (x ^ 1, y))
    wire = add(keep, got, BF16)
    steps = [(1 << b, 0) for b in range(1, nx.bit_length() - 1)] + [(0, 1 << b) for b in range(ny.bit_length() - 1)]
    for n, (dx, dy) in enumerate(steps):
        sent, got = step(wire, lambda x, y: (x ^ dx ^ 1, y ^ dy))
        wire = add(sent, got, F32 if n == len(steps) - 1 else BF16, 10**9 if n == len(steps) - 2 else 100_000)
    scale = 1.0 / math.sqrt(8 * nx * 16 * ny * Z)
    sent, got = step(wire, lambda x, y: (x ^ 1, y))
    for work, tied, _ in works:
        if work:
            work()
    filters, biases = finish(sent, got, scale)
    return state["data"], filters.reshape(3, 3, 3, C, C), biases.reshape(C)


def solution(mesh):
    in_specs = (P("gx", "gy", None), P("gx", "gy", None), P(), P())
    out_specs = (P("gx", "gy", None), P(), P())
    return jax.shard_map(shards, mesh=mesh, in_specs=in_specs, out_specs=out_specs, check_vma=False)
```

```python
import math

import jax
import jax.numpy as jnp
from jax import lax
from jax.experimental import pallas as pl
from jax.experimental.pallas import tpu as pltpu
from jax.sharding import PartitionSpec as P

C = 32
Z = 64
T = 128
ROW = 8 * T
HALF = 112
F32 = jnp.float32
BF16 = jnp.bfloat16
VMEM_LIMIT = 48 * 1024 * 1024
VMEM = pl.BlockSpec(memory_space=pltpu.VMEM)
HBM = pl.BlockSpec(memory_space=pltpu.HBM)


def call(body, out_shape, scratch_shapes, flops, *args, in_specs=None, out_specs=None, aliases=None):
    traffic = sum(math.prod(a.shape) * a.dtype.itemsize for a in (*args, *jax.tree.leaves(out_shape)))
    return pl.pallas_call(
        body,
        out_shape=jax.tree.map(lambda a: like(a.dtype, *a.shape), out_shape),
        in_specs=in_specs or [VMEM] * len(args),
        out_specs=out_specs or jax.tree.map(lambda _: VMEM, out_shape),
        scratch_shapes=scratch_shapes,
        input_output_aliases=aliases or {},
        compiler_params=pltpu.CompilerParams(vmem_limit_bytes=VMEM_LIMIT),
        cost_estimate=pl.CostEstimate(flops=flops, bytes_accessed=traffic, transcendentals=0),
    )(*args)


def like(dtype, *shape):
    return jax.ShapeDtypeStruct(shape, dtype)


def lane(shape):
    return lax.broadcasted_iota(jnp.int32, shape, len(shape) - 1)


def swap_halves(a):
    return pltpu.roll(a, T // 2, a.ndim - 1)


def halves(low, high):
    return jnp.where(lane(low.shape) < T // 2, low, high)


def exchange_halves(a, b):
    mixed = swap_halves(halves(b, a))
    return halves(a, mixed), halves(mixed, b)


def from_below(a):
    return jnp.where(lane(a.shape) % Z == 0, 0.0, pltpu.roll(a, 1, a.ndim - 1))


def from_above(a):
    return jnp.where(lane(a.shape) % Z == Z - 1, 0.0, pltpu.roll(a, T - 1, a.ndim - 1))


def tile(t):
    return slice(t * T, t * T + T)


def to_channels(rows, stage):
    rows = rows.astype(F32)
    for pair in range(C // 2):
        even, odd = exchange_halves(rows[:8, tile(pair)], rows[8:, tile(pair)])
        stage[pl.ds(pair * 16, 8), :] = even
        stage[pl.ds(pair * 16 + 8, 8), :] = odd
    return [stage[pl.ds(t, C, stride=8), :] for t in range(8)]


def is_even(axis):
    return lax.axis_index(axis) % 2 == 0


def clear_ends(axis, low, high):
    @pl.when(lax.axis_index(axis) == 0)
    def _():
        low[...] = jnp.zeros_like(low)

    @pl.when(lax.axis_index(axis) == lax.axis_size(axis) - 1)
    def _():
        high[...] = jnp.zeros_like(high)


def scales():
    return 1.0 + lax.broadcasted_iota(jnp.int32, (8, T), 0).astype(F32) * 0.125


def my_half():
    total = 0
    for axis in ("gx", "gy"):
        for b in range(lax.axis_size(axis).bit_length() - 1):
            total = total + lax.axis_index(axis) // (1 << b)
    return total % 2


def faces(field, even, odd):
    for when, low, high in ((is_even("gx"), odd, even), (jnp.logical_not(is_even("gx")), even, odd)):

        @pl.when(when)
        def _(low=low, high=high):
            for t in range(8):
                low[:, tile(t)] = field(0, t)
                high[:, tile(t)] = field(7, t)


def pack_body(array, out, stage):
    for x in range(array.shape[0]):
        for t, part in enumerate(to_channels(array[x], stage.at[x])):
            out[x, :, tile(t)] = part.astype(BF16)


def pack(array, *after):
    def body(array, *refs):
        pack_body(array, *refs[-2:])

    return call(body, like(BF16, 8, C, ROW), [pltpu.VMEM((8, 8 * C, T), F32)], 1_000_000, array, *after)


def whole(ref):
    return lambda x, t: ref[x, :, tile(t)]


def split(mid, edge):
    return lambda x, t: edge[x, :, tile(t // 7)] if t in (0, 7) else mid[x, :, tile(t - 1)]


def with_faces(field, xlow, xhigh):
    return lambda x, t: xlow[:, tile(t)] if x < 0 else xhigh[:, tile(t)] if x > 7 else field(x, t)


def faces_body(mid, edge, even, odd):
    faces(split(mid, edge), even, odd)


def gradient_faces(mid, edge):
    face = like(BF16, C, ROW)
    return call(faces_body, (face, face), [], 100_000, mid, edge)


def sort(axis, even, odd, low, high):
    @pl.when(is_even(axis))
    def _():
        low[...] = odd[...]
        high[...] = even[...]

    @pl.when(jnp.logical_not(is_even(axis)))
    def _():
        low[...] = even[...]
        high[...] = odd[...]

    clear_ends(axis, low, high)


def edge_message(field, low_when, out):
    @pl.when(low_when)
    def _():
        for row in range(5):
            out[row] = halves(field(row + 4, 0).astype(F32), swap_halves(field(row - 1, 0).astype(F32))).astype(BF16)

    @pl.when(jnp.logical_not(low_when))
    def _():
        for row in range(5):
            out[row] = halves(swap_halves(field(row - 1, 7).astype(F32)), field(row + 4, 7).astype(F32)).astype(BF16)


def ends(ref):
    last = ref.shape[-1] // T - 1
    return lambda x, t: ref[x, :, tile(last if t else 0)]


def odd_edge_body(field, xeven, xodd, out, xlow, xhigh, *scratch):
    if scratch:
        stage, packed = scratch
        pack_body(xeven, packed.at[pl.ds(0, 1)], stage.at[pl.ds(0, 1)])
        pack_body(xodd, packed.at[pl.ds(1, 1)], stage.at[pl.ds(1, 1)])
        xeven, xodd = packed.at[0], packed.at[1]
    sort("gx", xeven, xodd, xlow, xhigh)
    edge_message(with_faces(ends(field), xlow, xhigh), is_even("gy"), out)


def odd_edge(field, xeven, xodd):
    face = like(BF16, C, ROW)
    scratch = [pltpu.VMEM((2, 8 * C, T), F32), pltpu.VMEM((2, C, ROW), BF16)] if xeven.ndim == 3 else []
    return call(odd_edge_body, (like(BF16, 5, C, T), face, face), scratch, 100_000, field, xeven, xodd)


def even_edge_body(field, xlow, xhigh, out):
    edge_message(with_faces(ends(field), xlow, xhigh), jnp.logical_not(is_even("gy")), out)


def even_edge(field, xlow, xhigh):
    return call(even_edge_body, like(BF16, 5, C, T), [], 100_000, field, xlow, xhigh)


def sort_edges(even, odd, near):
    for when, low, high in ((is_even("gy"), odd, even), (jnp.logical_not(is_even("gy")), even, odd)):

        @pl.when(when)
        def _(low=low, high=high):
            for row in range(5):
                a, b = low[row].astype(F32), high[row].astype(F32)
                near[row] = halves(a, b)
                near[row + 5] = halves(swap_halves(a), swap_halves(b))

    place = lax.axis_index("gy")
    for when, empty in ((place == 0, 0), (place == lax.axis_size("gy") - 1, 1)):

        @pl.when(when)
        def _(empty=empty):
            for row in range(10):
                near[row] = halves(near[row], jnp.zeros((C, T), F32)) if empty else halves(jnp.zeros((C, T), F32), near[row])


def activation(pre, grad_out):
    sig = 1.0 / (1.0 + jnp.exp(-pre))
    return grad_out.astype(F32) * sig * (1.0 + pre * (1.0 - sig))


def stack(out, i, tiles, field, near=None):
    for n, t in enumerate(tiles):
        for dy in range(3):
            if t + dy == 0:
                part = halves(near, swap_halves(field(7).astype(F32))).astype(BF16)
            elif t + dy == 9:
                part = halves(swap_halves(field(0).astype(F32)), near).astype(BF16)
            else:
                part = field(t + dy - 1)
            out[(3 * i + dy) * C : (3 * i + dy + 1) * C, tile(n)] = part


def step_z(part):
    return from_below(part[:64]) + part[64:128] + from_above(part[128:])


def gradient(tiles, gx, wf, bias, cols, gps, out):
    offset = jnp.concatenate([bias[...]] * 2, axis=0)
    total = jnp.zeros((64, T), F32)
    for q in range(4):
        both = jnp.dot(wf[...], cols[q * 192 : q * 192 + 384, :], preferred_element_type=F32)
        for n, t in enumerate(tiles):
            grad_out = gx[2 * q : 2 * q + 2, :, tile(t)].reshape(64, T)
            grad = activation(step_z(both[:, tile(n)]) + offset, grad_out).astype(BF16)
            out[2 * q : 2 * q + 2, :, tile(n)] = grad.reshape(2, C, T)
            grad = grad.astype(F32)
            total = total + grad
            gps[q * 192 : q * 192 + 64, tile(n)] = from_above(grad).astype(BF16)
            gps[q * 192 + 64 : q * 192 + 128, tile(n)] = grad.astype(BF16)
            gps[q * 192 + 128 : q * 192 + 192, tile(n)] = from_below(grad).astype(BF16)
    prod = jnp.zeros((384, 192), F32)
    for q in range(4):
        prod = prod + lax.dot_general(
            cols[q * 192 : q * 192 + 384, :],
            gps[q * 192 : q * 192 + 192, :],
            (((1,), (1,)), ((), ())),
            preferred_element_type=F32,
        )
    return total, prod


MID = range(1, 7)
EDGE = (0, 7)


def middle_body(vx, gx, xlow, xhigh, wf, bias, gmid, total, prod, cols, gps):
    field = with_faces(whole(vx), xlow, xhigh)
    for x in range(-1, 9):
        stack(cols, x + 1, MID, lambda t, x=x: field(x, t))
    total[...], prod[...] = gradient(MID, gx, wf, bias, cols, gps, gmid)


def middle(vx, gx, xlow, xhigh, wf, bias):
    out = (like(BF16, 8, C, 6 * T), like(F32, 64, T), like(F32, 384, 192))
    scratch = [pltpu.VMEM((960, 6 * T), BF16), pltpu.VMEM((768, 6 * T), BF16)]
    return call(middle_body, out, scratch, 1_000_000, vx, gx, xlow, xhigh, wf, bias)


def outer_body(vx, gx, xlow, xhigh, yodd, yeven, wf, bias, total, prod, gedge, keep, give, near, cols, gps, wire):
    sort_edges(yeven, yodd, near)
    field = with_faces(whole(vx), xlow, xhigh)
    for x in range(-1, 9):
        stack(cols, x + 1, EDGE, lambda t, x=x: field(x, t), near[x + 1])
    more_total, more = gradient(EDGE, gx, wf, bias, cols, gps, gedge)
    total, prod = total[...] + more_total, prod[...] + more
    group = lane((8, T)) // C
    rows = []
    for row in range(0, 288, 8):
        a, b = prod[row : row + 8], prod[row + 96 : row + 104]
        a = jnp.concatenate([a[:, T:], jnp.zeros((8, 64), F32)], axis=1), a[:, :T]
        b = jnp.concatenate([b[:, T:], jnp.zeros((8, 64), F32)], axis=1), b[:, :T]
        near = a[1] + pltpu.roll(b[1], T - C, 1)
        far = a[0] + pltpu.roll(b[0], T - C, 1)
        rows.append((near, pltpu.roll(near, T - C, 1), pltpu.roll(far, 2 * C, 1), far))
    for i in range(27):
        near, moved, far, _ = rows[i]
        dz, at = divmod(i, 9)
        near2, moved2, far2, plain2 = rows[27 + at]
        last = pltpu.roll((near2, near2, plain2)[dz], (3 * C, C, 3 * C)[dz], 1)
        out = jnp.where(group == 0, near, jnp.where(group == 1, moved, jnp.where(group == 2, far, last)))
        wire[8 * i : 8 * i + 8] = out
    total = jnp.concatenate([total[:C] + total[C:], jnp.zeros((T - C, T), F32)], axis=0)
    total = jnp.sum(total.T, axis=0, keepdims=True)
    wire[216:] = total * scales()
    for half in range(2):

        @pl.when(my_half() == half)
        def _(half=half):
            keep[...] = wire[half * HALF : half * HALF + HALF]
            give[...] = wire[HALF - half * HALF : 2 * HALF - half * HALF]


def outer(vx, gx, xlow, xhigh, yodd, yeven, wf, bias, total, prod):
    out = (like(BF16, 8, C, 2 * T), like(F32, HALF, T), like(F32, HALF, T))
    scratch = [
        pltpu.VMEM((10, C, T), F32),
        pltpu.VMEM((960, 2 * T), BF16),
        pltpu.VMEM((768, 2 * T), BF16),
        pltpu.VMEM((2 * HALF, T), F32),
    ]
    args = (vx, gx, xlow, xhigh, yodd, yeven, wf, bias, total, prod)
    return call(outer_body, out, scratch, 700_000_000, *args)


def back_body(gmid, gedge, xlow, xhigh, yodd, yeven, wd, block, near, cols, stage):
    sort_edges(yeven, yodd, near)
    field = with_faces(split(gmid, gedge), xlow, xhigh)
    for x in range(-1, 9):
        stack(cols, x + 1, range(8), lambda t, x=x: field(x, t), near[x + 1])
    for q in range(4):
        both = jnp.dot(wd[...], cols[q * 192 : q * 192 + 384, :], preferred_element_type=F32)
        for t in range(8):
            out = step_z(both[:, tile(t)])
            for x in range(2):
                stage[2 * q + x, pl.ds(t, C, stride=8), :] = out[x * C : x * C + C]
        for x in (2 * q, 2 * q + 1):
            for pair in range(C // 2):
                even, odd = stage[x, pl.ds(pair * 16, 8), :], stage[x, pl.ds(pair * 16 + 8, 8), :]
                block[x, :, tile(pair)] = jnp.concatenate(exchange_halves(even, odd), axis=0).astype(BF16)


def back(gmid, gedge, xlow, xhigh, yodd, yeven, wd):
    scratch = [
        pltpu.VMEM((10, C, T), F32),
        pltpu.VMEM((960, ROW), BF16),
        pltpu.VMEM((8, 8 * C, T), F32),
    ]
    out = like(BF16, 8, 16, C * Z)
    return call(back_body, out, scratch, 1_000_000_000, gmid, gedge, xlow, xhigh, yodd, yeven, wd)


def flush_body(block, data, sem):
    copy = pltpu.make_async_copy(block, data, sem)
    copy.start()
    copy.wait()


def flush(block):
    return call(flush_body, block, [pltpu.SemaphoreType.DMA], 100_000, block, out_specs=HBM)


def add_body(a, b, out):
    out[...] = (a[...].astype(F32) + b[...].astype(F32)).astype(out.dtype)


def add(a, b, dtype, cost=100_000):
    return call(add_body, like(dtype, *a.shape), [], cost, a, b)


def finish_body(scale, own, other, filters, biases):
    for half, halves_of in enumerate(((own, other), (other, own))):

        @pl.when(my_half() == half)
        def _(halves_of=halves_of):
            for row in range(0, 288, 8):
                for dz in range(3):
                    at, group = (row, dz) if row < 216 else (row - 216 + 72 * dz, 3)
                    part = halves_of[at // HALF][at % HALF : at % HALF + 8]
                    moved = part if group == 0 else pltpu.roll(part, T - group * C, 1)
                    block, inside = divmod(row, C)
                    filters[block * 3 + dz, inside : inside + 8, :] = moved[:, :C] * scale
            eight = halves_of[1][216 - HALF :] / scales()
            biases[...] = jnp.sum(eight, axis=0, keepdims=True)[:, :C] * (scale / 8)


def finish(own, other, scale):
    out = (like(F32, 27, C, C), like(F32, 1, C))
    return call(lambda *refs: finish_body(scale, *refs), out, [], 100_000, own, other)


def permute(array, target):
    nx, ny = lax.axis_size("gx"), lax.axis_size("gy")
    pairs = []
    for x in range(nx):
        for y in range(ny):
            to = target(x, y)
            pairs.append((x * ny + y, to[0] * ny + to[1]))
    return lax.ppermute(array, ("gx", "gy"), pairs)


def swap_x(array, odd):
    nx = lax.axis_size("gx")
    return permute(array, lambda x, y: ((((x + odd) ^ 1) - odd) % nx, y))


def swap_y(array, odd):
    ny = lax.axis_size("gy")

    def target(x, y):
        to = ((y + odd) ^ 1) - odd
        return (x, to) if 0 <= to < ny else (x ^ 1, y)

    return permute(array, target)


def band(strip):
    pad = [jnp.pad(strip, ((0, 0), (0, 0), (96 * x, 96 - 96 * x))) for x in range(2)]
    return jnp.stack(pad, axis=1).reshape(192, 384)


def shards(volume, cotangent, weight, bias):
    nx, ny = lax.axis_size("gx"), lax.axis_size("gy")
    wf = band(jnp.transpose(weight, (2, 4, 0, 1, 3)).reshape(3, C, 288))
    wd = band(jnp.transpose(weight[::-1, ::-1, ::-1], (2, 3, 0, 1, 4)).reshape(3, C, 288))
    barrier = lax.optimization_barrier
    up = 7 * (1 - lax.axis_index("gx") % 2)
    xeven = lax.dynamic_slice_in_dim(volume, up, 1, 0)
    xodd = lax.dynamic_slice_in_dim(volume, 7 - up, 1, 0)
    xodd, xeven, bias = barrier((xodd, xeven, bias))
    offset = jnp.broadcast_to(bias[:, None], (C, T))
    vx = pack(volume, wf, offset)
    xodd = swap_x(xodd, 1)
    xeven = swap_x(xeven, 0)
    yodd, xlow, xhigh = odd_edge(vx, xeven, xodd)
    yodd, xlow, xhigh = barrier((yodd, xlow, xhigh))
    yeven = even_edge(vx, xlow, xhigh)
    yeven, xlow, xhigh, cotangent = barrier((yeven, xlow, xhigh, cotangent))
    yeven = swap_y(yeven, 0)
    yodd = swap_y(yodd, 1)
    gx = pack(cotangent)
    gmid, total, prod = middle(vx, gx, xlow, xhigh, wf, offset)
    yodd, total = barrier((yodd, total))
    gedge, keep, give = outer(vx, gx, xlow, xhigh, yodd, yeven, wf, offset, total, prod)

    state = dict(gmid=gmid, gedge=gedge)

    def along_x():
        xeven, xodd = gradient_faces(state["gmid"], state["gedge"])
        state["xodd"] = swap_x(xodd, 1)
        state["xeven"] = swap_x(xeven, 0)

    def along_y():
        yodd, state["xlow"], state["xhigh"] = odd_edge(state["gedge"], state["xeven"], state["xodd"])
        state["yeven"] = swap_y(even_edge(state["gedge"], state["xlow"], state["xhigh"]), 0)
        state["yodd"] = swap_y(yodd, 1)

    def data():
        names = ("gmid", "gedge", "xlow", "xhigh", "yodd", "yeven")
        state["block"] = back(*(state[name] for name in names), wd)

    def data_out():
        state["data"] = flush(state["block"])

    works = [
        (None, (), None),
        (along_x, ("gmid",), None),
        (None, (), None),
        (along_y, ("gedge", "xeven", "xodd"), None),
        (data, ("gmid",), "block"),
        (data_out, ("block",), "data"),
    ]

    def step(sent, target):
        work, tied, then = works.pop(0) if works else (None, None, None)
        if work:
            sent, given = barrier((sent, {name: state[name] for name in tied}))
            state.update(given)
        got = permute(sent, target)
        if work:
            work()
        if then:
            got, state[then] = barrier((got, state[then]))
        return sent, got

    _, got = step(give, lambda x, y: (x ^ 1, y))
    wire = add(keep, got, BF16)
    steps = [(1 << b, 0) for b in range(1, nx.bit_length() - 1)] + [(0, 1 << b) for b in range(ny.bit_length() - 1)]
    for n, (dx, dy) in enumerate(steps):
        sent, got = step(wire, lambda x, y: (x ^ dx ^ 1, y ^ dy))
        wire = add(sent, got, F32 if n == len(steps) - 1 else BF16, 10**9 if n == len(steps) - 2 else 100_000)
    scale = 1.0 / math.sqrt(8 * nx * 16 * ny * Z)
    sent, got = step(wire, lambda x, y: (x ^ 1, y))
    for work, tied, _ in works:
        if work:
            work()
    filters, biases = finish(sent, got, scale)
    return state["data"], filters.reshape(3, 3, 3, C, C), biases.reshape(C)


def solution(mesh):
    in_specs = (P("gx", "gy", None), P("gx", "gy", None), P(), P())
    out_specs = (P("gx", "gy", None), P(), P())
    return jax.shard_map(shards, mesh=mesh, in_specs=in_specs, out_specs=out_specs, check_vma=False)
```

```python
import math

import jax
import jax.numpy as jnp
from jax import lax
from jax.experimental import pallas as pl
from jax.experimental.pallas import tpu as pltpu
from jax.sharding import PartitionSpec as P

C = 32
Z = 64
T = 128
ROW = 8 * T
HALF = 112
F32 = jnp.float32
BF16 = jnp.bfloat16
VMEM_LIMIT = 48 * 1024 * 1024
VMEM = pl.BlockSpec(memory_space=pltpu.VMEM)
HBM = pl.BlockSpec(memory_space=pltpu.HBM)


def call(body, out_shape, scratch_shapes, flops, *args, in_specs=None, out_specs=None, aliases=None):
    traffic = sum(math.prod(a.shape) * a.dtype.itemsize for a in (*args, *jax.tree.leaves(out_shape)))
    return pl.pallas_call(
        body,
        out_shape=jax.tree.map(lambda a: like(a.dtype, *a.shape), out_shape),
        in_specs=in_specs or [VMEM] * len(args),
        out_specs=out_specs or jax.tree.map(lambda _: VMEM, out_shape),
        scratch_shapes=scratch_shapes,
        input_output_aliases=aliases or {},
        compiler_params=pltpu.CompilerParams(vmem_limit_bytes=VMEM_LIMIT),
        cost_estimate=pl.CostEstimate(flops=flops, bytes_accessed=traffic, transcendentals=0),
    )(*args)


def like(dtype, *shape):
    return jax.ShapeDtypeStruct(shape, dtype)


def lane(shape):
    return lax.broadcasted_iota(jnp.int32, shape, len(shape) - 1)


def swap_halves(a):
    return pltpu.roll(a, T // 2, a.ndim - 1)


def halves(low, high):
    return jnp.where(lane(low.shape) < T // 2, low, high)


def exchange_halves(a, b):
    mixed = swap_halves(halves(b, a))
    return halves(a, mixed), halves(mixed, b)


def from_below(a):
    return jnp.where(lane(a.shape) % Z == 0, 0.0, pltpu.roll(a, 1, a.ndim - 1))


def from_above(a):
    return jnp.where(lane(a.shape) % Z == Z - 1, 0.0, pltpu.roll(a, T - 1, a.ndim - 1))


def tile(t):
    return slice(t * T, t * T + T)


def to_channels(rows, stage):
    rows = rows.astype(F32)
    for pair in range(C // 2):
        even, odd = exchange_halves(rows[:8, tile(pair)], rows[8:, tile(pair)])
        stage[pl.ds(pair * 16, 8), :] = even
        stage[pl.ds(pair * 16 + 8, 8), :] = odd
    return [stage[pl.ds(t, C, stride=8), :] for t in range(8)]


def is_even(axis):
    return lax.axis_index(axis) % 2 == 0


def clear_ends(axis, low, high):
    @pl.when(lax.axis_index(axis) == 0)
    def _():
        low[...] = jnp.zeros_like(low)

    @pl.when(lax.axis_index(axis) == lax.axis_size(axis) - 1)
    def _():
        high[...] = jnp.zeros_like(high)


def scales():
    return 1.0 + lax.broadcasted_iota(jnp.int32, (8, T), 0).astype(F32) * 0.125


def my_half():
    total = 0
    for axis in ("gx", "gy"):
        for b in range(lax.axis_size(axis).bit_length() - 1):
            total = total + lax.axis_index(axis) // (1 << b)
    return total % 2


def faces(field, even, odd):
    for when, low, high in ((is_even("gx"), odd, even), (jnp.logical_not(is_even("gx")), even, odd)):

        @pl.when(when)
        def _(low=low, high=high):
            for t in range(8):
                low[:, tile(t)] = field(0, t)
                high[:, tile(t)] = field(7, t)


def pack_body(array, out, stage):
    for x in range(array.shape[0]):
        for t, part in enumerate(to_channels(array[x], stage.at[x])):
            out[x, :, tile(t)] = part.astype(BF16)


def pack(array, *after):
    def body(array, *refs):
        pack_body(array, *refs[-2:])

    return call(body, like(BF16, 8, C, ROW), [pltpu.VMEM((8, 8 * C, T), F32)], 1_000_000, array, *after)


def whole(ref):
    return lambda x, t: ref[x, :, tile(t)]


def split(mid, edge):
    return lambda x, t: edge[x, :, tile(t // 7)] if t in (0, 7) else mid[x, :, tile(t - 1)]


def with_faces(field, xlow, xhigh):
    return lambda x, t: xlow[:, tile(t)] if x < 0 else xhigh[:, tile(t)] if x > 7 else field(x, t)


def faces_body(mid, edge, even, odd):
    faces(split(mid, edge), even, odd)


def gradient_faces(mid, edge):
    face = like(BF16, C, ROW)
    return call(faces_body, (face, face), [], 100_000, mid, edge)


def sort(axis, even, odd, low, high):
    @pl.when(is_even(axis))
    def _():
        low[...] = odd[...]
        high[...] = even[...]

    @pl.when(jnp.logical_not(is_even(axis)))
    def _():
        low[...] = even[...]
        high[...] = odd[...]

    clear_ends(axis, low, high)


def edge_message(field, low_when, out):
    @pl.when(low_when)
    def _():
        for row in range(5):
            out[row] = halves(field(row + 4, 0).astype(F32), swap_halves(field(row - 1, 0).astype(F32))).astype(BF16)

    @pl.when(jnp.logical_not(low_when))
    def _():
        for row in range(5):
            out[row] = halves(swap_halves(field(row - 1, 7).astype(F32)), field(row + 4, 7).astype(F32)).astype(BF16)


def ends(ref):
    last = ref.shape[-1] // T - 1
    return lambda x, t: ref[x, :, tile(last if t else 0)]


def odd_edge_body(field, xeven, xodd, out, xlow, xhigh, *scratch):
    if scratch:
        stage, packed = scratch
        pack_body(xeven, packed.at[pl.ds(0, 1)], stage.at[pl.ds(0, 1)])
        pack_body(xodd, packed.at[pl.ds(1, 1)], stage.at[pl.ds(1, 1)])
        xeven, xodd = packed.at[0], packed.at[1]
    sort("gx", xeven, xodd, xlow, xhigh)
    edge_message(with_faces(ends(field), xlow, xhigh), is_even("gy"), out)


def odd_edge(field, xeven, xodd):
    face = like(BF16, C, ROW)
    scratch = [pltpu.VMEM((2, 8 * C, T), F32), pltpu.VMEM((2, C, ROW), BF16)] if xeven.ndim == 3 else []
    return call(odd_edge_body, (like(BF16, 5, C, T), face, face), scratch, 100_000, field, xeven, xodd)


def even_edge_body(field, xlow, xhigh, out):
    edge_message(with_faces(ends(field), xlow, xhigh), jnp.logical_not(is_even("gy")), out)


def even_edge(field, xlow, xhigh):
    return call(even_edge_body, like(BF16, 5, C, T), [], 100_000, field, xlow, xhigh)


def sort_edges(even, odd, near):
    for when, low, high in ((is_even("gy"), odd, even), (jnp.logical_not(is_even("gy")), even, odd)):

        @pl.when(when)
        def _(low=low, high=high):
            for row in range(5):
                a, b = low[row].astype(F32), high[row].astype(F32)
                near[row] = halves(a, b)
                near[row + 5] = halves(swap_halves(a), swap_halves(b))

    place = lax.axis_index("gy")
    for when, empty in ((place == 0, 0), (place == lax.axis_size("gy") - 1, 1)):

        @pl.when(when)
        def _(empty=empty):
            for row in range(10):
                near[row] = halves(near[row], jnp.zeros((C, T), F32)) if empty else halves(jnp.zeros((C, T), F32), near[row])


def activation(pre, grad_out):
    sig = 1.0 / (1.0 + jnp.exp(-pre))
    return grad_out.astype(F32) * sig * (1.0 + pre * (1.0 - sig))


def stack(out, i, tiles, field, near=None):
    for n, t in enumerate(tiles):
        for dy in range(3):
            if t + dy == 0:
                part = halves(near, swap_halves(field(7).astype(F32))).astype(BF16)
            elif t + dy == 9:
                part = halves(swap_halves(field(0).astype(F32)), near).astype(BF16)
            else:
                part = field(t + dy - 1)
            out[(3 * i + dy) * C : (3 * i + dy + 1) * C, tile(n)] = part


def step_z(part):
    return from_below(part[:64]) + part[64:128] + from_above(part[128:])


def gradient(tiles, gx, wf, bias, cols, gps, out):
    offset = jnp.concatenate([bias[...]] * 2, axis=0)
    total = jnp.zeros((64, T), F32)
    for q in range(4):
        both = jnp.dot(wf[...], cols[q * 192 : q * 192 + 384, :], preferred_element_type=F32)
        for n, t in enumerate(tiles):
            grad_out = gx[2 * q : 2 * q + 2, :, tile(t)].reshape(64, T)
            grad = activation(step_z(both[:, tile(n)]) + offset, grad_out).astype(BF16)
            out[2 * q : 2 * q + 2, :, tile(n)] = grad.reshape(2, C, T)
            grad = grad.astype(F32)
            total = total + grad
            gps[q * 192 : q * 192 + 64, tile(n)] = from_above(grad).astype(BF16)
            gps[q * 192 + 64 : q * 192 + 128, tile(n)] = grad.astype(BF16)
            gps[q * 192 + 128 : q * 192 + 192, tile(n)] = from_below(grad).astype(BF16)
    prod = jnp.zeros((384, 192), F32)
    for q in range(4):
        prod = prod + lax.dot_general(
            cols[q * 192 : q * 192 + 384, :],
            gps[q * 192 : q * 192 + 192, :],
            (((1,), (1,)), ((), ())),
            preferred_element_type=F32,
        )
    return total, prod


MID = range(1, 7)
EDGE = (0, 7)


def middle_body(vx, gx, xlow, xhigh, wf, bias, gmid, total, prod, cols, gps):
    field = with_faces(whole(vx), xlow, xhigh)
    for x in range(-1, 9):
        stack(cols, x + 1, MID, lambda t, x=x: field(x, t))
    total[...], prod[...] = gradient(MID, gx, wf, bias, cols, gps, gmid)


def middle(vx, gx, xlow, xhigh, wf, bias):
    out = (like(BF16, 8, C, 6 * T), like(F32, 64, T), like(F32, 384, 192))
    scratch = [pltpu.VMEM((960, 6 * T), BF16), pltpu.VMEM((768, 6 * T), BF16)]
    return call(middle_body, out, scratch, 1_000_000, vx, gx, xlow, xhigh, wf, bias)


def outer_body(vx, gx, xlow, xhigh, yodd, yeven, wf, bias, total, prod, gedge, keep, give, near, cols, gps, wire):
    sort_edges(yeven, yodd, near)
    field = with_faces(whole(vx), xlow, xhigh)
    for x in range(-1, 9):
        stack(cols, x + 1, EDGE, lambda t, x=x: field(x, t), near[x + 1])
    more_total, more = gradient(EDGE, gx, wf, bias, cols, gps, gedge)
    total, prod = total[...] + more_total, prod[...] + more
    group = lane((8, T)) // C
    rows = []
    for row in range(0, 288, 8):
        a, b = prod[row : row + 8], prod[row + 96 : row + 104]
        a = jnp.concatenate([a[:, T:], jnp.zeros((8, 64), F32)], axis=1), a[:, :T]
        b = jnp.concatenate([b[:, T:], jnp.zeros((8, 64), F32)], axis=1), b[:, :T]
        near = a[1] + pltpu.roll(b[1], T - C, 1)
        far = a[0] + pltpu.roll(b[0], T - C, 1)
        rows.append((near, pltpu.roll(near, T - C, 1), pltpu.roll(far, 2 * C, 1), far))
    for i in range(27):
        near, moved, far, _ = rows[i]
        dz, at = divmod(i, 9)
        near2, moved2, far2, plain2 = rows[27 + at]
        last = pltpu.roll((near2, near2, plain2)[dz], (3 * C, C, 3 * C)[dz], 1)
        out = jnp.where(group == 0, near, jnp.where(group == 1, moved, jnp.where(group == 2, far, last)))
        wire[8 * i : 8 * i + 8] = out
    total = jnp.concatenate([total[:C] + total[C:], jnp.zeros((T - C, T), F32)], axis=0)
    total = jnp.sum(total.T, axis=0, keepdims=True)
    wire[216:] = total * scales()
    for half in range(2):

        @pl.when(my_half() == half)
        def _(half=half):
            keep[...] = wire[half * HALF : half * HALF + HALF]
            give[...] = wire[HALF - half * HALF : 2 * HALF - half * HALF]


def outer(vx, gx, xlow, xhigh, yodd, yeven, wf, bias, total, prod):
    out = (like(BF16, 8, C, 2 * T), like(F32, HALF, T), like(F32, HALF, T))
    scratch = [
        pltpu.VMEM((10, C, T), F32),
        pltpu.VMEM((960, 2 * T), BF16),
        pltpu.VMEM((768, 2 * T), BF16),
        pltpu.VMEM((2 * HALF, T), F32),
    ]
    args = (vx, gx, xlow, xhigh, yodd, yeven, wf, bias, total, prod)
    return call(outer_body, out, scratch, 700_000_000, *args)


def back_body(gmid, gedge, xlow, xhigh, yodd, yeven, wd, block, near, cols, stage):
    sort_edges(yeven, yodd, near)
    field = with_faces(split(gmid, gedge), xlow, xhigh)
    for x in range(-1, 9):
        stack(cols, x + 1, range(8), lambda t, x=x: field(x, t), near[x + 1])
    for q in range(4):
        both = jnp.dot(wd[...], cols[q * 192 : q * 192 + 384, :], preferred_element_type=F32)
        for t in range(8):
            out = step_z(both[:, tile(t)])
            for x in range(2):
                stage[2 * q + x, pl.ds(t, C, stride=8), :] = out[x * C : x * C + C]
        for x in (2 * q, 2 * q + 1):
            for pair in range(C // 2):
                even, odd = stage[x, pl.ds(pair * 16, 8), :], stage[x, pl.ds(pair * 16 + 8, 8), :]
                block[x, :, tile(pair)] = jnp.concatenate(exchange_halves(even, odd), axis=0).astype(BF16)


def back(gmid, gedge, xlow, xhigh, yodd, yeven, wd):
    scratch = [
        pltpu.VMEM((10, C, T), F32),
        pltpu.VMEM((960, ROW), BF16),
        pltpu.VMEM((8, 8 * C, T), F32),
    ]
    out = like(BF16, 8, 16, C * Z)
    return call(back_body, out, scratch, 1_000_000_000, gmid, gedge, xlow, xhigh, yodd, yeven, wd)


def flush_body(block, data, sem):
    copy = pltpu.make_async_copy(block, data, sem)
    copy.start()
    copy.wait()


def flush(block):
    return call(flush_body, block, [pltpu.SemaphoreType.DMA], 100_000, block, out_specs=HBM)


def add_body(a, b, out):
    out[...] = (a[...].astype(F32) + b[...].astype(F32)).astype(out.dtype)


def add(a, b, dtype, cost=100_000):
    return call(add_body, like(dtype, *a.shape), [], cost, a, b)


def finish_body(scale, own, other, filters, biases):
    for half, halves_of in enumerate(((own, other), (other, own))):

        @pl.when(my_half() == half)
        def _(halves_of=halves_of):
            for row in range(0, 288, 8):
                for dz in range(3):
                    at, group = (row, dz) if row < 216 else (row - 216 + 72 * dz, 3)
                    part = halves_of[at // HALF][at % HALF : at % HALF + 8]
                    moved = part if group == 0 else pltpu.roll(part, T - group * C, 1)
                    block, inside = divmod(row, C)
                    filters[block * 3 + dz, inside : inside + 8, :] = moved[:, :C] * scale
            eight = halves_of[1][216 - HALF :] / scales()
            biases[...] = jnp.sum(eight, axis=0, keepdims=True)[:, :C] * (scale / 8)


def finish(own, other, scale):
    out = (like(F32, 27, C, C), like(F32, 1, C))
    return call(lambda *refs: finish_body(scale, *refs), out, [], 100_000, own, other)


def permute(array, target):
    nx, ny = lax.axis_size("gx"), lax.axis_size("gy")
    pairs = []
    for x in range(nx):
        for y in range(ny):
            to = target(x, y)
            pairs.append((x * ny + y, to[0] * ny + to[1]))
    return lax.ppermute(array, ("gx", "gy"), pairs)


def swap_x(array, odd):
    nx = lax.axis_size("gx")
    return permute(array, lambda x, y: ((((x + odd) ^ 1) - odd) % nx, y))


def swap_y(array, odd):
    ny = lax.axis_size("gy")

    def target(x, y):
        to = ((y + odd) ^ 1) - odd
        return (x, to) if 0 <= to < ny else (x ^ 1, y)

    return permute(array, target)


def band(strip):
    pad = [jnp.pad(strip, ((0, 0), (0, 0), (96 * x, 96 - 96 * x))) for x in range(2)]
    return jnp.stack(pad, axis=1).reshape(192, 384)


def shards(volume, cotangent, weight, bias):
    nx, ny = lax.axis_size("gx"), lax.axis_size("gy")
    wf = band(jnp.transpose(weight, (2, 4, 0, 1, 3)).reshape(3, C, 288))
    wd = band(jnp.transpose(weight[::-1, ::-1, ::-1], (2, 3, 0, 1, 4)).reshape(3, C, 288))
    barrier = lax.optimization_barrier
    up = 7 * (1 - lax.axis_index("gx") % 2)
    xeven = lax.dynamic_slice_in_dim(volume, up, 1, 0)
    xodd = lax.dynamic_slice_in_dim(volume, 7 - up, 1, 0)
    xodd, xeven, bias = barrier((xodd, xeven, bias))
    offset = jnp.broadcast_to(bias[:, None], (C, T))
    vx = pack(volume, wf, wd, offset)
    xodd = swap_x(xodd, 1)
    xeven = swap_x(xeven, 0)
    yodd, xlow, xhigh = odd_edge(vx, xeven, xodd)
    yodd, xlow, xhigh = barrier((yodd, xlow, xhigh))
    yeven = even_edge(vx, xlow, xhigh)
    yeven, xlow, xhigh, cotangent = barrier((yeven, xlow, xhigh, cotangent))
    yeven = swap_y(yeven, 0)
    yodd = swap_y(yodd, 1)
    gx = pack(cotangent)
    gmid, total, prod = middle(vx, gx, xlow, xhigh, wf, offset)
    yodd, total = barrier((yodd, total))
    gedge, keep, give = outer(vx, gx, xlow, xhigh, yodd, yeven, wf, offset, total, prod)

    state = dict(gmid=gmid, gedge=gedge)

    def along_x():
        xeven, xodd = gradient_faces(state["gmid"], state["gedge"])
        state["xodd"] = swap_x(xodd, 1)
        state["xeven"] = swap_x(xeven, 0)

    def along_y():
        yodd, state["xlow"], state["xhigh"] = odd_edge(state["gedge"], state["xeven"], state["xodd"])
        state["yeven"] = swap_y(even_edge(state["gedge"], state["xlow"], state["xhigh"]), 0)
        state["yodd"] = swap_y(yodd, 1)

    def data():
        names = ("gmid", "gedge", "xlow", "xhigh", "yodd", "yeven")
        state["block"] = back(*(state[name] for name in names), wd)

    def data_out():
        state["data"] = flush(state["block"])

    works = [
        (None, (), None),
        (along_x, ("gmid",), None),
        (None, (), None),
        (along_y, ("gedge", "xeven", "xodd"), None),
        (data, ("gmid",), "block"),
        (data_out, ("block",), "data"),
    ]

    def step(sent, target):
        work, tied, then = works.pop(0) if works else (None, None, None)
        if work:
            sent, given = barrier((sent, {name: state[name] for name in tied}))
            state.update(given)
        got = permute(sent, target)
        if work:
            work()
        if then:
            got, state[then] = barrier((got, state[then]))
        return sent, got

    _, got = step(give, lambda x, y: (x ^ 1, y))
    wire = add(keep, got, BF16)
    steps = [(1 << b, 0) for b in range(1, nx.bit_length() - 1)] + [(0, 1 << b) for b in range(ny.bit_length() - 1)]
    for n, (dx, dy) in enumerate(steps):
        sent, got = step(wire, lambda x, y: (x ^ dx ^ 1, y ^ dy))
        wire = add(sent, got, F32 if n == len(steps) - 1 else BF16, 10**9 if n == len(steps) - 2 else 100_000)
    scale = 1.0 / math.sqrt(8 * nx * 16 * ny * Z)
    sent, got = step(wire, lambda x, y: (x ^ 1, y))
    for work, tied, _ in works:
        if work:
            work()
    filters, biases = finish(sent, got, scale)
    return state["data"], filters.reshape(3, 3, 3, C, C), biases.reshape(C)


def solution(mesh):
    in_specs = (P("gx", "gy", None), P("gx", "gy", None), P(), P())
    out_specs = (P("gx", "gy", None), P(), P())
    return jax.shard_map(shards, mesh=mesh, in_specs=in_specs, out_specs=out_specs, check_vma=False)
```

```python
import math

import jax
import jax.numpy as jnp
from jax import lax
from jax.experimental import pallas as pl
from jax.experimental.pallas import tpu as pltpu
from jax.sharding import PartitionSpec as P

C = 32
Z = 64
T = 128
ROW = 8 * T
HALF = 112
F32 = jnp.float32
BF16 = jnp.bfloat16
VMEM_LIMIT = 48 * 1024 * 1024
VMEM = pl.BlockSpec(memory_space=pltpu.VMEM)
HBM = pl.BlockSpec(memory_space=pltpu.HBM)


def call(body, out_shape, scratch_shapes, flops, *args, in_specs=None, out_specs=None, aliases=None):
    traffic = sum(math.prod(a.shape) * a.dtype.itemsize for a in (*args, *jax.tree.leaves(out_shape)))
    return pl.pallas_call(
        body,
        out_shape=jax.tree.map(lambda a: like(a.dtype, *a.shape), out_shape),
        in_specs=in_specs or [VMEM] * len(args),
        out_specs=out_specs or jax.tree.map(lambda _: VMEM, out_shape),
        scratch_shapes=scratch_shapes,
        input_output_aliases=aliases or {},
        compiler_params=pltpu.CompilerParams(vmem_limit_bytes=VMEM_LIMIT),
        cost_estimate=pl.CostEstimate(flops=flops, bytes_accessed=traffic, transcendentals=0),
    )(*args)


def like(dtype, *shape):
    return jax.ShapeDtypeStruct(shape, dtype)


def lane(shape):
    return lax.broadcasted_iota(jnp.int32, shape, len(shape) - 1)


def swap_halves(a):
    return pltpu.roll(a, T // 2, a.ndim - 1)


def halves(low, high):
    return jnp.where(lane(low.shape) < T // 2, low, high)


def exchange_halves(a, b):
    mixed = swap_halves(halves(b, a))
    return halves(a, mixed), halves(mixed, b)


def from_below(a):
    return jnp.where(lane(a.shape) % Z == 0, 0.0, pltpu.roll(a, 1, a.ndim - 1))


def from_above(a):
    return jnp.where(lane(a.shape) % Z == Z - 1, 0.0, pltpu.roll(a, T - 1, a.ndim - 1))


def tile(t):
    return slice(t * T, t * T + T)


def to_channels(rows, stage):
    rows = rows.astype(F32)
    for pair in range(C // 2):
        even, odd = exchange_halves(rows[:8, tile(pair)], rows[8:, tile(pair)])
        stage[pl.ds(pair * 16, 8), :] = even
        stage[pl.ds(pair * 16 + 8, 8), :] = odd
    return [stage[pl.ds(t, C, stride=8), :] for t in range(8)]


def is_even(axis):
    return (lax.axis_index(axis) & 1) == 0


def clear_ends(axis, low, high):
    @pl.when(lax.axis_index(axis) == 0)
    def _():
        low[...] = jnp.zeros_like(low)

    @pl.when(lax.axis_index(axis) == lax.axis_size(axis) - 1)
    def _():
        high[...] = jnp.zeros_like(high)


def scales():
    return 1.0 + lax.broadcasted_iota(jnp.int32, (8, T), 0).astype(F32) * 0.125


def my_half():
    total = 0
    for axis in ("gx", "gy"):
        for b in range(lax.axis_size(axis).bit_length() - 1):
            total = total + (lax.axis_index(axis) >> b)
    return total & 1


def faces(field, even, odd):
    for when, low, high in ((is_even("gx"), odd, even), (jnp.logical_not(is_even("gx")), even, odd)):

        @pl.when(when)
        def _(low=low, high=high):
            for t in range(8):
                low[:, tile(t)] = field(0, t)
                high[:, tile(t)] = field(7, t)


def pack_body(array, out, stage):
    for x in range(array.shape[0]):
        for t, part in enumerate(to_channels(array[x], stage.at[x])):
            out[x, :, tile(t)] = part.astype(BF16)


def pack(array, *after):
    def body(array, *refs):
        pack_body(array, *refs[-2:])

    return call(body, like(BF16, 8, C, ROW), [pltpu.VMEM((8, 8 * C, T), F32)], 1_000_000, array, *after)


def whole(ref):
    return lambda x, t: ref[x, :, tile(t)]


def split(mid, edge):
    return lambda x, t: edge[x, :, tile(t // 7)] if t in (0, 7) else mid[x, :, tile(t - 1)]


def with_faces(field, xlow, xhigh):
    return lambda x, t: xlow[:, tile(t)] if x < 0 else xhigh[:, tile(t)] if x > 7 else field(x, t)


def faces_body(mid, edge, even, odd):
    faces(split(mid, edge), even, odd)


def gradient_faces(mid, edge):
    face = like(BF16, C, ROW)
    return call(faces_body, (face, face), [], 100_000, mid, edge)


def sort(axis, even, odd, low, high):
    @pl.when(is_even(axis))
    def _():
        low[...] = odd[...]
        high[...] = even[...]

    @pl.when(jnp.logical_not(is_even(axis)))
    def _():
        low[...] = even[...]
        high[...] = odd[...]

    clear_ends(axis, low, high)


def edge_message(field, low_when, out):
    @pl.when(low_when)
    def _():
        for row in range(5):
            out[row] = halves(field(row + 4, 0).astype(F32), swap_halves(field(row - 1, 0).astype(F32))).astype(BF16)

    @pl.when(jnp.logical_not(low_when))
    def _():
        for row in range(5):
            out[row] = halves(swap_halves(field(row - 1, 7).astype(F32)), field(row + 4, 7).astype(F32)).astype(BF16)


def ends(ref):
    last = ref.shape[-1] // T - 1
    return lambda x, t: ref[x, :, tile(last if t else 0)]


def odd_edge_body(field, xeven, xodd, out, xlow, xhigh, *scratch):
    if scratch:
        stage, packed = scratch
        pack_body(xeven, packed.at[pl.ds(0, 1)], stage.at[pl.ds(0, 1)])
        pack_body(xodd, packed.at[pl.ds(1, 1)], stage.at[pl.ds(1, 1)])
        xeven, xodd = packed.at[0], packed.at[1]
    sort("gx", xeven, xodd, xlow, xhigh)
    edge_message(with_faces(ends(field), xlow, xhigh), is_even("gy"), out)


def odd_edge(field, xeven, xodd):
    face = like(BF16, C, ROW)
    scratch = [pltpu.VMEM((2, 8 * C, T), F32), pltpu.VMEM((2, C, ROW), BF16)] if xeven.ndim == 3 else []
    return call(odd_edge_body, (like(BF16, 5, C, T), face, face), scratch, 100_000, field, xeven, xodd)


def even_edge_body(field, xlow, xhigh, out):
    edge_message(with_faces(ends(field), xlow, xhigh), jnp.logical_not(is_even("gy")), out)


def even_edge(field, xlow, xhigh):
    return call(even_edge_body, like(BF16, 5, C, T), [], 100_000, field, xlow, xhigh)


def sort_edges(even, odd, near):
    for when, low, high in ((is_even("gy"), odd, even), (jnp.logical_not(is_even("gy")), even, odd)):

        @pl.when(when)
        def _(low=low, high=high):
            for row in range(5):
                a, b = low[row].astype(F32), high[row].astype(F32)
                near[row] = halves(a, b)
                near[row + 5] = halves(swap_halves(a), swap_halves(b))

    place = lax.axis_index("gy")
    for when, empty in ((place == 0, 0), (place == lax.axis_size("gy") - 1, 1)):

        @pl.when(when)
        def _(empty=empty):
            for row in range(10):
                near[row] = halves(near[row], jnp.zeros((C, T), F32)) if empty else halves(jnp.zeros((C, T), F32), near[row])


def activation(pre, grad_out):
    sig = 1.0 / (1.0 + jnp.exp(-pre))
    return grad_out.astype(F32) * sig * (1.0 + pre * (1.0 - sig))


def stack(out, i, tiles, field, near=None):
    for n, t in enumerate(tiles):
        for dy in range(3):
            if t + dy == 0:
                part = halves(near, swap_halves(field(7).astype(F32))).astype(BF16)
            elif t + dy == 9:
                part = halves(swap_halves(field(0).astype(F32)), near).astype(BF16)
            else:
                part = field(t + dy - 1)
            out[(3 * i + dy) * C : (3 * i + dy + 1) * C, tile(n)] = part


def step_z(part):
    return from_below(part[:64]) + part[64:128] + from_above(part[128:])


def gradient(tiles, gx, wf, bias, cols, gps, out):
    offset = jnp.concatenate([bias[...]] * 2, axis=0)
    total = jnp.zeros((64, T), F32)
    for q in range(4):
        both = jnp.dot(wf[...], cols[q * 192 : q * 192 + 384, :], preferred_element_type=F32)
        for n, t in enumerate(tiles):
            grad_out = gx[2 * q : 2 * q + 2, :, tile(t)].reshape(64, T)
            grad = activation(step_z(both[:, tile(n)]) + offset, grad_out).astype(BF16)
            out[2 * q : 2 * q + 2, :, tile(n)] = grad.reshape(2, C, T)
            grad = grad.astype(F32)
            total = total + grad
            gps[q * 192 : q * 192 + 64, tile(n)] = from_above(grad).astype(BF16)
            gps[q * 192 + 64 : q * 192 + 128, tile(n)] = grad.astype(BF16)
            gps[q * 192 + 128 : q * 192 + 192, tile(n)] = from_below(grad).astype(BF16)
    prod = jnp.zeros((384, 192), F32)
    for q in range(4):
        prod = prod + lax.dot_general(
            cols[q * 192 : q * 192 + 384, :],
            gps[q * 192 : q * 192 + 192, :],
            (((1,), (1,)), ((), ())),
            preferred_element_type=F32,
        )
    return total, prod


MID = range(1, 7)
EDGE = (0, 7)


def middle_body(vx, gx, xlow, xhigh, wf, bias, gmid, total, prod, cols, gps):
    field = with_faces(whole(vx), xlow, xhigh)
    for x in range(-1, 9):
        stack(cols, x + 1, MID, lambda t, x=x: field(x, t))
    total[...], prod[...] = gradient(MID, gx, wf, bias, cols, gps, gmid)


def middle(vx, gx, xlow, xhigh, wf, bias):
    out = (like(BF16, 8, C, 6 * T), like(F32, 64, T), like(F32, 384, 192))
    scratch = [pltpu.VMEM((960, 6 * T), BF16), pltpu.VMEM((768, 6 * T), BF16)]
    return call(middle_body, out, scratch, 1_000_000, vx, gx, xlow, xhigh, wf, bias)


def outer_body(vx, gx, xlow, xhigh, yodd, yeven, wf, bias, total, prod, gedge, keep, give, near, cols, gps, wire):
    sort_edges(yeven, yodd, near)
    field = with_faces(whole(vx), xlow, xhigh)
    for x in range(-1, 9):
        stack(cols, x + 1, EDGE, lambda t, x=x: field(x, t), near[x + 1])
    more_total, more = gradient(EDGE, gx, wf, bias, cols, gps, gedge)
    total, prod = total[...] + more_total, prod[...] + more
    group = lane((8, T)) // C
    rows = []
    for row in range(0, 288, 8):
        a, b = prod[row : row + 8], prod[row + 96 : row + 104]
        a = jnp.concatenate([a[:, T:], jnp.zeros((8, 64), F32)], axis=1), a[:, :T]
        b = jnp.concatenate([b[:, T:], jnp.zeros((8, 64), F32)], axis=1), b[:, :T]
        near = a[1] + pltpu.roll(b[1], T - C, 1)
        far = a[0] + pltpu.roll(b[0], T - C, 1)
        rows.append((near, pltpu.roll(near, T - C, 1), pltpu.roll(far, 2 * C, 1), far))
    for i in range(27):
        near, moved, far, _ = rows[i]
        dz, at = divmod(i, 9)
        near2, moved2, far2, plain2 = rows[27 + at]
        last = pltpu.roll((near2, near2, plain2)[dz], (3 * C, C, 3 * C)[dz], 1)
        out = jnp.where(group == 0, near, jnp.where(group == 1, moved, jnp.where(group == 2, far, last)))
        wire[8 * i : 8 * i + 8] = out
    total = jnp.concatenate([total[:C] + total[C:], jnp.zeros((T - C, T), F32)], axis=0)
    total = jnp.sum(total.T, axis=0, keepdims=True)
    wire[216:] = total * scales()
    for half in range(2):

        @pl.when(my_half() == half)
        def _(half=half):
            keep[...] = wire[half * HALF : half * HALF + HALF]
            give[...] = wire[HALF - half * HALF : 2 * HALF - half * HALF]


def outer(vx, gx, xlow, xhigh, yodd, yeven, wf, bias, total, prod):
    out = (like(BF16, 8, C, 2 * T), like(F32, HALF, T), like(F32, HALF, T))
    scratch = [
        pltpu.VMEM((10, C, T), F32),
        pltpu.VMEM((960, 2 * T), BF16),
        pltpu.VMEM((768, 2 * T), BF16),
        pltpu.VMEM((2 * HALF, T), F32),
    ]
    args = (vx, gx, xlow, xhigh, yodd, yeven, wf, bias, total, prod)
    return call(outer_body, out, scratch, 700_000_000, *args)


def back_body(gmid, gedge, xlow, xhigh, yodd, yeven, wd, block, near, cols, stage):
    sort_edges(yeven, yodd, near)
    field = with_faces(split(gmid, gedge), xlow, xhigh)
    for x in range(-1, 9):
        stack(cols, x + 1, range(8), lambda t, x=x: field(x, t), near[x + 1])
    for q in range(4):
        both = jnp.dot(wd[...], cols[q * 192 : q * 192 + 384, :], preferred_element_type=F32)
        for t in range(8):
            out = step_z(both[:, tile(t)])
            for x in range(2):
                stage[2 * q + x, pl.ds(t, C, stride=8), :] = out[x * C : x * C + C]
        for x in (2 * q, 2 * q + 1):
            for pair in range(C // 2):
                even, odd = stage[x, pl.ds(pair * 16, 8), :], stage[x, pl.ds(pair * 16 + 8, 8), :]
                block[x, :, tile(pair)] = jnp.concatenate(exchange_halves(even, odd), axis=0).astype(BF16)


def back(gmid, gedge, xlow, xhigh, yodd, yeven, wd):
    scratch = [
        pltpu.VMEM((10, C, T), F32),
        pltpu.VMEM((960, ROW), BF16),
        pltpu.VMEM((8, 8 * C, T), F32),
    ]
    out = like(BF16, 8, 16, C * Z)
    return call(back_body, out, scratch, 1_000_000_000, gmid, gedge, xlow, xhigh, yodd, yeven, wd)


def flush_body(block, data, sem):
    copy = pltpu.make_async_copy(block, data, sem)
    copy.start()
    copy.wait()


def flush(block):
    return call(flush_body, block, [pltpu.SemaphoreType.DMA], 100_000, block, out_specs=HBM)


def add_body(a, b, out):
    out[...] = (a[...].astype(F32) + b[...].astype(F32)).astype(out.dtype)


def add(a, b, dtype, cost=100_000):
    return call(add_body, like(dtype, *a.shape), [], cost, a, b)


def finish_body(scale, own, other, filters, biases):
    for half, halves_of in enumerate(((own, other), (other, own))):

        @pl.when(my_half() == half)
        def _(halves_of=halves_of):
            for row in range(0, 288, 8):
                for dz in range(3):
                    at, group = (row, dz) if row < 216 else (row - 216 + 72 * dz, 3)
                    part = halves_of[at // HALF][at % HALF : at % HALF + 8]
                    moved = part if group == 0 else pltpu.roll(part, T - group * C, 1)
                    block, inside = divmod(row, C)
                    filters[block * 3 + dz, inside : inside + 8, :] = moved[:, :C] * scale
            eight = halves_of[1][216 - HALF :] / scales()
            biases[...] = jnp.sum(eight, axis=0, keepdims=True)[:, :C] * (scale / 8)


def finish(own, other, scale):
    out = (like(F32, 27, C, C), like(F32, 1, C))
    return call(lambda *refs: finish_body(scale, *refs), out, [], 100_000, own, other)


def permute(array, target):
    nx, ny = lax.axis_size("gx"), lax.axis_size("gy")
    pairs = []
    for x in range(nx):
        for y in range(ny):
            to = target(x, y)
            pairs.append((x * ny + y, to[0] * ny + to[1]))
    return lax.ppermute(array, ("gx", "gy"), pairs)


def swap_x(array, odd):
    nx = lax.axis_size("gx")
    return permute(array, lambda x, y: ((((x + odd) ^ 1) - odd) % nx, y))


def swap_y(array, odd):
    ny = lax.axis_size("gy")

    def target(x, y):
        to = ((y + odd) ^ 1) - odd
        return (x, to) if 0 <= to < ny else (x ^ 1, y)

    return permute(array, target)


def band(strip):
    pad = [jnp.pad(strip, ((0, 0), (0, 0), (96 * x, 96 - 96 * x))) for x in range(2)]
    return jnp.stack(pad, axis=1).reshape(192, 384)


def shards(volume, cotangent, weight, bias):
    nx, ny = lax.axis_size("gx"), lax.axis_size("gy")
    wf = band(jnp.transpose(weight, (2, 4, 0, 1, 3)).reshape(3, C, 288))
    wd = band(jnp.transpose(weight[::-1, ::-1, ::-1], (2, 3, 0, 1, 4)).reshape(3, C, 288))
    barrier = lax.optimization_barrier
    up = 7 * (1 - lax.axis_index("gx") % 2)
    xeven = lax.dynamic_slice_in_dim(volume, up, 1, 0)
    xodd = lax.dynamic_slice_in_dim(volume, 7 - up, 1, 0)
    xodd, xeven, bias = barrier((xodd, xeven, bias))
    offset = jnp.broadcast_to(bias[:, None], (C, T))
    vx = pack(volume, wf, offset)
    xodd = swap_x(xodd, 1)
    xeven = swap_x(xeven, 0)
    yodd, xlow, xhigh = odd_edge(vx, xeven, xodd)
    yodd, xlow, xhigh = barrier((yodd, xlow, xhigh))
    yeven = even_edge(vx, xlow, xhigh)
    yeven, xlow, xhigh, cotangent = barrier((yeven, xlow, xhigh, cotangent))
    yeven = swap_y(yeven, 0)
    yodd = swap_y(yodd, 1)
    gx = pack(cotangent)
    gmid, total, prod = middle(vx, gx, xlow, xhigh, wf, offset)
    yodd, total = barrier((yodd, total))
    gedge, keep, give = outer(vx, gx, xlow, xhigh, yodd, yeven, wf, offset, total, prod)

    state = dict(gmid=gmid, gedge=gedge)

    def along_x():
        xeven, xodd = gradient_faces(state["gmid"], state["gedge"])
        state["xodd"] = swap_x(xodd, 1)
        state["xeven"] = swap_x(xeven, 0)

    def along_y():
        yodd, state["xlow"], state["xhigh"] = odd_edge(state["gedge"], state["xeven"], state["xodd"])
        state["yeven"] = swap_y(even_edge(state["gedge"], state["xlow"], state["xhigh"]), 0)
        state["yodd"] = swap_y(yodd, 1)

    def data():
        names = ("gmid", "gedge", "xlow", "xhigh", "yodd", "yeven")
        state["block"] = back(*(state[name] for name in names), wd)

    def data_out():
        state["data"] = flush(state["block"])

    works = [
        (None, (), None),
        (along_x, ("gmid",), None),
        (None, (), None),
        (along_y, ("gedge", "xeven", "xodd"), None),
        (data, ("gmid",), "block"),
        (data_out, ("block",), "data"),
    ]

    def step(sent, target):
        work, tied, then = works.pop(0) if works else (None, None, None)
        if work:
            sent, given = barrier((sent, {name: state[name] for name in tied}))
            state.update(given)
        got = permute(sent, target)
        if work:
            work()
        if then:
            got, state[then] = barrier((got, state[then]))
        return sent, got

    _, got = step(give, lambda x, y: (x ^ 1, y))
    wire = add(keep, got, BF16)
    steps = [(1 << b, 0) for b in range(1, nx.bit_length() - 1)] + [(0, 1 << b) for b in range(ny.bit_length() - 1)]
    for n, (dx, dy) in enumerate(steps):
        sent, got = step(wire, lambda x, y: (x ^ dx ^ 1, y ^ dy))
        wire = add(sent, got, F32 if n == len(steps) - 1 else BF16, 10**9 if n == len(steps) - 2 else 100_000)
    scale = 1.0 / math.sqrt(8 * nx * 16 * ny * Z)
    sent, got = step(wire, lambda x, y: (x ^ 1, y))
    for work, tied, _ in works:
        if work:
            work()
    filters, biases = finish(sent, got, scale)
    return state["data"], filters.reshape(3, 3, 3, C, C), biases.reshape(C)


def solution(mesh):
    in_specs = (P("gx", "gy", None), P("gx", "gy", None), P(), P())
    out_specs = (P("gx", "gy", None), P(), P())
    return jax.shard_map(shards, mesh=mesh, in_specs=in_specs, out_specs=out_specs, check_vma=False)
```
